32 devices in a mesh: row: 4 (over x, core), col: 2 (over y), mat: 4 (over z).
Axes of the slice: x: 2, y: 2, z: 4, core: 2. Of those that a mesh axis runs over, the one named last changes fastest.
Arguments:
- grads: float32 [4, 4096, 4096], P('mat', 'row', 'col'), may hold values from -6 to 6
- left_stats: float32 [4, 4096, 256], P('mat', 'row'), as said below
- right_stats: float32 [4, 4096, 256], P('mat', 'col'), as said below
Outputs:
- update: float32 [4, 4096, 4096], P('mat', ('row', 'col'))
The draws below stay inside these ranges and needn't reach their ends.
Inputs may be any that keep to these rules, and one draw needn't show every extreme that they name: `left_stats`: each aligned block of 256 rows along the second dimension, taken as a 256 x 256 matrix, is symmetric positive definite. `right_stats`: each aligned block of 256 rows along the second dimension, taken as a 256 x 256 matrix, is symmetric positive definite.
All inputs are finite; a program needn't handle non-finite values.
Results may differ from the reference program's by a relative error of at most 0.00011.
Values sent between devices are 32-bit elements; how exact they have to be, the bound alone decides.
No kernel may reach another device: no remote copies, remote signals or barrier semaphores. Data moves between devices by JAX's collectives and lax.ppermute only.
A program may use at most 64 MiB of HBM per device.

```python
import jax
import jax.numpy as jnp
from jax import lax

D = 4096
BLK = 256
ITERS = 3
MATS = 4


def spd_blocks(key):
    nblk = D // BLK
    first, second = jax.random.split(key)
    raw = jax.random.normal(first, (MATS, nblk, BLK, BLK), jnp.float32)
    prod = jnp.einsum('mibk,mick->mibc', raw, raw, precision=lax.Precision.HIGHEST) / BLK
    diag = jax.random.uniform(jax.random.fold_in(second, 3), (MATS, nblk, BLK), jnp.float32, 0.3, 2.0)
    prod = prod + diag[..., None] * jnp.eye(BLK, dtype=jnp.float32)
    return prod.reshape(MATS, D, BLK)


def draw_left_stats(key, part):
    return spd_blocks(jax.random.fold_in(key, 11))


def draw_right_stats(key, part):
    return spd_blocks(jax.random.fold_in(key, 23))


def shard_levels(stream_key, dims, pieces, least, largest):
    def one(axis_at, parts):
        steps = jax.random.uniform(jax.random.fold_in(jax.random.fold_in(stream_key, 6), axis_at), (parts,), jnp.float32, least / len(pieces), largest / len(pieces))
        return jnp.repeat(jnp.exp(steps), dims[axis_at] // parts).reshape((-1,) + (1,) * (len(dims) - axis_at - 1))

    factor_of = one(*pieces[0])
    for cut in pieces[1:]:
        factor_of = factor_of * one(*cut)
    return factor_of


def normal_values(key, dims, spread, bound, pieces=(), kind=jnp.bfloat16):
    factor_of = shard_levels(key, dims, pieces, -0.22, 0.18) if pieces else 1.0
    values = jax.random.normal(key, dims, jnp.float32) * spread * factor_of
    return jnp.minimum(jnp.maximum(values, -bound), bound).astype(kind)


def setup_inputs(seed: int = 0) -> dict:
    streams_of = jax.random.split(jax.random.key(seed), 4)
    return {
        "grads": normal_values(streams_of[0], (MATS, D, D), 1.0, 6.0, ((0, 4), (1, 4), (2, 2)), jnp.float32),
        "left_stats": draw_left_stats(jax.random.fold_in(streams_of[3], 71), 0),
        "right_stats": draw_right_stats(jax.random.fold_in(streams_of[3], 71), 0),
    }


beta_mix = 0.5
eps_shift = 0.001

def matmul(left, right):
    return jnp.einsum('...ij,...jk->...ik', left, right, precision=lax.Precision.HIGHEST)

def newton_root(factor):
    size = factor.shape[-1]
    ident = jnp.eye(size, dtype=factor.dtype)
    scale = jnp.sqrt(lax.optimization_barrier(jnp.sum(factor * factor, axis=(-2, -1), keepdims=True)))
    moving = factor / scale
    result = jnp.broadcast_to(ident, factor.shape)
    for count in range(ITERS):
        step_mat = (5.0 * ident - moving) * 0.25
        result = matmul(result, step_mat)
        squared = matmul(step_mat, step_mat)
        moving = matmul(matmul(squared, squared), moving)
    return result * jnp.power(scale, -0.25)

def reference(grads, left_stats, right_stats):
    mats = grads.shape[0]
    nblk = D // BLK
    ident = jnp.eye(BLK, dtype=grads.dtype)
    by_rows = grads.reshape(mats, nblk, BLK, D)
    left_gram = jnp.einsum('mibd,mied->mibe', by_rows, by_rows, precision=lax.Precision.HIGHEST) / D
    by_cols = grads.reshape(mats, D, nblk, BLK)
    right_gram = jnp.einsum('mdjb,mdje->mjbe', by_cols, by_cols, precision=lax.Precision.HIGHEST) / D
    left_factor = beta_mix * left_stats.reshape(mats, nblk, BLK, BLK) + (1.0 - beta_mix) * left_gram + eps_shift * ident
    right_factor = beta_mix * right_stats.reshape(mats, nblk, BLK, BLK) + (1.0 - beta_mix) * right_gram + eps_shift * ident
    left_root = newton_root(left_factor)
    right_root = newton_root(right_factor)
    half = jnp.einsum('mibe,mied->mibd', left_root, by_rows, precision=lax.Precision.HIGHEST)
    half = half.reshape(mats, D, nblk, BLK)
    full = jnp.einsum('mdjb,mjbe->mdje', half, right_root, precision=lax.Precision.HIGHEST)
    return full.reshape(mats, D, D)
```

```python
import functools

import jax
import jax.numpy as jnp
from jax import lax
from jax.experimental import pallas as pl
from jax.experimental.pallas import tpu as pltpu
from jax.sharding import PartitionSpec as P

ITERS = 3
beta_mix = 0.5
eps_shift = 0.001
PAD = 8
VMEM_LIMIT = 24 * 1024 * 1024
SMALL = pl.CostEstimate(flops=1, bytes_accessed=1, transcendentals=0)


def matmul(left, right):
    return jnp.einsum("...ij,...jk->...ik", left, right, precision=lax.Precision.HIGHEST)


def newton_root(factor):
    size = factor.shape[-1]
    ident = jnp.eye(size, dtype=jnp.float32)
    scale = jnp.sqrt(jnp.sum(factor * factor, axis=(-2, -1), keepdims=True))
    moving = factor / scale
    result = jnp.broadcast_to(ident, factor.shape)
    for count in range(ITERS):
        step_mat = (5.0 * ident - moving) * 0.25
        result = matmul(result, step_mat)
        squared = matmul(step_mat, step_mat)
        moving = matmul(matmul(squared, squared), moving)
    return result * jnp.power(scale, -0.25)


def general_device(full_dim, grads, left_stats, right_stats):
    mats, tile_rows, tile_cols = grads.shape
    blk = left_stats.shape[2]
    row_blocks = tile_rows // blk
    col_blocks = tile_cols // blk
    ident = jnp.eye(blk, dtype=jnp.float32)
    by_rows = grads.reshape(mats, row_blocks, blk, tile_cols)
    left_part = jnp.einsum("mibd,mied->mibe", by_rows, by_rows, precision=lax.Precision.HIGHEST) / full_dim
    by_cols = grads.reshape(mats, tile_rows, col_blocks, blk)
    right_part = (
        jnp.einsum("mdjb,mdje->mjbe", by_cols, by_cols, precision=lax.Precision.HIGHEST) / full_dim
    )
    left_gram = lax.psum(left_part, "col")
    right_gram = lax.psum(right_part, "row")
    left_factor = (
        beta_mix * left_stats.reshape(mats, row_blocks, blk, blk)
        + (1.0 - beta_mix) * left_gram
        + eps_shift * ident
    )
    right_factor = (
        beta_mix * right_stats.reshape(mats, col_blocks, blk, blk)
        + (1.0 - beta_mix) * right_gram
        + eps_shift * ident
    )
    left_root = newton_root(left_factor)
    right_root = newton_root(right_factor)
    half = jnp.einsum("mibe,mied->mibd", left_root, by_rows, precision=lax.Precision.HIGHEST)
    half = half.reshape(mats, tile_rows, col_blocks, blk)
    full = jnp.einsum("mdjb,mjbe->mdje", half, right_root, precision=lax.Precision.HIGHEST)
    full = full.reshape(mats, tile_rows, tile_cols)
    return lax.all_to_all(full, "col", split_axis=1, concat_axis=2, tiled=True)


def split(value):
    high = value.astype(jnp.bfloat16)
    low = (value - high.astype(jnp.float32)).astype(jnp.bfloat16)
    return high, low


def dot(left, right, dims=((1,), (0,))):
    return lax.dot_general(left, right, (dims, ((), ())), preferred_element_type=jnp.float32)


def product(left, right):
    lh, ll = left
    rh, rl = right
    return dot(lh, rh) + (dot(lh, rl) + dot(ll, rh))


def places(blk):
    rows = lax.broadcasted_iota(jnp.int32, (blk, blk), 0)
    cols = lax.broadcasted_iota(jnp.int32, (blk, blk), 1)
    return rows, cols


def pack(first, second):
    blk = first.shape[0]
    rows, cols = places(blk)
    body = jnp.where(rows <= cols, first, second)
    diag = jnp.sum(jnp.where(rows == cols, second, 0.0), axis=0, keepdims=True)
    return body, jnp.broadcast_to(diag, (PAD, blk))


def unpack(body, diag):
    blk = body.shape[0]
    rows, cols = places(blk)
    turned = body.T
    first = jnp.where(rows <= cols, body, turned)
    second = jnp.where(rows > cols, body, jnp.where(rows == cols, diag, turned))
    return first, second


def gram_kernel(place, g_ref, after_ref, send_ref, keep_ref, lsend_ref, lkeep_ref, lhh, lcross):
    step = pl.program_id(0)
    last = pl.num_programs(0) - 1
    col_at = place[1]
    rows, wide = g_ref.shape
    blk = wide // 2
    high, low = split(g_ref[...])

    grams = []
    for b in range(2):
        hb = high[:, b * blk : (b + 1) * blk]
        lb = low[:, b * blk : (b + 1) * blk]
        both = dot(hb, hb, ((0,), (0,)))
        cross = dot(hb, lb, ((0,), (0,)))
        grams.append(both + (cross + cross.T))
    body, diag = pack(*grams)

    @pl.when(step < 2)
    def _():
        send_ref[0, :blk, :] = body
        send_ref[0, blk:, :] = diag

    @pl.when(step >= 2)
    def _():
        keep_ref[0, :blk, :] = body
        keep_ref[0, blk:, :] = diag

    for i in range(rows // blk):
        hi = high[i * blk : (i + 1) * blk, :]
        lo = low[i * blk : (i + 1) * blk, :]
        both = dot(hi, hi, ((1,), (1,)))
        cross = dot(hi, lo, ((1,), (1,)))

        @pl.when(step == 0)
        def _():
            lhh[i] = both
            lcross[i] = cross

        @pl.when(step > 0)
        def _():
            lhh[i] += both
            lcross[i] += cross

    @pl.when(step == last)
    def _():
        for ref, owner in ((lsend_ref, 1 - col_at), (lkeep_ref, col_at)):
            pair = []
            for b in range(2):
                cross = lcross[owner * 2 + b]
                pair.append(lhh[owner * 2 + b] + (cross + cross.T))
            body, diag = pack(*pair)
            ref[:blk, :] = body
            ref[blk:, :] = diag


def grams(place, tile, blk, after):
    rows, width = tile.shape
    pairs = width // (2 * blk)
    tall = blk + PAD

    def pair_of(step, place):
        flip = jnp.where(step == 0, 3, jnp.where(step == 3, 0, step))
        return (0, place[0] ^ flip)

    shape = jax.ShapeDtypeStruct((2, tall, blk), jnp.float32)
    flat = jax.ShapeDtypeStruct((tall, blk), jnp.float32)
    return pl.pallas_call(
        gram_kernel,
        out_shape=(shape, shape, flat, flat),
        grid_spec=pltpu.PrefetchScalarGridSpec(
            num_scalar_prefetch=1,
            grid=(pairs,),
            in_specs=[pl.BlockSpec((rows, 2 * blk), pair_of), pl.BlockSpec(memory_space=pl.ANY)],
            out_specs=(
                pl.BlockSpec((1, tall, blk), lambda s, place: (jnp.minimum(s, 1), 0, 0)),
                pl.BlockSpec((1, tall, blk), lambda s, place: (jnp.maximum(s - 2, 0), 0, 0)),
                pl.BlockSpec((tall, blk), lambda s, place: (0, 0)),
                pl.BlockSpec((tall, blk), lambda s, place: (0, 0)),
            ),
            scratch_shapes=[
                pltpu.VMEM((rows // blk, blk, blk), jnp.float32),
                pltpu.VMEM((rows // blk, blk, blk), jnp.float32),
            ],
        ),
        compiler_params=pltpu.CompilerParams(vmem_limit_bytes=VMEM_LIMIT),
        cost_estimate=SMALL,
        name="grams",
    )(place, tile, after)


def take_kernel(place, g_ref, *rest):
    rest[-1][...] = g_ref[...]


def take(place, tile, blk, chunk, after):
    flip, at, blocks = chunk
    rows = tile.shape[0] // 2
    operands = [place, tile]
    in_specs = [pl.BlockSpec((rows, blk), lambda s, place: (1 - place[1], (place[0] ^ flip) * 2 + at + s))]
    for other in after:
        operands.append(other)
        in_specs.append(pl.BlockSpec(memory_space=pl.ANY))
    return pl.pallas_call(
        take_kernel,
        out_shape=jax.ShapeDtypeStruct((rows, blocks * blk), jnp.float32),
        grid_spec=pltpu.PrefetchScalarGridSpec(
            num_scalar_prefetch=1,
            grid=(blocks,),
            in_specs=in_specs,
            out_specs=pl.BlockSpec((rows, blk), lambda s, place: (0, s)),
        ),
        compiler_params=pltpu.CompilerParams(vmem_limit_bytes=VMEM_LIMIT),
        cost_estimate=SMALL,
        name="take",
    )(*operands)


def fold_kernel(a_ref, b_ref, after_ref, out_ref):
    out_ref[...] = a_ref[0] + b_ref[0]


def fold(kept, near, after):
    tall, blk = kept.shape[1:]
    return pl.pallas_call(
        fold_kernel,
        out_shape=jax.ShapeDtypeStruct((tall, blk), jnp.float32),
        grid=(1,),
        in_specs=[
            pl.BlockSpec((1, tall, blk), lambda s: (0, 0, 0)),
            pl.BlockSpec((1, tall, blk), lambda s: (0, 0, 0)),
            pl.BlockSpec(memory_space=pl.ANY),
        ],
        out_specs=pl.BlockSpec((tall, blk), lambda s: (0, 0)),
        compiler_params=pltpu.CompilerParams(vmem_limit_bytes=VMEM_LIMIT),
        cost_estimate=SMALL,
        name="fold",
    )(kept, near, after)


def pair_roots(full_dim, stats_ref, body, diag):
    blk = body.shape[0]
    rows, cols = places(blk)
    ident = jnp.where(rows == cols, 1.0, 0.0)
    moving, scales = [], []
    for b, gram in enumerate(unpack(body, diag)):
        factor = (
            beta_mix * stats_ref[b * blk : (b + 1) * blk, :]
            + (1.0 - beta_mix) * (gram / full_dim)
            + eps_shift * ident
        )
        scale = jnp.sqrt(jnp.sum(factor * factor, keepdims=True))
        moving.append(factor / scale)
        scales.append(scale)
    result = None
    for count in range(ITERS):
        steps = [(5.0 * ident - m) * 0.25 for m in moving]
        parts = [split(s) for s in steps]
        if result is None:
            result = steps
        else:
            result = [product(split(r), p) for r, p in zip(result, parts)]
        if count < ITERS - 1:
            squared = [split(product(p, p)) for p in parts]
            fourth = [split(product(s, s)) for s in squared]
            moving = [product(f, split(m)) for f, m in zip(fourth, moving)]
    return [r * jnp.exp(-0.25 * jnp.log(s)) for r, s in zip(result, scales)]


def right_kernel(full_dim, place, stats_ref, a_ref, b_ref, c_ref, out_ref):
    blk = stats_ref.shape[1]
    total = a_ref[0] + b_ref[0] + c_ref[...]
    body, diag = pack(*pair_roots(full_dim, stats_ref, total[:blk], total[blk : blk + 1]))
    out_ref[:blk, :] = body
    out_ref[blk:, :] = diag


def right_roots(full_dim, place, stats, kept, near, far):
    blk = stats.shape[1]
    tall = blk + PAD
    return pl.pallas_call(
        functools.partial(right_kernel, full_dim),
        out_shape=jax.ShapeDtypeStruct((tall, blk), jnp.float32),
        grid_spec=pltpu.PrefetchScalarGridSpec(
            num_scalar_prefetch=1,
            grid=(1,),
            in_specs=[
                pl.BlockSpec((2 * blk, blk), lambda s, place: (place[0], 0)),
                pl.BlockSpec((1, tall, blk), lambda s, place: (1, 0, 0)),
                pl.BlockSpec((1, tall, blk), lambda s, place: (1, 0, 0)),
                pl.BlockSpec((tall, blk), lambda s, place: (0, 0)),
            ],
            out_specs=pl.BlockSpec((tall, blk), lambda s, place: (0, 0)),
        ),
        compiler_params=pltpu.CompilerParams(vmem_limit_bytes=VMEM_LIMIT),
        cost_estimate=SMALL,
        name="right_roots",
    )(place, stats, kept, near, far)


def left_kernel(full_dim, place, stats_ref, a_ref, b_ref, out_ref):
    blk = stats_ref.shape[1]
    total = a_ref[...] + b_ref[...]
    for b, root in enumerate(pair_roots(full_dim, stats_ref, total[:blk], total[blk : blk + 1])):
        high, low = split(root)
        out_ref[b, 0] = high
        out_ref[b, 1] = low


def left_roots(full_dim, place, stats, kept, came):
    blk = stats.shape[1]
    tall = blk + PAD
    return pl.pallas_call(
        functools.partial(left_kernel, full_dim),
        out_shape=jax.ShapeDtypeStruct((2, 2, blk, blk), jnp.bfloat16),
        grid_spec=pltpu.PrefetchScalarGridSpec(
            num_scalar_prefetch=1,
            grid=(1,),
            in_specs=[
                pl.BlockSpec((2 * blk, blk), lambda s, place: (place[1], 0)),
                pl.BlockSpec((tall, blk), lambda s, place: (0, 0)),
                pl.BlockSpec((tall, blk), lambda s, place: (0, 0)),
            ],
            out_specs=pl.BlockSpec((2, 2, blk, blk), lambda s, place: (0, 0, 0, 0)),
        ),
        compiler_params=pltpu.CompilerParams(vmem_limit_bytes=VMEM_LIMIT),
        cost_estimate=SMALL,
        name="left_roots",
    )(place, stats, kept, came)


def spread_kernel(*refs):
    out_ref = refs[-1]
    blk = out_ref.shape[-1]
    for at, ref in enumerate(refs[:-1]):
        for b, root in enumerate(unpack(ref[:blk, :], ref[blk : blk + 1, :])):
            high, low = split(root)
            out_ref[2 * at + b, 0] = high
            out_ref[2 * at + b, 1] = low


def spread_roots(packed):
    blk = packed[0].shape[1]
    count = len(packed)
    return pl.pallas_call(
        spread_kernel,
        out_shape=jax.ShapeDtypeStruct((2 * count, 2, blk, blk), jnp.bfloat16),
        compiler_params=pltpu.CompilerParams(vmem_limit_bytes=VMEM_LIMIT),
        cost_estimate=SMALL,
        name="spread_roots",
    )(*packed)


def update_kernel(place, g_ref, left_ref, right_ref, *rest):
    out_ref = rest[-1]
    blk = right_ref.shape[-1]
    right = (right_ref[0, 0], right_ref[0, 1])
    half = product(split(g_ref[...]), right)
    for i in range(g_ref.shape[0] // blk):
        part = split(half[i * blk : (i + 1) * blk])
        out_ref[i * blk : (i + 1) * blk, :] = product((left_ref[i, 0], left_ref[i, 1]), part)


def update(place, source, left, right, out, out_shape, blocks, g_map, right_at, out_map):
    blk = right.shape[-1]
    rows = out_shape[0]
    in_specs = [
        pl.BlockSpec((rows, blk), g_map),
        pl.BlockSpec((2, 2, blk, blk), lambda s, place: (0, 0, 0, 0)),
        pl.BlockSpec((1, 2, blk, blk), lambda s, place: (right_at + s, 0, 0, 0)),
    ]
    operands = [source, left, right]
    aliases = {}
    if out is not None:
        in_specs.append(pl.BlockSpec(memory_space=pl.ANY))
        operands.append(out)
        aliases = {4: 0}
    return pl.pallas_call(
        update_kernel,
        out_shape=jax.ShapeDtypeStruct(out_shape, jnp.float32),
        grid_spec=pltpu.PrefetchScalarGridSpec(
            num_scalar_prefetch=1,
            grid=(blocks,),
            in_specs=in_specs,
            out_specs=pl.BlockSpec((rows, blk), out_map),
        ),
        input_output_aliases=aliases,
        compiler_params=pltpu.CompilerParams(vmem_limit_bytes=VMEM_LIMIT),
        cost_estimate=SMALL,
        name="update",
    )(place, *operands)


def exchange_device(full_dim, n_row, grads, left_stats, right_stats):
    tile_rows, tile_cols = grads.shape[1:]
    blk = left_stats.shape[2]
    tile = pltpu.with_memory_space_constraint(grads.reshape(tile_rows, tile_cols), pltpu.HBM)
    lstats = left_stats.reshape(tile_rows, blk)
    rstats = right_stats.reshape(tile_cols, blk)
    r = lax.axis_index("row")
    c = lax.axis_index("col")
    place = jnp.stack([r, c]).astype(jnp.int32)
    rows = tile_rows // 2
    halves = tile_cols // blk

    def over(axis, value):
        if axis == "col":
            return lax.ppermute(value, "col", [(0, 1), (1, 0)])
        flip = {"core": 1, "x": 2}[axis]
        return lax.ppermute(value, "row", [(i, i ^ flip) for i in range(n_row)])

    chunks = [(0, 0, 2), (1, 0, 2), (2, 0, 2), (3, 0, 1), (3, 1, 1)]
    first = take(place, tile, blk, chunks[0], ())
    came = [over("col", first)]

    send, keep, lsend, lkeep = grams(place, tile, blk, first)
    near = over("core", send)
    lcame = over("col", lsend)
    for k in (1,):
        came.append(over("col", take(place, tile, blk, chunks[k], (lsend,))))
    far = over("x", fold(keep, near, came[0]))
    own = right_roots(full_dim, place, rstats, keep, near, far)
    across = over("col", own)
    for k in (2, 3, 4):
        came.append(over("col", take(place, tile, blk, chunks[k], (own,))))
    left = left_roots(full_dim, place, lstats, lkeep, lcame)

    own_x = over("x", own)
    own_c = over("core", own)
    own_xc = over("core", own_x)
    mine = spread_roots([own, own_c, own_x, own_xc])
    across_x = over("x", across)
    across_c = over("core", across)
    across_xc = over("core", across_x)
    theirs = spread_roots([across, across_c, across_x, across_xc])

    def block_of(flip_block, place):
        return ((place[0] ^ (flip_block // 2)) * 2) + flip_block % 2

    shape = (rows, 2 * tile_cols)
    out = update(
        place, tile, left, mine, None, shape, halves,
        lambda s, place: (place[1], block_of(s, place)),
        0,
        lambda s, place: (0, place[1] * halves + block_of(s, place)),
    )
    for (flip, at, blocks), value in zip(chunks, came):
        base = 2 * flip + at
        out = update(
            place, value, left, theirs, out, shape, blocks,
            lambda s, place: (0, s),
            base,
            lambda s, place, base=base: (0, (1 - place[1]) * halves + block_of(base + s, place)),
        )
    return out.reshape(1, rows, 2 * tile_cols)


def per_device(n_row, n_col, grads, left_stats, right_stats):
    mats, tile_rows, tile_cols = grads.shape
    blk = left_stats.shape[2]
    full_dim = tile_cols * n_col
    if mats == 1 and n_col == 2 and n_row == 4 and tile_rows == 4 * blk and tile_cols == 8 * blk:
        return exchange_device(full_dim, n_row, grads, left_stats, right_stats)
    return general_device(full_dim, grads, left_stats, right_stats)


def solution(mesh):
    return jax.shard_map(
        functools.partial(per_device, mesh.shape["row"], mesh.shape["col"]),
        mesh=mesh,
        in_specs=(P("mat", "row", "col"), P("mat", "row", None), P("mat", "col", None)),
        out_specs=P("mat", ("row", "col"), None),
        check_vma=False,
    )
```

```python
import functools

import jax
import jax.numpy as jnp
from jax import lax
from jax.experimental import pallas as pl
from jax.experimental.pallas import tpu as pltpu
from jax.sharding import PartitionSpec as P

ITERS = 3
beta_mix = 0.5
eps_shift = 0.001
PAD = 8
VMEM_LIMIT = 24 * 1024 * 1024
SMALL = pl.CostEstimate(flops=1, bytes_accessed=1, transcendentals=0)


def matmul(left, right):
    return jnp.einsum("...ij,...jk->...ik", left, right, precision=lax.Precision.HIGHEST)


def newton_root(factor):
    size = factor.shape[-1]
    ident = jnp.eye(size, dtype=jnp.float32)
    scale = jnp.sqrt(jnp.sum(factor * factor, axis=(-2, -1), keepdims=True))
    moving = factor / scale
    result = jnp.broadcast_to(ident, factor.shape)
    for count in range(ITERS):
        step_mat = (5.0 * ident - moving) * 0.25
        result = matmul(result, step_mat)
        squared = matmul(step_mat, step_mat)
        moving = matmul(matmul(squared, squared), moving)
    return result * jnp.power(scale, -0.25)


def general_device(full_dim, grads, left_stats, right_stats):
    mats, tile_rows, tile_cols = grads.shape
    blk = left_stats.shape[2]
    row_blocks = tile_rows // blk
    col_blocks = tile_cols // blk
    ident = jnp.eye(blk, dtype=jnp.float32)
    by_rows = grads.reshape(mats, row_blocks, blk, tile_cols)
    left_part = jnp.einsum("mibd,mied->mibe", by_rows, by_rows, precision=lax.Precision.HIGHEST) / full_dim
    by_cols = grads.reshape(mats, tile_rows, col_blocks, blk)
    right_part = (
        jnp.einsum("mdjb,mdje->mjbe", by_cols, by_cols, precision=lax.Precision.HIGHEST) / full_dim
    )
    left_gram = lax.psum(left_part, "col")
    right_gram = lax.psum(right_part, "row")
    left_factor = (
        beta_mix * left_stats.reshape(mats, row_blocks, blk, blk)
        + (1.0 - beta_mix) * left_gram
        + eps_shift * ident
    )
    right_factor = (
        beta_mix * right_stats.reshape(mats, col_blocks, blk, blk)
        + (1.0 - beta_mix) * right_gram
        + eps_shift * ident
    )
    left_root = newton_root(left_factor)
    right_root = newton_root(right_factor)
    half = jnp.einsum("mibe,mied->mibd", left_root, by_rows, precision=lax.Precision.HIGHEST)
    half = half.reshape(mats, tile_rows, col_blocks, blk)
    full = jnp.einsum("mdjb,mjbe->mdje", half, right_root, precision=lax.Precision.HIGHEST)
    full = full.reshape(mats, tile_rows, tile_cols)
    return lax.all_to_all(full, "col", split_axis=1, concat_axis=2, tiled=True)


def split(value):
    high = value.astype(jnp.bfloat16)
    low = (value - high.astype(jnp.float32)).astype(jnp.bfloat16)
    return high, low


def dot(left, right, dims=((1,), (0,))):
    return lax.dot_general(left, right, (dims, ((), ())), preferred_element_type=jnp.float32)


def product(left, right):
    lh, ll = left
    rh, rl = right
    return dot(lh, rh) + (dot(lh, rl) + dot(ll, rh))


def places(blk):
    rows = lax.broadcasted_iota(jnp.int32, (blk, blk), 0)
    cols = lax.broadcasted_iota(jnp.int32, (blk, blk), 1)
    return rows, cols


def pack(first, second):
    blk = first.shape[0]
    rows, cols = places(blk)
    body = jnp.where(rows <= cols, first, second)
    diag = jnp.sum(jnp.where(rows == cols, second, 0.0), axis=0, keepdims=True)
    return body, jnp.broadcast_to(diag, (PAD, blk))


def unpack(body, diag):
    blk = body.shape[0]
    rows, cols = places(blk)
    turned = body.T
    first = jnp.where(rows <= cols, body, turned)
    second = jnp.where(rows > cols, body, jnp.where(rows == cols, diag, turned))
    return first, second


def pair_of(step, place):
    flip = jnp.where(step == 0, 3, jnp.where(step == 3, 0, step))
    return (0, place[0] ^ flip)


def right_gram_kernel(place, g_ref, after_ref, *out_refs):
    step = pl.program_id(0)
    blk = g_ref.shape[1] // 2
    high, low = split(g_ref[...])
    grams = []
    for b in range(2):
        hb = high[:, b * blk : (b + 1) * blk]
        lb = low[:, b * blk : (b + 1) * blk]
        both = dot(hb, hb, ((0,), (0,)))
        cross = dot(hb, lb, ((0,), (0,)))
        grams.append(both + (cross + cross.T))
    body, diag = pack(*grams)

    for at, ref in enumerate(out_refs):

        @pl.when(step == at)
        def _():
            ref[:blk, :] = body
            ref[blk:, :] = diag


def right_grams(place, tile, blk, after):
    rows, width = tile.shape
    tall = blk + PAD
    pairs = width // (2 * blk)
    return pl.pallas_call(
        right_gram_kernel,
        out_shape=(jax.ShapeDtypeStruct((tall, blk), jnp.float32),) * pairs,
        grid_spec=pltpu.PrefetchScalarGridSpec(
            num_scalar_prefetch=1,
            grid=(pairs,),
            in_specs=[pl.BlockSpec((rows, 2 * blk), pair_of), pl.BlockSpec(memory_space=pl.ANY)],
            out_specs=(pl.BlockSpec((tall, blk), lambda s, place: (0, 0)),) * pairs,
        ),
        compiler_params=pltpu.CompilerParams(vmem_limit_bytes=VMEM_LIMIT),
        cost_estimate=SMALL,
        name="right_grams",
    )(place, tile, after)


def left_gram_kernel(place, g_ref, after_ref, lsend_ref, lkeep_ref, lhh, lcross):
    step = pl.program_id(0)
    last = pl.num_programs(0) - 1
    col_at = place[1]
    rows = g_ref.shape[0]
    blk = lhh.shape[-1]
    high, low = split(g_ref[...])
    for i in range(rows // blk):
        hi = high[i * blk : (i + 1) * blk, :]
        lo = low[i * blk : (i + 1) * blk, :]
        both = dot(hi, hi, ((1,), (1,)))
        cross = dot(hi, lo, ((1,), (1,)))

        @pl.when(step == 0)
        def _():
            lhh[i] = both
            lcross[i] = cross

        @pl.when(step > 0)
        def _():
            lhh[i] += both
            lcross[i] += cross

    @pl.when(step == last)
    def _():
        for ref, owner in ((lsend_ref, 1 - col_at), (lkeep_ref, col_at)):
            pair = []
            for b in range(2):
                cross = lcross[owner * 2 + b]
                pair.append(lhh[owner * 2 + b] + (cross + cross.T))
            body, diag = pack(*pair)
            ref[:blk, :] = body
            ref[blk:, :] = diag


def left_grams(place, tile, blk, after):
    rows, width = tile.shape
    tall = blk + PAD
    flat = jax.ShapeDtypeStruct((tall, blk), jnp.float32)
    return pl.pallas_call(
        left_gram_kernel,
        out_shape=(flat, flat),
        grid_spec=pltpu.PrefetchScalarGridSpec(
            num_scalar_prefetch=1,
            grid=(width // (2 * blk),),
            in_specs=[
                pl.BlockSpec((rows, 2 * blk), lambda s, place: (0, s)),
                pl.BlockSpec(memory_space=pl.ANY),
            ],
            out_specs=(
                pl.BlockSpec((tall, blk), lambda s, place: (0, 0)),
                pl.BlockSpec((tall, blk), lambda s, place: (0, 0)),
            ),
            scratch_shapes=[
                pltpu.VMEM((rows // blk, blk, blk), jnp.float32),
                pltpu.VMEM((rows // blk, blk, blk), jnp.float32),
            ],
        ),
        compiler_params=pltpu.CompilerParams(vmem_limit_bytes=VMEM_LIMIT),
        cost_estimate=SMALL,
        name="left_grams",
    )(place, tile, after)


def take_kernel(place, g_ref, out_ref, sem):
    rows, wide = out_ref.shape
    top = pl.multiple_of((1 - place[1]) * rows, rows)
    start = pl.multiple_of((place[0] ^ raw_flip(place)) * wide, wide)
    copy = pltpu.make_async_copy(g_ref.at[pl.ds(top, rows), pl.ds(start, wide)], out_ref, sem)
    copy.start()
    copy.wait()


def take(place, tile, blk):
    return pl.pallas_call(
        take_kernel,
        out_shape=jax.ShapeDtypeStruct((tile.shape[0] // 2, 2 * blk), jnp.float32),
        grid_spec=pltpu.PrefetchScalarGridSpec(
            num_scalar_prefetch=1,
            grid=(1,),
            in_specs=[pl.BlockSpec(memory_space=pl.ANY)],
            out_specs=pl.BlockSpec(memory_space=pl.ANY),
            scratch_shapes=[pltpu.SemaphoreType.DMA],
        ),
        compiler_params=pltpu.CompilerParams(vmem_limit_bytes=VMEM_LIMIT),
        cost_estimate=SMALL,
        name="take",
    )(place, tile)


def fold_kernel(a_ref, b_ref, out_ref):
    out_ref[...] = a_ref[...] + b_ref[...]


def fold(kept, near):
    return pl.pallas_call(
        fold_kernel,
        out_shape=jax.ShapeDtypeStruct(kept.shape, jnp.float32),
        compiler_params=pltpu.CompilerParams(vmem_limit_bytes=VMEM_LIMIT),
        cost_estimate=SMALL,
        name="fold",
    )(kept, near)


def hold_kernel(a_ref, *rest):
    out_ref = rest[-1]
    out_ref[...] = a_ref[...]


def hold(value, *after):
    return pl.pallas_call(
        hold_kernel,
        out_shape=jax.ShapeDtypeStruct(value.shape, jnp.float32),
        in_specs=[pl.BlockSpec(memory_space=pltpu.VMEM)] + [pl.BlockSpec(memory_space=pl.ANY)] * len(after),
        compiler_params=pltpu.CompilerParams(vmem_limit_bytes=VMEM_LIMIT),
        cost_estimate=SMALL,
        name="hold",
    )(value, *after)


def pair_roots(full_dim, stats_ref, body, diag):
    blk = body.shape[0]
    rows, cols = places(blk)
    ident = jnp.where(rows == cols, 1.0, 0.0)
    moving, scales = [], []
    for b, gram in enumerate(unpack(body, diag)):
        factor = (
            beta_mix * stats_ref[b * blk : (b + 1) * blk, :]
            + (1.0 - beta_mix) * (gram / full_dim)
            + eps_shift * ident
        )
        scale = jnp.sqrt(jnp.sum(factor * factor, keepdims=True))
        moving.append(factor / scale)
        scales.append(scale)
    result = None
    for count in range(ITERS):
        steps = [(5.0 * ident - m) * 0.25 for m in moving]
        parts = [split(s) for s in steps]
        if result is None:
            result = steps
        else:
            result = [product(split(r), p) for r, p in zip(result, parts)]
        if count < ITERS - 1:
            squared = [split(product(p, p)) for p in parts]
            fourth = [split(product(s, s)) for s in squared]
            moving = [product(f, split(m)) for f, m in zip(fourth, moving)]
    return [r * jnp.exp(-0.25 * jnp.log(s)) for r, s in zip(result, scales)]


def right_kernel(full_dim, place, stats_ref, a_ref, b_ref, c_ref, after_ref, out_ref, halves_ref):
    blk = stats_ref.shape[1]
    total = a_ref[...] + b_ref[...] + c_ref[...]
    roots = pair_roots(full_dim, stats_ref, total[:blk], total[blk : blk + 1])
    body, diag = pack(*roots)
    out_ref[:blk, :] = body
    out_ref[blk:, :] = diag
    for b, root in enumerate(roots):
        high, low = split(root)
        halves_ref[b, 0] = high
        halves_ref[b, 1] = low


def right_roots(full_dim, place, stats, kept, near, far, after):
    blk = stats.shape[1]
    tall = blk + PAD
    return pl.pallas_call(
        functools.partial(right_kernel, full_dim),
        out_shape=(
            jax.ShapeDtypeStruct((tall, blk), jnp.float32),
            jax.ShapeDtypeStruct((2, 2, blk, blk), jnp.bfloat16),
        ),
        grid_spec=pltpu.PrefetchScalarGridSpec(
            num_scalar_prefetch=1,
            grid=(1,),
            in_specs=[
                pl.BlockSpec((2 * blk, blk), lambda s, place: (place[0], 0)),
                pl.BlockSpec((tall, blk), lambda s, place: (0, 0)),
                pl.BlockSpec((tall, blk), lambda s, place: (0, 0)),
                pl.BlockSpec((tall, blk), lambda s, place: (0, 0)),
                pl.BlockSpec(memory_space=pl.ANY),
            ],
            out_specs=(
                pl.BlockSpec((tall, blk), lambda s, place: (0, 0)),
                pl.BlockSpec((2, 2, blk, blk), lambda s, place: (0, 0, 0, 0)),
            ),
        ),
        compiler_params=pltpu.CompilerParams(vmem_limit_bytes=VMEM_LIMIT),
        cost_estimate=SMALL,
        name="right_roots",
    )(place, stats, kept, near, far, after)


def left_kernel(full_dim, place, stats_ref, a_ref, b_ref, out_ref):
    blk = stats_ref.shape[1]
    total = a_ref[...] + b_ref[b_ref.shape[0] - a_ref.shape[0] :, :]
    for b, root in enumerate(pair_roots(full_dim, stats_ref, total[:blk], total[blk : blk + 1])):
        high, low = split(root)
        out_ref[b, 0] = high
        out_ref[b, 1] = low


def left_roots(full_dim, place, stats, kept, came):
    blk = stats.shape[1]
    tall = blk + PAD
    return pl.pallas_call(
        functools.partial(left_kernel, full_dim),
        out_shape=jax.ShapeDtypeStruct((2, 2, blk, blk), jnp.bfloat16),
        grid_spec=pltpu.PrefetchScalarGridSpec(
            num_scalar_prefetch=1,
            grid=(1,),
            in_specs=[
                pl.BlockSpec((2 * blk, blk), lambda s, place: (place[1], 0)),
                pl.BlockSpec((tall, blk), lambda s, place: (0, 0)),
                pl.BlockSpec(came.shape, lambda s, place: (0, 0)),
            ],
            out_specs=pl.BlockSpec((2, 2, blk, blk), lambda s, place: (0, 0, 0, 0)),
        ),
        compiler_params=pltpu.CompilerParams(vmem_limit_bytes=VMEM_LIMIT),
        cost_estimate=SMALL,
        name="left_roots",
    )(place, stats, kept, came)


def raw_flip(place):
    return 2 + (place[0] & 1)


def put_roots(out_ref, at, body, diag):
    for b, root in enumerate(unpack(body, diag)):
        high, low = split(root)
        out_ref[2 * at + b, 0] = high
        out_ref[2 * at + b, 1] = low


def spread_kernel(*refs):
    out_ref = refs[-1]
    blk = out_ref.shape[-1]
    for at, ref in enumerate(refs[:-1]):
        put_roots(out_ref, at, ref[:blk, :], ref[blk : blk + 1, :])


def spread_roots(*packed):
    blk = packed[0].shape[1]
    return pl.pallas_call(
        spread_kernel,
        out_shape=jax.ShapeDtypeStruct((2 * len(packed), 2, blk, blk), jnp.bfloat16),
        compiler_params=pltpu.CompilerParams(vmem_limit_bytes=VMEM_LIMIT),
        cost_estimate=SMALL,
        name="spread_roots",
    )(*packed)


def cut_kernel(place, x_ref, xc_ref, out_ref):
    half = out_ref.shape[0] - PAD

    @pl.when((place[0] & 1) == 0)
    def _():
        out_ref[:half, :] = x_ref[:half, :]
        out_ref[half:, :] = x_ref[2 * half :, :]

    @pl.when((place[0] & 1) == 1)
    def _():
        out_ref[:half, :] = xc_ref[half : 2 * half, :]
        out_ref[half:, :] = xc_ref[2 * half :, :]


def cut(place, of_x, of_xc):
    tall, blk = of_x.shape
    whole = pl.BlockSpec((tall, blk), lambda s, place: (0, 0))
    return pl.pallas_call(
        cut_kernel,
        out_shape=jax.ShapeDtypeStruct((blk // 2 + PAD, blk), jnp.float32),
        grid_spec=pltpu.PrefetchScalarGridSpec(
            num_scalar_prefetch=1,
            grid=(1,),
            in_specs=[whole, whole],
            out_specs=pl.BlockSpec((blk // 2 + PAD, blk), lambda s, place: (0, 0)),
        ),
        compiler_params=pltpu.CompilerParams(vmem_limit_bytes=VMEM_LIMIT),
        cost_estimate=SMALL,
        name="cut",
    )(place, of_x, of_xc)


def rest_kernel(a_ref, out_ref):
    out_ref[...] = a_ref[a_ref.shape[0] - out_ref.shape[0] :, :]


def rest_of(value, rows):
    return pl.pallas_call(
        rest_kernel,
        out_shape=jax.ShapeDtypeStruct((value.shape[0] - rows, value.shape[1]), jnp.float32),
        compiler_params=pltpu.CompilerParams(vmem_limit_bytes=VMEM_LIMIT),
        cost_estimate=SMALL,
        name="rest_of",
    )(value)


def join_kernel(place, mine_ref, other_ref, out_ref, body):
    half = mine_ref.shape[0] - PAD
    core = place[0] & 1
    body[pl.ds(pl.multiple_of(core * half, half), half), :] = mine_ref[:half, :]
    body[pl.ds(pl.multiple_of((1 - core) * half, half), half), :] = other_ref[:half, :]
    put_roots(out_ref, 0, body[...], mine_ref[half : half + 1, :])


def join_roots(place, mine, other):
    tall, blk = mine.shape
    half = pl.BlockSpec((tall, blk), lambda s, place: (0, 0))
    return pl.pallas_call(
        join_kernel,
        out_shape=jax.ShapeDtypeStruct((2, 2, blk, blk), jnp.bfloat16),
        grid_spec=pltpu.PrefetchScalarGridSpec(
            num_scalar_prefetch=1,
            grid=(1,),
            in_specs=[half, half],
            out_specs=pl.BlockSpec((2, 2, blk, blk), lambda s, place: (0, 0, 0, 0)),
            scratch_shapes=[pltpu.VMEM((blk, blk), jnp.float32)],
        ),
        compiler_params=pltpu.CompilerParams(vmem_limit_bytes=VMEM_LIMIT),
        cost_estimate=SMALL,
        name="join_roots",
    )(place, mine, other)


def right_apply_kernel(width, carries, place, g_ref, right_ref, *rest):
    step = pl.program_id(0)
    out_refs = rest[-len(width) :]
    value = product(split(g_ref[...]), (right_ref[0, 0], right_ref[0, 1]))
    blk = value.shape[1]
    start = 0
    for size, ref in zip(width, out_refs):
        for b in range(start // blk, -(-(start + size) // blk)):
            low, high = max(start, b * blk), min(start + size, (b + 1) * blk)

            @pl.when(step == b)
            def _():
                ref[: value.shape[0], low - start : high - start] = value[:, low - b * blk : high - b * blk]

        start += size
    if carries:
        out_refs[0][value.shape[0] :, :] = rest[0][...]


def right_apply(place, tile, right, flip, right_at, first, width, under, after):
    rows = tile.shape[0] // 2
    blk = right.shape[-1]
    in_specs = [
        pl.BlockSpec((rows, blk), lambda s, place: (1 - place[1], (place[0] ^ flip(place)) * 2 + first + s)),
        pl.BlockSpec((1, 2, blk, blk), lambda s, place: (right_at(place) + first + s, 0, 0, 0)),
    ]
    operands = [tile, right]
    tall = rows
    if under is not None:
        tall += under.shape[0]
        in_specs.append(pl.BlockSpec(under.shape, lambda s, place: (0, 0)))
        operands.append(under)
    return pl.pallas_call(
        functools.partial(right_apply_kernel, width, under is not None),
        out_shape=tuple(jax.ShapeDtypeStruct((tall, w), jnp.float32) for w in width),
        grid_spec=pltpu.PrefetchScalarGridSpec(
            num_scalar_prefetch=1,
            grid=(sum(width) // blk,),
            in_specs=in_specs + [pl.BlockSpec(memory_space=pl.ANY)] * len(after),
            out_specs=tuple(pl.BlockSpec((tall, w), lambda s, place: (0, 0)) for w in width),
        ),
        compiler_params=pltpu.CompilerParams(vmem_limit_bytes=VMEM_LIMIT),
        cost_estimate=SMALL,
        name="right_apply",
    )(place, *operands, *after)


def left_product(left_ref, value, out_ref):
    blk = left_ref.shape[-1]
    for i in range(value.shape[0] // blk):
        part = split(value[i * blk : (i + 1) * blk])
        out_ref[i * blk : (i + 1) * blk, :] = product((left_ref[i, 0], left_ref[i, 1]), part)


def update_kernel(place, g_ref, left_ref, right_ref, *rest):
    half = product(split(g_ref[...]), (right_ref[0, 0], right_ref[0, 1]))
    left_product(left_ref, half, rest[-2])
    rest[-1][...] = jnp.zeros_like(rest[-1])


def finish_kernel(place, half_ref, left_ref, out_before, out_ref, done_ref):
    left_product(left_ref, half_ref[...], out_ref)
    done_ref[...] = jnp.zeros_like(done_ref)


def into_output(kernel, name, place, source, left, right, out, out_shape, wide, steps, g_map, right_at, out_map):
    rows = out_shape[0]
    blk = left.shape[-1]
    in_specs = [
        pl.BlockSpec((rows, wide), g_map),
        pl.BlockSpec((2, 2, blk, blk), lambda s, place: (0, 0, 0, 0)),
    ]
    operands = [source, left]
    if right is not None:
        in_specs.append(pl.BlockSpec((1, 2, blk, blk), lambda s, place: (right_at + s, 0, 0, 0)))
        operands.append(right)
    aliases = {}
    if out is not None:
        aliases = {1 + len(operands): 0}
        in_specs.append(pl.BlockSpec(memory_space=pl.ANY))
        operands.append(out)
    return pl.pallas_call(
        kernel,
        out_shape=(jax.ShapeDtypeStruct(out_shape, jnp.float32), jax.ShapeDtypeStruct((8, 128), jnp.float32)),
        grid_spec=pltpu.PrefetchScalarGridSpec(
            num_scalar_prefetch=1,
            grid=(steps,),
            in_specs=in_specs,
            out_specs=(pl.BlockSpec((rows, wide), out_map), pl.BlockSpec((8, 128), lambda s, place: (0, 0))),
        ),
        input_output_aliases=aliases,
        compiler_params=pltpu.CompilerParams(vmem_limit_bytes=VMEM_LIMIT),
        cost_estimate=SMALL,
        name=name,
    )(place, *operands)


def exchange_device(full_dim, n_row, grads, left_stats, right_stats):
    tile_rows, tile_cols = grads.shape[1:]
    blk = left_stats.shape[2]
    tile = pltpu.with_memory_space_constraint(grads.reshape(tile_rows, tile_cols), pltpu.HBM)
    lstats = left_stats.reshape(tile_rows, blk)
    rstats = right_stats.reshape(tile_cols, blk)
    r = lax.axis_index("row")
    c = lax.axis_index("col")
    place = jnp.stack([r, c]).astype(jnp.int32)
    rows = tile_rows // 2
    shape = (rows, 2 * tile_cols)
    halves = tile_cols // blk

    def over(axis, value):
        if axis == "y":
            return lax.ppermute(value, "col", [(0, 1), (1, 0)])
        flip = {"core": 1, "x": 2}[axis]
        return lax.ppermute(value, "row", [(i, i ^ flip) for i in range(n_row)])

    first = take(place, tile, blk)
    raw = over("y", first)

    send_on, send, keep_on, keep = right_grams(place, tile, blk, first)
    near_on = over("core", send_on)
    near = over("core", send)
    lsend, lkeep = left_grams(place, tile, blk, send)
    far = over("x", fold(keep_on, near_on))
    own, roots_own = right_roots(full_dim, place, rstats, keep, near, far, lsend)

    own_pair, core_pair = (lambda place: 0), (lambda place: 1)
    last_pair = lambda place: 3 - (place[0] & 1)
    begin = lambda place: 0
    last_at = lambda place: 2 * (1 - (place[0] & 1))
    tail = (blk, blk // 2, blk // 2)

    held = right_apply(place, tile, roots_own, own_pair, begin, 0, (blk,), lsend, ())
    came_0a = over("y", held[0])
    own = hold(own, raw, held[0])
    own_c = over("core", own)
    own_x = over("x", own)
    own_xc = over("core", own_x)
    held = right_apply(place, tile, roots_own, own_pair, begin, 1, (blk,), None, (own,))
    came_0b = over("y", held[0])
    roots_core = spread_roots(own_c)
    held = right_apply(place, tile, roots_core, core_pair, begin, 0, (2 * blk,), None, (came_0a, own_xc))
    came_1 = over("y", held[0])
    own_x = hold(own_x, came_0b)
    roots_far = spread_roots(own_x, own_xc)
    held = right_apply(place, tile, roots_far, last_pair, last_at, 0, tail[:1], cut(place, own_x, own_xc), ())
    came_2 = [over("y", held[0])]
    mine = rest_of(came_2[0], rows)
    roots_raw = join_roots(place, mine, over("core", mine))

    left = left_roots(full_dim, place, lstats, lkeep, came_0a)

    def own_cols(base):
        return lambda s, place: (place[1], (place[0] ^ (base + s // 2)) * 2 + s % 2)

    out = None
    for base, roots in ((0, roots_own), (1, roots_core), (2, roots_far)):
        at = own_cols(base)
        out, done = into_output(
            update_kernel, "update", place, tile, left, roots, out, shape, blk, roots.shape[0], at, 0,
            lambda s, place, at=at: (0, place[1] * halves + at(s, place)[1]),
        )

    def finish(out, value, wide, width, start, flip):
        per_pair = 2 * blk // wide
        return into_output(
            finish_kernel, "finish", place, value, left, None, out, shape, wide, width // wide,
            lambda s, place: (0, s), 0,
            lambda s, place: (
                0,
                (1 - place[1]) * (tile_cols // wide) + (place[0] ^ flip(place)) * per_pair + start // wide + s,
            ),
        )

    for b, value in enumerate((came_0a, came_0b)):
        out, done = finish(out, value, blk, blk, b * blk, own_pair)
    held = right_apply(place, tile, roots_far, last_pair, last_at, 1, tail[1:], None, (came_1, done))
    came_2 += [over("y", half) for half in held]
    out, done = finish(out, came_1, blk, 2 * blk, 0, core_pair)
    out, done = into_output(
        update_kernel, "update", place, raw, left, roots_raw, out, shape, blk, 2,
        lambda s, place: (0, s), 0,
        lambda s, place: (0, (1 - place[1]) * halves + (place[0] ^ raw_flip(place)) * 2 + s),
    )
    start = 0
    for wide, value in zip(tail, came_2):
        out, done = finish(out, value, wide, wide, start, last_pair)
        start += wide
    return out.reshape(1, rows, 2 * tile_cols)


def per_device(n_row, n_col, grads, left_stats, right_stats):
    mats, tile_rows, tile_cols = grads.shape
    blk = left_stats.shape[2]
    full_dim = tile_cols * n_col
    if mats == 1 and n_col == 2 and n_row == 4 and tile_rows == 4 * blk and tile_cols == 8 * blk:
        return exchange_device(full_dim, n_row, grads, left_stats, right_stats)
    return general_device(full_dim, grads, left_stats, right_stats)


def solution(mesh):
    return jax.shard_map(
        functools.partial(per_device, mesh.shape["row"], mesh.shape["col"]),
        mesh=mesh,
        in_specs=(P("mat", "row", "col"), P("mat", "row", None), P("mat", "col", None)),
        out_specs=P("mat", ("row", "col"), None),
        check_vma=False,
    )
```

```python
import functools

import jax
import jax.numpy as jnp
from jax import lax
from jax.experimental import pallas as pl
from jax.experimental.pallas import tpu as pltpu
from jax.sharding import PartitionSpec as P

ITERS = 3
beta_mix = 0.5
eps_shift = 0.001
PAD = 8
VMEM_LIMIT = 24 * 1024 * 1024
SMALL = pl.CostEstimate(flops=1, bytes_accessed=1, transcendentals=0)


def matmul(left, right):
    return jnp.einsum("...ij,...jk->...ik", left, right, precision=lax.Precision.HIGHEST)


def newton_root(factor):
    size = factor.shape[-1]
    ident = jnp.eye(size, dtype=jnp.float32)
    scale = jnp.sqrt(jnp.sum(factor * factor, axis=(-2, -1), keepdims=True))
    moving = factor / scale
    result = jnp.broadcast_to(ident, factor.shape)
    for count in range(ITERS):
        step_mat = (5.0 * ident - moving) * 0.25
        result = matmul(result, step_mat)
        squared = matmul(step_mat, step_mat)
        moving = matmul(matmul(squared, squared), moving)
    return result * jnp.power(scale, -0.25)


def general_device(full_dim, grads, left_stats, right_stats):
    mats, tile_rows, tile_cols = grads.shape
    blk = left_stats.shape[2]
    row_blocks = tile_rows // blk
    col_blocks = tile_cols // blk
    ident = jnp.eye(blk, dtype=jnp.float32)
    by_rows = grads.reshape(mats, row_blocks, blk, tile_cols)
    left_part = jnp.einsum("mibd,mied->mibe", by_rows, by_rows, precision=lax.Precision.HIGHEST) / full_dim
    by_cols = grads.reshape(mats, tile_rows, col_blocks, blk)
    right_part = (
        jnp.einsum("mdjb,mdje->mjbe", by_cols, by_cols, precision=lax.Precision.HIGHEST) / full_dim
    )
    left_gram = lax.psum(left_part, "col")
    right_gram = lax.psum(right_part, "row")
    left_factor = (
        beta_mix * left_stats.reshape(mats, row_blocks, blk, blk)
        + (1.0 - beta_mix) * left_gram
        + eps_shift * ident
    )
    right_factor = (
        beta_mix * right_stats.reshape(mats, col_blocks, blk, blk)
        + (1.0 - beta_mix) * right_gram
        + eps_shift * ident
    )
    left_root = newton_root(left_factor)
    right_root = newton_root(right_factor)
    half = jnp.einsum("mibe,mied->mibd", left_root, by_rows, precision=lax.Precision.HIGHEST)
    half = half.reshape(mats, tile_rows, col_blocks, blk)
    full = jnp.einsum("mdjb,mjbe->mdje", half, right_root, precision=lax.Precision.HIGHEST)
    full = full.reshape(mats, tile_rows, tile_cols)
    return lax.all_to_all(full, "col", split_axis=1, concat_axis=2, tiled=True)


def split(value):
    high = value.astype(jnp.bfloat16)
    low = (value - high.astype(jnp.float32)).astype(jnp.bfloat16)
    return high, low


def dot(left, right, dims=((1,), (0,))):
    return lax.dot_general(left, right, (dims, ((), ())), preferred_element_type=jnp.float32)


def product(left, right):
    lh, ll = left
    rh, rl = right
    return dot(lh, rh) + (dot(lh, rl) + dot(ll, rh))


def places(blk):
    rows = lax.broadcasted_iota(jnp.int32, (blk, blk), 0)
    cols = lax.broadcasted_iota(jnp.int32, (blk, blk), 1)
    return rows, cols


def pack(first, second):
    blk = first.shape[0]
    rows, cols = places(blk)
    body = jnp.where(rows <= cols, first, second)
    diag = jnp.sum(jnp.where(rows == cols, second, 0.0), axis=0, keepdims=True)
    return body, jnp.broadcast_to(diag, (PAD, blk))


def unpack(body, diag):
    blk = body.shape[0]
    rows, cols = places(blk)
    turned = body.T
    first = jnp.where(rows <= cols, body, turned)
    second = jnp.where(rows > cols, body, jnp.where(rows == cols, diag, turned))
    return first, second


def right_gram_kernel(place, g_ref, after_ref, *out_refs):
    step = pl.program_id(0)
    blk = g_ref.shape[1] // 2
    high, low = split(g_ref[...])
    grams = []
    for b in range(2):
        hb = high[:, b * blk : (b + 1) * blk]
        lb = low[:, b * blk : (b + 1) * blk]
        both = dot(hb, hb, ((0,), (0,)))
        cross = dot(hb, lb, ((0,), (0,)))
        grams.append(both + (cross + cross.T))
    body, diag = pack(*grams)

    for at, ref in enumerate(out_refs):

        @pl.when(step == at)
        def _():
            ref[:blk, :] = body
            ref[blk:, :] = diag


def right_grams(place, tile, blk, flips, after):
    rows = tile.shape[0]
    tall = blk + PAD
    flip = lambda s: jnp.where(s == 0, flips[0], flips[1])
    return pl.pallas_call(
        right_gram_kernel,
        out_shape=(jax.ShapeDtypeStruct((tall, blk), jnp.float32),) * 2,
        grid_spec=pltpu.PrefetchScalarGridSpec(
            num_scalar_prefetch=1,
            grid=(2,),
            in_specs=[
                pl.BlockSpec((rows, 2 * blk), lambda s, place: (0, place[0] ^ flip(s))),
                pl.BlockSpec(memory_space=pl.ANY),
            ],
            out_specs=(pl.BlockSpec((tall, blk), lambda s, place: (0, 0)),) * 2,
        ),
        compiler_params=pltpu.CompilerParams(vmem_limit_bytes=VMEM_LIMIT),
        cost_estimate=SMALL,
        name="right_grams",
    )(place, tile, after)


def left_gram_kernel(place, g_ref, after_ref, out_ref, lhh, lcross):
    step = pl.program_id(0)
    last = pl.num_programs(0) - 1
    blk = lhh.shape[-1]
    high, low = split(g_ref[...])
    for i in range(2):
        hi = high[i * blk : (i + 1) * blk, :]
        lo = low[i * blk : (i + 1) * blk, :]
        both = dot(hi, hi, ((1,), (1,)))
        cross = dot(lo, hi, ((1,), (1,)))

        @pl.when(step == 0)
        def _():
            lhh[i] = both
            lcross[i] = cross

        @pl.when(step > 0)
        def _():
            lhh[i] += both
            lcross[i] += cross

    @pl.when(step == last)
    def _():
        body, diag = pack(*(lhh[b] + (lcross[b] + lcross[b].T) for b in range(2)))
        out_ref[:blk, :] = body
        out_ref[blk:, :] = diag


def left_grams(place, tile, blk, at, after):
    width = tile.shape[1]
    tall = blk + PAD
    return pl.pallas_call(
        left_gram_kernel,
        out_shape=jax.ShapeDtypeStruct((tall, blk), jnp.float32),
        grid_spec=pltpu.PrefetchScalarGridSpec(
            num_scalar_prefetch=1,
            grid=(width // (4 * blk),),
            in_specs=[
                pl.BlockSpec((2 * blk, 4 * blk), lambda s, place: (at(place), s)),
                pl.BlockSpec(memory_space=pl.ANY),
            ],
            out_specs=pl.BlockSpec((tall, blk), lambda s, place: (0, 0)),
            scratch_shapes=[
                pltpu.VMEM((2, blk, blk), jnp.float32),
                pltpu.VMEM((2, blk, blk), jnp.float32),
            ],
        ),
        compiler_params=pltpu.CompilerParams(vmem_limit_bytes=VMEM_LIMIT),
        cost_estimate=SMALL,
        name="left_grams",
    )(place, tile, after)


def take_kernel(place, g_ref, out_ref, sems):
    rows, wide = out_ref.shape
    count = sems.shape[0]
    part = rows // count
    start = pl.multiple_of((place[0] ^ raw_flip(place)) * wide, wide)
    copies = []
    for k in range(count):
        top = pl.multiple_of((1 - place[1]) * rows + k * part, part)
        copies.append(
            pltpu.make_async_copy(
                g_ref.at[pl.ds(top, part), pl.ds(start, wide)], out_ref.at[pl.ds(k * part, part), :], sems.at[k]
            )
        )
    for copy in copies:
        copy.start()
    for copy in copies:
        copy.wait()


def take(place, tile, blk):
    return pl.pallas_call(
        take_kernel,
        out_shape=jax.ShapeDtypeStruct((tile.shape[0] // 2, 2 * blk), jnp.float32),
        grid_spec=pltpu.PrefetchScalarGridSpec(
            num_scalar_prefetch=1,
            grid=(1,),
            in_specs=[pl.BlockSpec(memory_space=pl.ANY)],
            out_specs=pl.BlockSpec(memory_space=pl.ANY),
            scratch_shapes=[pltpu.SemaphoreType.DMA((8,))],
        ),
        compiler_params=pltpu.CompilerParams(vmem_limit_bytes=VMEM_LIMIT),
        cost_estimate=SMALL,
        name="take",
    )(place, tile)


def fold_kernel(a_ref, b_ref, out_ref):
    out_ref[...] = a_ref[...] + b_ref[...]


def fold(kept, near):
    return pl.pallas_call(
        fold_kernel,
        out_shape=jax.ShapeDtypeStruct(kept.shape, jnp.float32),
        compiler_params=pltpu.CompilerParams(vmem_limit_bytes=VMEM_LIMIT),
        cost_estimate=SMALL,
        name="fold",
    )(kept, near)


def hold_kernel(a_ref, *rest):
    out_ref = rest[-1]
    out_ref[...] = a_ref[...]


def hold(value, *after):
    return pl.pallas_call(
        hold_kernel,
        out_shape=jax.ShapeDtypeStruct(value.shape, jnp.float32),
        in_specs=[pl.BlockSpec(memory_space=pltpu.VMEM)] + [pl.BlockSpec(memory_space=pl.ANY)] * len(after),
        compiler_params=pltpu.CompilerParams(vmem_limit_bytes=VMEM_LIMIT),
        cost_estimate=SMALL,
        name="hold",
    )(value, *after)


def pair_roots(full_dim, stats_ref, body, diag):
    blk = body.shape[0]
    rows, cols = places(blk)
    ident = jnp.where(rows == cols, 1.0, 0.0)
    moving, scales = [], []
    for b, gram in enumerate(unpack(body, diag)):
        factor = (
            beta_mix * stats_ref[b * blk : (b + 1) * blk, :]
            + (1.0 - beta_mix) * (gram / full_dim)
            + eps_shift * ident
        )
        scale = jnp.sqrt(jnp.sum(factor * factor, keepdims=True))
        moving.append(factor / scale)
        scales.append(scale)
    result = None
    for count in range(ITERS):
        steps = [(5.0 * ident - m) * 0.25 for m in moving]
        parts = [split(s) for s in steps]
        if result is None:
            result = steps
        else:
            result = [product(split(r), p) for r, p in zip(result, parts)]
        if count < ITERS - 1:
            squared = [split(product(p, p)) for p in parts]
            fourth = [split(product(s, s)) for s in squared]
            moving = [product(f, split(m)) for f, m in zip(fourth, moving)]
    return [r * jnp.exp(-0.25 * jnp.log(s)) for r, s in zip(result, scales)]


def right_kernel(full_dim, place, stats_ref, a_ref, b_ref, c_ref, g_ref, under_ref, out_ref, halves_ref, half_ref):
    blk = stats_ref.shape[1]
    rows = g_ref.shape[0]
    total = a_ref[...] + b_ref[...] + c_ref[...]
    roots = pair_roots(full_dim, stats_ref, total[:blk], total[blk : blk + 1])
    half_ref[:rows, :] = product(split(g_ref[...]), split(roots[0]))
    half_ref[rows:, :] = under_ref[...]
    body, diag = pack(*roots)
    out_ref[:blk, :] = body
    out_ref[blk:, :] = diag
    for b, root in enumerate(roots):
        high, low = split(root)
        halves_ref[b, 0] = high
        halves_ref[b, 1] = low


def right_roots(full_dim, place, stats, kept, near, far, tile, under):
    blk = stats.shape[1]
    tall = blk + PAD
    rows = tile.shape[0] // 2
    flat = pl.BlockSpec((tall, blk), lambda s, place: (0, 0))
    return pl.pallas_call(
        functools.partial(right_kernel, full_dim),
        out_shape=(
            jax.ShapeDtypeStruct((tall, blk), jnp.float32),
            jax.ShapeDtypeStruct((2, 2, blk, blk), jnp.bfloat16),
            jax.ShapeDtypeStruct((rows + tall, blk), jnp.float32),
        ),
        grid_spec=pltpu.PrefetchScalarGridSpec(
            num_scalar_prefetch=1,
            grid=(1,),
            in_specs=[
                pl.BlockSpec((2 * blk, blk), lambda s, place: (place[0], 0)),
                flat,
                flat,
                flat,
                pl.BlockSpec((rows, blk), lambda s, place: (1 - place[1], place[0] * 2)),
                flat,
            ],
            out_specs=(
                flat,
                pl.BlockSpec((2, 2, blk, blk), lambda s, place: (0, 0, 0, 0)),
                pl.BlockSpec((rows + tall, blk), lambda s, place: (0, 0)),
            ),
        ),
        compiler_params=pltpu.CompilerParams(vmem_limit_bytes=VMEM_LIMIT),
        cost_estimate=SMALL,
        name="right_roots",
    )(place, stats, kept, near, far, tile, under)


def left_kernel(full_dim, place, stats_ref, a_ref, b_ref, out_ref):
    blk = stats_ref.shape[1]
    total = a_ref[...] + b_ref[b_ref.shape[0] - a_ref.shape[0] :, :]
    for b, root in enumerate(pair_roots(full_dim, stats_ref, total[:blk], total[blk : blk + 1])):
        high, low = split(root)
        out_ref[b, 0] = high
        out_ref[b, 1] = low


def left_roots(full_dim, place, stats, kept, came):
    blk = stats.shape[1]
    tall = blk + PAD
    return pl.pallas_call(
        functools.partial(left_kernel, full_dim),
        out_shape=jax.ShapeDtypeStruct((2, 2, blk, blk), jnp.bfloat16),
        grid_spec=pltpu.PrefetchScalarGridSpec(
            num_scalar_prefetch=1,
            grid=(1,),
            in_specs=[
                pl.BlockSpec((2 * blk, blk), lambda s, place: (place[1], 0)),
                pl.BlockSpec((tall, blk), lambda s, place: (0, 0)),
                pl.BlockSpec(came.shape, lambda s, place: (0, 0)),
            ],
            out_specs=pl.BlockSpec((2, 2, blk, blk), lambda s, place: (0, 0, 0, 0)),
        ),
        compiler_params=pltpu.CompilerParams(vmem_limit_bytes=VMEM_LIMIT),
        cost_estimate=SMALL,
        name="left_roots",
    )(place, stats, kept, came)


def raw_flip(place):
    return 2 + (place[0] & 1)


def put_roots(out_ref, at, body, diag):
    for b, root in enumerate(unpack(body, diag)):
        high, low = split(root)
        out_ref[2 * at + b, 0] = high
        out_ref[2 * at + b, 1] = low


def spread_kernel(*refs):
    out_ref = refs[-1]
    blk = out_ref.shape[-1]
    for at, ref in enumerate(refs[:-1]):
        put_roots(out_ref, at, ref[:blk, :], ref[blk : blk + 1, :])


def spread_roots(*packed):
    blk = packed[0].shape[1]
    return pl.pallas_call(
        spread_kernel,
        out_shape=jax.ShapeDtypeStruct((2 * len(packed), 2, blk, blk), jnp.bfloat16),
        compiler_params=pltpu.CompilerParams(vmem_limit_bytes=VMEM_LIMIT),
        cost_estimate=SMALL,
        name="spread_roots",
    )(*packed)


def cut_kernel(place, x_ref, xc_ref, out_ref):
    half = out_ref.shape[0] - PAD

    @pl.when((place[0] & 1) == 0)
    def _():
        out_ref[:half, :] = x_ref[:half, :]
        out_ref[half:, :] = x_ref[2 * half :, :]

    @pl.when((place[0] & 1) == 1)
    def _():
        out_ref[:half, :] = xc_ref[half : 2 * half, :]
        out_ref[half:, :] = xc_ref[2 * half :, :]


def cut(place, of_x, of_xc):
    tall, blk = of_x.shape
    whole = pl.BlockSpec((tall, blk), lambda s, place: (0, 0))
    return pl.pallas_call(
        cut_kernel,
        out_shape=jax.ShapeDtypeStruct((blk // 2 + PAD, blk), jnp.float32),
        grid_spec=pltpu.PrefetchScalarGridSpec(
            num_scalar_prefetch=1,
            grid=(1,),
            in_specs=[whole, whole],
            out_specs=pl.BlockSpec((blk // 2 + PAD, blk), lambda s, place: (0, 0)),
        ),
        compiler_params=pltpu.CompilerParams(vmem_limit_bytes=VMEM_LIMIT),
        cost_estimate=SMALL,
        name="cut",
    )(place, of_x, of_xc)


def rest_kernel(a_ref, out_ref):
    out_ref[...] = a_ref[a_ref.shape[0] - out_ref.shape[0] :, :]


def rest_of(value, rows):
    return pl.pallas_call(
        rest_kernel,
        out_shape=jax.ShapeDtypeStruct((value.shape[0] - rows, value.shape[1]), jnp.float32),
        compiler_params=pltpu.CompilerParams(vmem_limit_bytes=VMEM_LIMIT),
        cost_estimate=SMALL,
        name="rest_of",
    )(value)


def join_kernel(place, mine_ref, other_ref, out_ref, body):
    half = mine_ref.shape[0] - PAD
    core = place[0] & 1
    body[pl.ds(pl.multiple_of(core * half, half), half), :] = mine_ref[:half, :]
    body[pl.ds(pl.multiple_of((1 - core) * half, half), half), :] = other_ref[:half, :]
    put_roots(out_ref, 0, body[...], mine_ref[half : half + 1, :])


def join_roots(place, mine, other):
    tall, blk = mine.shape
    half = pl.BlockSpec((tall, blk), lambda s, place: (0, 0))
    return pl.pallas_call(
        join_kernel,
        out_shape=jax.ShapeDtypeStruct((2, 2, blk, blk), jnp.bfloat16),
        grid_spec=pltpu.PrefetchScalarGridSpec(
            num_scalar_prefetch=1,
            grid=(1,),
            in_specs=[half, half],
            out_specs=pl.BlockSpec((2, 2, blk, blk), lambda s, place: (0, 0, 0, 0)),
            scratch_shapes=[pltpu.VMEM((blk, blk), jnp.float32)],
        ),
        compiler_params=pltpu.CompilerParams(vmem_limit_bytes=VMEM_LIMIT),
        cost_estimate=SMALL,
        name="join_roots",
    )(place, mine, other)


def right_apply_kernel(width, carries, place, g_ref, right_ref, *rest):
    step = pl.program_id(0)
    out_refs = rest[-len(width) :]
    value = product(split(g_ref[...]), (right_ref[0, 0], right_ref[0, 1]))
    blk = value.shape[1]
    start = 0
    for size, ref in zip(width, out_refs):
        for b in range(start // blk, -(-(start + size) // blk)):
            low, high = max(start, b * blk), min(start + size, (b + 1) * blk)

            @pl.when(step == b)
            def _():
                ref[: value.shape[0], low - start : high - start] = value[:, low - b * blk : high - b * blk]

        start += size
    if carries:
        out_refs[0][value.shape[0] :, :] = rest[0][...]


def right_apply(place, tile, right, flip, right_at, first, width, under, after):
    rows = tile.shape[0] // 2
    blk = right.shape[-1]
    in_specs = [
        pl.BlockSpec((rows, blk), lambda s, place: (1 - place[1], (place[0] ^ flip(place)) * 2 + first + s)),
        pl.BlockSpec((1, 2, blk, blk), lambda s, place: (right_at(place) + first + s, 0, 0, 0)),
    ]
    operands = [tile, right]
    tall = rows
    if under is not None:
        tall += under.shape[0]
        in_specs.append(pl.BlockSpec(under.shape, lambda s, place: (0, 0)))
        operands.append(under)
    return pl.pallas_call(
        functools.partial(right_apply_kernel, width, under is not None),
        out_shape=tuple(jax.ShapeDtypeStruct((tall, w), jnp.float32) for w in width),
        grid_spec=pltpu.PrefetchScalarGridSpec(
            num_scalar_prefetch=1,
            grid=(sum(width) // blk,),
            in_specs=in_specs + [pl.BlockSpec(memory_space=pl.ANY)] * len(after),
            out_specs=tuple(pl.BlockSpec((tall, w), lambda s, place: (0, 0)) for w in width),
        ),
        compiler_params=pltpu.CompilerParams(vmem_limit_bytes=VMEM_LIMIT),
        cost_estimate=SMALL,
        name="right_apply",
    )(place, *operands, *after)


def left_product(left_ref, value, out_ref):
    blk = left_ref.shape[-1]
    for i in range(value.shape[0] // blk):
        part = split(value[i * blk : (i + 1) * blk])
        out_ref[i * blk : (i + 1) * blk, :] = product((left_ref[i, 0], left_ref[i, 1]), part)


def update_kernel(place, g_ref, left_ref, right_ref, *rest):
    half = product(split(g_ref[...]), (right_ref[0, 0], right_ref[0, 1]))
    left_product(left_ref, half, rest[-2])
    rest[-1][...] = jnp.zeros_like(rest[-1])


def finish_kernel(column, width, place, half_ref, left_ref, out_before, out_ref, done_ref, stage, sems):
    blk = left_ref.shape[-1]
    start = pl.multiple_of(column(place), width)
    copies = []
    for i in range(left_ref.shape[0]):
        rows = pl.ds(i * blk, blk)
        for b in range(0, width, blk):
            cols = pl.ds(b, min(blk, width))
            stage[rows, cols] = product((left_ref[i, 0], left_ref[i, 1]), split(half_ref[rows, cols]))
        copies.append(
            pltpu.make_async_copy(stage.at[rows, :], out_ref.at[rows, pl.ds(start, width)], sems.at[i])
        )
        copies[i].start()
    done_ref[...] = jnp.zeros_like(done_ref)
    for copy in copies:
        copy.wait()


def finish(place, half, left, out, column):
    width = half.shape[1]
    rows = out.shape[0]
    vmem = pl.BlockSpec(memory_space=pltpu.VMEM)
    return pl.pallas_call(
        functools.partial(finish_kernel, column, width),
        out_shape=(jax.ShapeDtypeStruct(out.shape, jnp.float32), jax.ShapeDtypeStruct((8, 128), jnp.float32)),
        in_specs=[pl.BlockSpec(memory_space=pltpu.SMEM), vmem, vmem, pl.BlockSpec(memory_space=pl.ANY)],
        out_specs=(pl.BlockSpec(memory_space=pl.ANY), vmem),
        scratch_shapes=[pltpu.VMEM((rows, width), jnp.float32), pltpu.SemaphoreType.DMA((left.shape[0],))],
        input_output_aliases={3: 0},
        compiler_params=pltpu.CompilerParams(vmem_limit_bytes=VMEM_LIMIT),
        cost_estimate=SMALL,
        name="finish",
    )(place, half, left, out)


def update(place, source, left, right, out, out_shape, g_map, out_map):
    rows = out_shape[0]
    blk = left.shape[-1]
    in_specs = [
        pl.BlockSpec((rows, blk), g_map),
        pl.BlockSpec((2, 2, blk, blk), lambda s, place: (0, 0, 0, 0)),
        pl.BlockSpec((1, 2, blk, blk), lambda s, place: (s, 0, 0, 0)),
    ]
    operands = [source, left, right]
    aliases = {}
    if out is not None:
        aliases = {1 + len(operands): 0}
        in_specs.append(pl.BlockSpec(memory_space=pl.ANY))
        operands.append(out)
    return pl.pallas_call(
        update_kernel,
        out_shape=(jax.ShapeDtypeStruct(out_shape, jnp.float32), jax.ShapeDtypeStruct((8, 128), jnp.float32)),
        grid_spec=pltpu.PrefetchScalarGridSpec(
            num_scalar_prefetch=1,
            grid=(right.shape[0],),
            in_specs=in_specs,
            out_specs=(pl.BlockSpec((rows, blk), out_map), pl.BlockSpec((8, 128), lambda s, place: (0, 0))),
        ),
        input_output_aliases=aliases,
        compiler_params=pltpu.CompilerParams(vmem_limit_bytes=VMEM_LIMIT),
        cost_estimate=SMALL,
        name="update",
    )(place, *operands)


def exchange_device(full_dim, n_row, grads, left_stats, right_stats):
    tile_rows, tile_cols = grads.shape[1:]
    blk = left_stats.shape[2]
    tile = pltpu.with_memory_space_constraint(grads.reshape(tile_rows, tile_cols), pltpu.HBM)
    lstats = left_stats.reshape(tile_rows, blk)
    rstats = right_stats.reshape(tile_cols, blk)
    r = lax.axis_index("row")
    c = lax.axis_index("col")
    place = jnp.stack([r, c]).astype(jnp.int32)
    rows = tile_rows // 2
    shape = (rows, 2 * tile_cols)
    halves = tile_cols // blk

    def over(axis, value):
        if axis == "y":
            return lax.ppermute(value, "col", [(0, 1), (1, 0)])
        flip = {"core": 1, "x": 2}[axis]
        return lax.ppermute(value, "row", [(i, i ^ flip) for i in range(n_row)])

    first = take(place, tile, blk)
    raw = over("y", first)

    send_on, keep_on = right_grams(place, tile, blk, (3, 2), first)
    near_on = over("core", send_on)
    send, keep = right_grams(place, tile, blk, (1, 0), keep_on)
    near = over("core", send)
    far = over("x", fold(keep_on, near_on))
    lsend = left_grams(place, tile, blk, lambda place: 1 - place[1], send)

    own_pair, core_pair = (lambda place: 0), (lambda place: 1)
    last_pair = lambda place: 3 - (place[0] & 1)
    begin = lambda place: 0
    last_at = lambda place: 2 * (1 - (place[0] & 1))
    tail = (blk, blk // 2, blk // 2)

    own, roots_own, half = right_roots(full_dim, place, rstats, keep, near, far, tile, lsend)
    came_0a = over("y", half)
    own = hold(own, raw, half)
    lkeep = left_grams(place, tile, blk, lambda place: place[1], own)
    own_c = over("core", own)
    own_x = over("x", own)
    own_xc = over("core", own_x)
    held = right_apply(place, tile, roots_own, own_pair, begin, 1, (blk,), None, (lkeep,))
    came_0b = over("y", held[0])
    roots_core = spread_roots(own_c)
    held = right_apply(place, tile, roots_core, core_pair, begin, 0, (2 * blk,), None, (came_0a, own_xc))
    came_1 = over("y", held[0])
    own_x = hold(own_x, came_0b)
    roots_far = spread_roots(own_x, own_xc)
    held = right_apply(place, tile, roots_far, last_pair, last_at, 0, tail[:1], cut(place, own_x, own_xc), ())
    came_2 = [over("y", held[0])]
    mine = rest_of(came_2[0], rows)
    roots_raw = join_roots(place, mine, over("core", mine))

    left = left_roots(full_dim, place, lstats, lkeep, came_0a)

    def own_cols(base):
        return lambda s, place: (place[1], (place[0] ^ (base + s // 2)) * 2 + s % 2)

    out = None
    for base, roots in ((0, roots_own), (1, roots_core), (2, roots_far)):
        at = own_cols(base)
        out, done = update(
            place, tile, left, roots, out, shape, at,
            lambda s, place, at=at: (0, place[1] * halves + at(s, place)[1]),
        )

    def crossed(start, flip):
        return lambda place: (1 - place[1]) * tile_cols + (place[0] ^ flip(place)) * 2 * blk + start

    for b, value in enumerate((came_0a, came_0b)):
        out, done = finish(place, value, left, out, crossed(b * blk, own_pair))
    out, done = finish(place, came_1, left, out, crossed(0, core_pair))
    held = right_apply(place, tile, roots_far, last_pair, last_at, 1, tail[1:], None, (came_1, done))
    came_2 += [over("y", half) for half in held]
    out, done = update(
        place, raw, left, roots_raw, out, shape,
        lambda s, place: (0, s),
        lambda s, place: (0, (1 - place[1]) * halves + (place[0] ^ raw_flip(place)) * 2 + s),
    )
    start = 0
    for wide, value in zip(tail, came_2):
        out, done = finish(place, value, left, out, crossed(start, last_pair))
        start += wide
    return out.reshape(1, rows, 2 * tile_cols)


def per_device(n_row, n_col, grads, left_stats, right_stats):
    mats, tile_rows, tile_cols = grads.shape
    blk = left_stats.shape[2]
    full_dim = tile_cols * n_col
    if mats == 1 and n_col == 2 and n_row == 4 and tile_rows == 4 * blk and tile_cols == 8 * blk:
        return exchange_device(full_dim, n_row, grads, left_stats, right_stats)
    return general_device(full_dim, grads, left_stats, right_stats)


def solution(mesh):
    return jax.shard_map(
        functools.partial(per_device, mesh.shape["row"], mesh.shape["col"]),
        mesh=mesh,
        in_specs=(P("mat", "row", "col"), P("mat", "row", None), P("mat", "col", None)),
        out_specs=P("mat", ("row", "col"), None),
        check_vma=False,
    )
```

```python
import functools

import jax
import jax.numpy as jnp
from jax import lax
from jax.experimental import pallas as pl
from jax.experimental.pallas import tpu as pltpu
from jax.sharding import PartitionSpec as P

ITERS = 3
beta_mix = 0.5
eps_shift = 0.001
PAD = 8
VMEM_LIMIT = 24 * 1024 * 1024
SMALL = pl.CostEstimate(flops=1, bytes_accessed=1, transcendentals=0)


def matmul(left, right):
    return jnp.einsum("...ij,...jk->...ik", left, right, precision=lax.Precision.HIGHEST)


def newton_root(factor):
    size = factor.shape[-1]
    ident = jnp.eye(size, dtype=jnp.float32)
    scale = jnp.sqrt(jnp.sum(factor * factor, axis=(-2, -1), keepdims=True))
    moving = factor / scale
    result = jnp.broadcast_to(ident, factor.shape)
    for count in range(ITERS):
        step_mat = (5.0 * ident - moving) * 0.25
        result = matmul(result, step_mat)
        squared = matmul(step_mat, step_mat)
        moving = matmul(matmul(squared, squared), moving)
    return result * jnp.power(scale, -0.25)


def general_device(full_dim, grads, left_stats, right_stats):
    mats, tile_rows, tile_cols = grads.shape
    blk = left_stats.shape[2]
    row_blocks = tile_rows // blk
    col_blocks = tile_cols // blk
    ident = jnp.eye(blk, dtype=jnp.float32)
    by_rows = grads.reshape(mats, row_blocks, blk, tile_cols)
    left_part = jnp.einsum("mibd,mied->mibe", by_rows, by_rows, precision=lax.Precision.HIGHEST) / full_dim
    by_cols = grads.reshape(mats, tile_rows, col_blocks, blk)
    right_part = (
        jnp.einsum("mdjb,mdje->mjbe", by_cols, by_cols, precision=lax.Precision.HIGHEST) / full_dim
    )
    left_gram = lax.psum(left_part, "col")
    right_gram = lax.psum(right_part, "row")
    left_factor = (
        beta_mix * left_stats.reshape(mats, row_blocks, blk, blk)
        + (1.0 - beta_mix) * left_gram
        + eps_shift * ident
    )
    right_factor = (
        beta_mix * right_stats.reshape(mats, col_blocks, blk, blk)
        + (1.0 - beta_mix) * right_gram
        + eps_shift * ident
    )
    left_root = newton_root(left_factor)
    right_root = newton_root(right_factor)
    half = jnp.einsum("mibe,mied->mibd", left_root, by_rows, precision=lax.Precision.HIGHEST)
    half = half.reshape(mats, tile_rows, col_blocks, blk)
    full = jnp.einsum("mdjb,mjbe->mdje", half, right_root, precision=lax.Precision.HIGHEST)
    full = full.reshape(mats, tile_rows, tile_cols)
    return lax.all_to_all(full, "col", split_axis=1, concat_axis=2, tiled=True)


def split(value):
    high = value.astype(jnp.bfloat16)
    low = (value - high.astype(jnp.float32)).astype(jnp.bfloat16)
    return high, low


def dot(left, right, dims=((1,), (0,))):
    return lax.dot_general(left, right, (dims, ((), ())), preferred_element_type=jnp.float32)


def product(left, right):
    lh, ll = left
    rh, rl = right
    return dot(lh, rh) + (dot(lh, rl) + dot(ll, rh))


def places(blk):
    rows = lax.broadcasted_iota(jnp.int32, (blk, blk), 0)
    cols = lax.broadcasted_iota(jnp.int32, (blk, blk), 1)
    return rows, cols


def pack(first, second):
    blk = first.shape[0]
    rows, cols = places(blk)
    body = jnp.where(rows <= cols, first, second)
    diag = jnp.sum(jnp.where(rows == cols, second, 0.0), axis=0, keepdims=True)
    return body, jnp.broadcast_to(diag, (PAD, blk))


def unpack(body, diag):
    blk = body.shape[0]
    rows, cols = places(blk)
    turned = body.T
    first = jnp.where(rows <= cols, body, turned)
    second = jnp.where(rows > cols, body, jnp.where(rows == cols, diag, turned))
    return first, second


def right_gram_kernel(place, g_ref, after_ref, *out_refs):
    step = pl.program_id(0)
    blk = g_ref.shape[1] // 2
    high, low = split(g_ref[...])
    grams = []
    for b in range(2):
        hb = high[:, b * blk : (b + 1) * blk]
        lb = low[:, b * blk : (b + 1) * blk]
        both = dot(hb, hb, ((0,), (0,)))
        cross = dot(hb, lb, ((0,), (0,)))
        grams.append(both + (cross + cross.T))
    body, diag = pack(*grams)

    for at, ref in enumerate(out_refs):

        @pl.when(step == at)
        def _():
            ref[:blk, :] = body
            ref[blk:, :] = diag


def right_grams(place, tile, blk, flips, after):
    rows = tile.shape[0]
    tall = blk + PAD
    flip = lambda s: jnp.where(s == 0, flips[0], flips[1])
    return pl.pallas_call(
        right_gram_kernel,
        out_shape=(jax.ShapeDtypeStruct((tall, blk), jnp.float32),) * 2,
        grid_spec=pltpu.PrefetchScalarGridSpec(
            num_scalar_prefetch=1,
            grid=(2,),
            in_specs=[
                pl.BlockSpec((rows, 2 * blk), lambda s, place: (0, place[0] ^ flip(s))),
                pl.BlockSpec(memory_space=pl.ANY),
            ],
            out_specs=(pl.BlockSpec((tall, blk), lambda s, place: (0, 0)),) * 2,
        ),
        compiler_params=pltpu.CompilerParams(vmem_limit_bytes=VMEM_LIMIT),
        cost_estimate=SMALL,
        name="right_grams",
    )(place, tile, after)


def left_gram_kernel(place, g_ref, after_ref, out_ref, lhh, lcross):
    step = pl.program_id(0)
    last = pl.num_programs(0) - 1
    blk = lhh.shape[-1]
    high, low = split(g_ref[...])
    for i in range(2):
        hi = high[i * blk : (i + 1) * blk, :]
        lo = low[i * blk : (i + 1) * blk, :]
        both = dot(hi, hi, ((1,), (1,)))
        cross = dot(lo, hi, ((1,), (1,)))

        @pl.when(step == 0)
        def _():
            lhh[i] = both
            lcross[i] = cross

        @pl.when(step > 0)
        def _():
            lhh[i] += both
            lcross[i] += cross

    @pl.when(step == last)
    def _():
        body, diag = pack(*(lhh[b] + (lcross[b] + lcross[b].T) for b in range(2)))
        out_ref[:blk, :] = body
        out_ref[blk:, :] = diag


def left_grams(place, tile, blk, at, after):
    width = tile.shape[1]
    tall = blk + PAD
    return pl.pallas_call(
        left_gram_kernel,
        out_shape=jax.ShapeDtypeStruct((tall, blk), jnp.float32),
        grid_spec=pltpu.PrefetchScalarGridSpec(
            num_scalar_prefetch=1,
            grid=(width // (4 * blk),),
            in_specs=[
                pl.BlockSpec((2 * blk, 4 * blk), lambda s, place: (at(place), s)),
                pl.BlockSpec(memory_space=pl.ANY),
            ],
            out_specs=pl.BlockSpec((tall, blk), lambda s, place: (0, 0)),
            scratch_shapes=[
                pltpu.VMEM((2, blk, blk), jnp.float32),
                pltpu.VMEM((2, blk, blk), jnp.float32),
            ],
        ),
        compiler_params=pltpu.CompilerParams(vmem_limit_bytes=VMEM_LIMIT),
        cost_estimate=SMALL,
        name="left_grams",
    )(place, tile, after)


def here():
    return lax.axis_index("row"), lax.axis_index("col")


def take_kernel(g_ref, out_ref, sem):
    rows, wide = out_ref.shape
    place = here()
    start = pl.multiple_of((place[0] ^ raw_flip(place)) * wide, wide)
    top = pl.multiple_of((1 - place[1]) * rows, rows)
    copy = pltpu.make_async_copy(g_ref.at[pl.ds(top, rows), pl.ds(start, wide)], out_ref, sem)
    copy.start()
    copy.wait()


def take(tile, blk):
    return pl.pallas_call(
        take_kernel,
        out_shape=jax.ShapeDtypeStruct((tile.shape[0] // 2, 2 * blk), jnp.float32),
        in_specs=[pl.BlockSpec(memory_space=pl.ANY)],
        out_specs=pl.BlockSpec(memory_space=pl.ANY),
        scratch_shapes=[pltpu.SemaphoreType.DMA],
        compiler_params=pltpu.CompilerParams(vmem_limit_bytes=VMEM_LIMIT),
        cost_estimate=SMALL,
        name="take",
    )(tile)


def fold_kernel(a_ref, b_ref, out_ref):
    out_ref[...] = a_ref[...] + b_ref[...]


def fold(kept, near):
    return pl.pallas_call(
        fold_kernel,
        out_shape=jax.ShapeDtypeStruct(kept.shape, jnp.float32),
        compiler_params=pltpu.CompilerParams(vmem_limit_bytes=VMEM_LIMIT),
        cost_estimate=SMALL,
        name="fold",
    )(kept, near)


def hold_kernel(a_ref, *rest):
    out_ref = rest[-1]
    out_ref[...] = a_ref[...]


def hold(value, *after):
    return pl.pallas_call(
        hold_kernel,
        out_shape=jax.ShapeDtypeStruct(value.shape, jnp.float32),
        in_specs=[pl.BlockSpec(memory_space=pltpu.VMEM)] + [pl.BlockSpec(memory_space=pl.ANY)] * len(after),
        compiler_params=pltpu.CompilerParams(vmem_limit_bytes=VMEM_LIMIT),
        cost_estimate=SMALL,
        name="hold",
    )(value, *after)


def pair_roots(full_dim, stats_ref, body, diag):
    blk = body.shape[0]
    rows, cols = places(blk)
    ident = jnp.where(rows == cols, 1.0, 0.0)
    moving, scales = [], []
    for b, gram in enumerate(unpack(body, diag)):
        factor = (
            beta_mix * stats_ref[b * blk : (b + 1) * blk, :]
            + (1.0 - beta_mix) * (gram / full_dim)
            + eps_shift * ident
        )
        scale = jnp.sqrt(jnp.sum(factor * factor, keepdims=True))
        moving.append(factor / scale)
        scales.append(scale)
    result = None
    for count in range(ITERS):
        steps = [(5.0 * ident - m) * 0.25 for m in moving]
        parts = [split(s) for s in steps]
        if result is None:
            result = steps
        else:
            result = [product(split(r), p) for r, p in zip(result, parts)]
        if count < ITERS - 1:
            squared = [split(product(p, p)) for p in parts]
            fourth = [split(product(s, s)) for s in squared]
            moving = [product(f, split(m)) for f, m in zip(fourth, moving)]
    return [r * jnp.exp(-0.25 * jnp.log(s)) for r, s in zip(result, scales)]


def right_kernel(full_dim, place, stats_ref, a_ref, b_ref, c_ref, g_ref, under_ref, out_ref, halves_ref, half_ref):
    blk = stats_ref.shape[1]
    rows = g_ref.shape[0]
    total = a_ref[...] + b_ref[...] + c_ref[...]
    roots = pair_roots(full_dim, stats_ref, total[:blk], total[blk : blk + 1])
    half_ref[:rows, :] = product(split(g_ref[...]), split(roots[0]))
    half_ref[rows:, :] = under_ref[...]
    body, diag = pack(*roots)
    out_ref[:blk, :] = body
    out_ref[blk:, :] = diag
    for b, root in enumerate(roots):
        high, low = split(root)
        halves_ref[b, 0] = high
        halves_ref[b, 1] = low


def right_roots(full_dim, place, stats, kept, near, far, tile, under):
    blk = stats.shape[1]
    tall = blk + PAD
    rows = tile.shape[0] // 2
    flat = pl.BlockSpec((tall, blk), lambda s, place: (0, 0))
    return pl.pallas_call(
        functools.partial(right_kernel, full_dim),
        out_shape=(
            jax.ShapeDtypeStruct((tall, blk), jnp.float32),
            jax.ShapeDtypeStruct((2, 2, blk, blk), jnp.bfloat16),
            jax.ShapeDtypeStruct((rows + tall, blk), jnp.float32),
        ),
        grid_spec=pltpu.PrefetchScalarGridSpec(
            num_scalar_prefetch=1,
            grid=(1,),
            in_specs=[
                pl.BlockSpec((2 * blk, blk), lambda s, place: (place[0], 0)),
                flat,
                flat,
                flat,
                pl.BlockSpec((rows, blk), lambda s, place: (1 - place[1], place[0] * 2)),
                flat,
            ],
            out_specs=(
                flat,
                pl.BlockSpec((2, 2, blk, blk), lambda s, place: (0, 0, 0, 0)),
                pl.BlockSpec((rows + tall, blk), lambda s, place: (0, 0)),
            ),
        ),
        compiler_params=pltpu.CompilerParams(vmem_limit_bytes=VMEM_LIMIT),
        cost_estimate=SMALL,
        name="right_roots",
    )(place, stats, kept, near, far, tile, under)


def left_kernel(full_dim, place, stats_ref, a_ref, b_ref, out_ref):
    blk = stats_ref.shape[1]
    total = a_ref[...] + b_ref[b_ref.shape[0] - a_ref.shape[0] :, :]
    for b, root in enumerate(pair_roots(full_dim, stats_ref, total[:blk], total[blk : blk + 1])):
        high, low = split(root)
        out_ref[b, 0] = high
        out_ref[b, 1] = low


def left_roots(full_dim, place, stats, kept, came):
    blk = stats.shape[1]
    tall = blk + PAD
    return pl.pallas_call(
        functools.partial(left_kernel, full_dim),
        out_shape=jax.ShapeDtypeStruct((2, 2, blk, blk), jnp.bfloat16),
        grid_spec=pltpu.PrefetchScalarGridSpec(
            num_scalar_prefetch=1,
            grid=(1,),
            in_specs=[
                pl.BlockSpec((2 * blk, blk), lambda s, place: (place[1], 0)),
                pl.BlockSpec((tall, blk), lambda s, place: (0, 0)),
                pl.BlockSpec(came.shape, lambda s, place: (0, 0)),
            ],
            out_specs=pl.BlockSpec((2, 2, blk, blk), lambda s, place: (0, 0, 0, 0)),
        ),
        compiler_params=pltpu.CompilerParams(vmem_limit_bytes=VMEM_LIMIT),
        cost_estimate=SMALL,
        name="left_roots",
    )(place, stats, kept, came)


def raw_flip(place):
    return 2 + (place[0] & 1)


def put_roots(out_ref, at, body, diag):
    for b, root in enumerate(unpack(body, diag)):
        high, low = split(root)
        out_ref[2 * at + b, 0] = high
        out_ref[2 * at + b, 1] = low


def spread_kernel(*refs):
    out_ref = refs[-1]
    blk = out_ref.shape[-1]
    for at, ref in enumerate(refs[:-1]):
        put_roots(out_ref, at, ref[:blk, :], ref[blk : blk + 1, :])


def spread_roots(*packed):
    blk = packed[0].shape[1]
    return pl.pallas_call(
        spread_kernel,
        out_shape=jax.ShapeDtypeStruct((2 * len(packed), 2, blk, blk), jnp.bfloat16),
        compiler_params=pltpu.CompilerParams(vmem_limit_bytes=VMEM_LIMIT),
        cost_estimate=SMALL,
        name="spread_roots",
    )(*packed)


def cut_kernel(place, x_ref, xc_ref, out_ref):
    half = out_ref.shape[0] - PAD

    @pl.when((place[0] & 1) == 0)
    def _():
        out_ref[:half, :] = x_ref[:half, :]
        out_ref[half:, :] = x_ref[2 * half :, :]

    @pl.when((place[0] & 1) == 1)
    def _():
        out_ref[:half, :] = xc_ref[half : 2 * half, :]
        out_ref[half:, :] = xc_ref[2 * half :, :]


def cut(place, of_x, of_xc):
    tall, blk = of_x.shape
    whole = pl.BlockSpec((tall, blk), lambda s, place: (0, 0))
    return pl.pallas_call(
        cut_kernel,
        out_shape=jax.ShapeDtypeStruct((blk // 2 + PAD, blk), jnp.float32),
        grid_spec=pltpu.PrefetchScalarGridSpec(
            num_scalar_prefetch=1,
            grid=(1,),
            in_specs=[whole, whole],
            out_specs=pl.BlockSpec((blk // 2 + PAD, blk), lambda s, place: (0, 0)),
        ),
        compiler_params=pltpu.CompilerParams(vmem_limit_bytes=VMEM_LIMIT),
        cost_estimate=SMALL,
        name="cut",
    )(place, of_x, of_xc)


def rest_kernel(a_ref, out_ref):
    out_ref[...] = a_ref[a_ref.shape[0] - out_ref.shape[0] :, :]


def rest_of(value, rows):
    return pl.pallas_call(
        rest_kernel,
        out_shape=jax.ShapeDtypeStruct((value.shape[0] - rows, value.shape[1]), jnp.float32),
        compiler_params=pltpu.CompilerParams(vmem_limit_bytes=VMEM_LIMIT),
        cost_estimate=SMALL,
        name="rest_of",
    )(value)


def join_kernel(place, mine_ref, other_ref, out_ref, body):
    half = mine_ref.shape[0] - PAD
    core = place[0] & 1
    body[pl.ds(pl.multiple_of(core * half, half), half), :] = mine_ref[:half, :]
    body[pl.ds(pl.multiple_of((1 - core) * half, half), half), :] = other_ref[:half, :]
    put_roots(out_ref, 0, body[...], mine_ref[half : half + 1, :])


def join_roots(place, mine, other):
    tall, blk = mine.shape
    half = pl.BlockSpec((tall, blk), lambda s, place: (0, 0))
    return pl.pallas_call(
        join_kernel,
        out_shape=jax.ShapeDtypeStruct((2, 2, blk, blk), jnp.bfloat16),
        grid_spec=pltpu.PrefetchScalarGridSpec(
            num_scalar_prefetch=1,
            grid=(1,),
            in_specs=[half, half],
            out_specs=pl.BlockSpec((2, 2, blk, blk), lambda s, place: (0, 0, 0, 0)),
            scratch_shapes=[pltpu.VMEM((blk, blk), jnp.float32)],
        ),
        compiler_params=pltpu.CompilerParams(vmem_limit_bytes=VMEM_LIMIT),
        cost_estimate=SMALL,
        name="join_roots",
    )(place, mine, other)


def right_apply_kernel(width, carries, place, g_ref, right_ref, *rest):
    step = pl.program_id(0)
    out_refs = rest[-len(width) :]
    value = product(split(g_ref[...]), (right_ref[0, 0], right_ref[0, 1]))
    blk = value.shape[1]
    start = 0
    for size, ref in zip(width, out_refs):
        for b in range(start // blk, -(-(start + size) // blk)):
            low, high = max(start, b * blk), min(start + size, (b + 1) * blk)

            @pl.when(step == b)
            def _():
                ref[: value.shape[0], low - start : high - start] = value[:, low - b * blk : high - b * blk]

        start += size
    if carries:
        out_refs[0][value.shape[0] :, :] = rest[0][...]


def right_apply(place, tile, right, flip, right_at, first, width, under, after):
    rows = tile.shape[0] // 2
    blk = right.shape[-1]
    in_specs = [
        pl.BlockSpec((rows, blk), lambda s, place: (1 - place[1], (place[0] ^ flip(place)) * 2 + first + s)),
        pl.BlockSpec((1, 2, blk, blk), lambda s, place: (right_at(place) + first + s, 0, 0, 0)),
    ]
    operands = [tile, right]
    tall = rows
    if under is not None:
        tall += under.shape[0]
        in_specs.append(pl.BlockSpec(under.shape, lambda s, place: (0, 0)))
        operands.append(under)
    return pl.pallas_call(
        functools.partial(right_apply_kernel, width, under is not None),
        out_shape=tuple(jax.ShapeDtypeStruct((tall, w), jnp.float32) for w in width),
        grid_spec=pltpu.PrefetchScalarGridSpec(
            num_scalar_prefetch=1,
            grid=(sum(width) // blk,),
            in_specs=in_specs + [pl.BlockSpec(memory_space=pl.ANY)] * len(after),
            out_specs=tuple(pl.BlockSpec((tall, w), lambda s, place: (0, 0)) for w in width),
        ),
        compiler_params=pltpu.CompilerParams(vmem_limit_bytes=VMEM_LIMIT),
        cost_estimate=SMALL,
        name="right_apply",
    )(place, *operands, *after)


def left_product(left_ref, value, out_ref):
    blk = left_ref.shape[-1]
    for i in range(value.shape[0] // blk):
        part = split(value[i * blk : (i + 1) * blk])
        out_ref[i * blk : (i + 1) * blk, :] = product((left_ref[i, 0], left_ref[i, 1]), part)


def update_kernel(place, g_ref, left_ref, right_ref, *rest):
    half = product(split(g_ref[...]), (right_ref[0, 0], right_ref[0, 1]))
    left_product(left_ref, half, rest[-2])
    rest[-1][...] = jnp.zeros_like(rest[-1])


def finish_kernel(column, width, half_ref, left_ref, out_before, out_ref, *rest):
    stage, sems = rest[-2:]
    blk = left_ref.shape[-1]
    start = pl.multiple_of(column(here()), width)
    copies = []
    for i in range(left_ref.shape[0]):
        rows = pl.ds(i * blk, blk)
        for b in range(0, width, blk):
            cols = pl.ds(b, min(blk, width))
            stage[rows, cols] = product((left_ref[i, 0], left_ref[i, 1]), split(half_ref[rows, cols]))
        copies.append(
            pltpu.make_async_copy(stage.at[rows, :], out_ref.at[rows, pl.ds(start, width)], sems.at[i])
        )
        copies[i].start()
    for done_ref in rest[:-2]:
        done_ref[...] = jnp.zeros_like(done_ref)
    for copy in copies:
        copy.wait()


def finish(half, left, out, column, mark=False):
    width = half.shape[1]
    rows = out.shape[0]
    vmem = pl.BlockSpec(memory_space=pltpu.VMEM)
    anywhere = pl.BlockSpec(memory_space=pl.ANY)
    shapes = (jax.ShapeDtypeStruct(out.shape, jnp.float32), jax.ShapeDtypeStruct((8, 128), jnp.float32))
    return pl.pallas_call(
        functools.partial(finish_kernel, column, width),
        out_shape=shapes if mark else shapes[:1],
        in_specs=[vmem, vmem, anywhere],
        out_specs=(anywhere, vmem) if mark else (anywhere,),
        scratch_shapes=[pltpu.VMEM((rows, width), jnp.float32), pltpu.SemaphoreType.DMA((left.shape[0],))],
        input_output_aliases={2: 0},
        compiler_params=pltpu.CompilerParams(vmem_limit_bytes=VMEM_LIMIT),
        cost_estimate=SMALL,
        name="finish",
    )(half, left, out)


def update(place, source, left, right, out, out_shape, g_map, out_map):
    rows = out_shape[0]
    blk = left.shape[-1]
    in_specs = [
        pl.BlockSpec((rows, blk), g_map),
        pl.BlockSpec((2, 2, blk, blk), lambda s, place: (0, 0, 0, 0)),
        pl.BlockSpec((1, 2, blk, blk), lambda s, place: (s, 0, 0, 0)),
    ]
    operands = [source, left, right]
    aliases = {}
    if out is not None:
        aliases = {1 + len(operands): 0}
        in_specs.append(pl.BlockSpec(memory_space=pl.ANY))
        operands.append(out)
    return pl.pallas_call(
        update_kernel,
        out_shape=(jax.ShapeDtypeStruct(out_shape, jnp.float32), jax.ShapeDtypeStruct((8, 128), jnp.float32)),
        grid_spec=pltpu.PrefetchScalarGridSpec(
            num_scalar_prefetch=1,
            grid=(right.shape[0],),
            in_specs=in_specs,
            out_specs=(pl.BlockSpec((rows, blk), out_map), pl.BlockSpec((8, 128), lambda s, place: (0, 0))),
        ),
        input_output_aliases=aliases,
        compiler_params=pltpu.CompilerParams(vmem_limit_bytes=VMEM_LIMIT),
        cost_estimate=SMALL,
        name="update",
    )(place, *operands)


def exchange_device(full_dim, n_row, grads, left_stats, right_stats):
    tile_rows, tile_cols = grads.shape[1:]
    blk = left_stats.shape[2]
    tile = pltpu.with_memory_space_constraint(grads.reshape(tile_rows, tile_cols), pltpu.HBM)
    lstats = left_stats.reshape(tile_rows, blk)
    rstats = right_stats.reshape(tile_cols, blk)
    r = lax.axis_index("row")
    c = lax.axis_index("col")
    place = jnp.stack([r, c]).astype(jnp.int32)
    rows = tile_rows // 2
    shape = (rows, 2 * tile_cols)
    halves = tile_cols // blk

    def over(axis, value):
        if axis == "y":
            return lax.ppermute(value, "col", [(0, 1), (1, 0)])
        flip = {"core": 1, "x": 2}[axis]
        return lax.ppermute(value, "row", [(i, i ^ flip) for i in range(n_row)])

    first = take(tile, blk)
    raw = over("y", first)

    send_on, keep_on = right_grams(place, tile, blk, (3, 2), first)
    near_on = over("core", send_on)
    send, keep = right_grams(place, tile, blk, (1, 0), keep_on)
    near = over("core", send)
    far = over("x", fold(keep_on, near_on))
    lsend = left_grams(place, tile, blk, lambda place: 1 - place[1], send)

    own_pair, core_pair = (lambda place: 0), (lambda place: 1)
    last_pair = lambda place: 3 - (place[0] & 1)
    begin = lambda place: 0
    last_at = lambda place: 2 * (1 - (place[0] & 1))
    tail = (blk, blk // 2, blk // 2)

    own, roots_own, half = right_roots(full_dim, place, rstats, keep, near, far, tile, lsend)
    came_0a = over("y", half)
    own = hold(own, raw, half)
    lkeep = left_grams(place, tile, blk, lambda place: place[1], own)
    own_c = over("core", own)
    own_x = over("x", own)
    own_xc = over("core", own_x)
    held = right_apply(place, tile, roots_own, own_pair, begin, 1, (blk,), None, (lkeep,))
    came_0b = over("y", held[0])
    roots_core = spread_roots(own_c)
    held = right_apply(place, tile, roots_core, core_pair, begin, 0, (2 * blk,), None, (came_0a, own_xc))
    came_1 = over("y", held[0])
    own_x = hold(own_x, came_0b)
    roots_far = spread_roots(own_x, own_xc)
    held = right_apply(place, tile, roots_far, last_pair, last_at, 0, tail[:1], cut(place, own_x, own_xc), ())
    came_2 = [over("y", held[0])]
    mine = rest_of(came_2[0], rows)
    roots_raw = join_roots(place, mine, over("core", mine))

    left = left_roots(full_dim, place, lstats, lkeep, came_0a)

    def own_cols(base):
        return lambda s, place: (place[1], (place[0] ^ (base + s // 2)) * 2 + s % 2)

    out = None
    for base, roots in ((0, roots_own), (1, roots_core), (2, roots_far)):
        at = own_cols(base)
        out, done = update(
            place, tile, left, roots, out, shape, at,
            lambda s, place, at=at: (0, place[1] * halves + at(s, place)[1]),
        )

    def crossed(start, flip):
        return lambda place: (1 - place[1]) * tile_cols + (place[0] ^ flip(place)) * 2 * blk + start

    for b, value in enumerate((came_0a, came_0b)):
        (out,) = finish(value, left, out, crossed(b * blk, own_pair))
    out, done = finish(came_1, left, out, crossed(0, core_pair), mark=True)
    held = right_apply(place, tile, roots_far, last_pair, last_at, 1, tail[1:], None, (came_1, done))
    came_2 += [over("y", half) for half in held]
    out, done = update(
        place, raw, left, roots_raw, out, shape,
        lambda s, place: (0, s),
        lambda s, place: (0, (1 - place[1]) * halves + (place[0] ^ raw_flip(place)) * 2 + s),
    )
    start = 0
    for wide, value in zip(tail, came_2):
        (out,) = finish(value, left, out, crossed(start, last_pair))
        start += wide
    return out.reshape(1, rows, 2 * tile_cols)


def per_device(n_row, n_col, grads, left_stats, right_stats):
    mats, tile_rows, tile_cols = grads.shape
    blk = left_stats.shape[2]
    full_dim = tile_cols * n_col
    if mats == 1 and n_col == 2 and n_row == 4 and tile_rows == 4 * blk and tile_cols == 8 * blk:
        return exchange_device(full_dim, n_row, grads, left_stats, right_stats)
    return general_device(full_dim, grads, left_stats, right_stats)


def solution(mesh):
    return jax.shard_map(
        functools.partial(per_device, mesh.shape["row"], mesh.shape["col"]),
        mesh=mesh,
        in_specs=(P("mat", "row", "col"), P("mat", "row", None), P("mat", "col", None)),
        out_specs=P("mat", ("row", "col"), None),
        check_vma=False,
    )
```

```python
import functools

import jax
import jax.numpy as jnp
from jax import lax
from jax.experimental import pallas as pl
from jax.experimental.pallas import tpu as pltpu
from jax.sharding import PartitionSpec as P

ITERS = 3
beta_mix = 0.5
eps_shift = 0.001
PAD = 8
VMEM_LIMIT = 24 * 1024 * 1024
SMALL = pl.CostEstimate(flops=1, bytes_accessed=1, transcendentals=0)


def matmul(left, right):
    return jnp.einsum("...ij,...jk->...ik", left, right, precision=lax.Precision.HIGHEST)


def newton_root(factor):
    size = factor.shape[-1]
    ident = jnp.eye(size, dtype=jnp.float32)
    scale = jnp.sqrt(jnp.sum(factor * factor, axis=(-2, -1), keepdims=True))
    moving = factor / scale
    result = jnp.broadcast_to(ident, factor.shape)
    for count in range(ITERS):
        step_mat = (5.0 * ident - moving) * 0.25
        result = matmul(result, step_mat)
        squared = matmul(step_mat, step_mat)
        moving = matmul(matmul(squared, squared), moving)
    return result * jnp.power(scale, -0.25)


def general_device(full_dim, grads, left_stats, right_stats):
    mats, tile_rows, tile_cols = grads.shape
    blk = left_stats.shape[2]
    row_blocks = tile_rows // blk
    col_blocks = tile_cols // blk
    ident = jnp.eye(blk, dtype=jnp.float32)
    by_rows = grads.reshape(mats, row_blocks, blk, tile_cols)
    left_part = jnp.einsum("mibd,mied->mibe", by_rows, by_rows, precision=lax.Precision.HIGHEST) / full_dim
    by_cols = grads.reshape(mats, tile_rows, col_blocks, blk)
    right_part = (
        jnp.einsum("mdjb,mdje->mjbe", by_cols, by_cols, precision=lax.Precision.HIGHEST) / full_dim
    )
    left_gram = lax.psum(left_part, "col")
    right_gram = lax.psum(right_part, "row")
    left_factor = (
        beta_mix * left_stats.reshape(mats, row_blocks, blk, blk)
        + (1.0 - beta_mix) * left_gram
        + eps_shift * ident
    )
    right_factor = (
        beta_mix * right_stats.reshape(mats, col_blocks, blk, blk)
        + (1.0 - beta_mix) * right_gram
        + eps_shift * ident
    )
    left_root = newton_root(left_factor)
    right_root = newton_root(right_factor)
    half = jnp.einsum("mibe,mied->mibd", left_root, by_rows, precision=lax.Precision.HIGHEST)
    half = half.reshape(mats, tile_rows, col_blocks, blk)
    full = jnp.einsum("mdjb,mjbe->mdje", half, right_root, precision=lax.Precision.HIGHEST)
    full = full.reshape(mats, tile_rows, tile_cols)
    return lax.all_to_all(full, "col", split_axis=1, concat_axis=2, tiled=True)


def split(value):
    high = value.astype(jnp.bfloat16)
    low = (value - high.astype(jnp.float32)).astype(jnp.bfloat16)
    return high, low


def dot(left, right, dims=((1,), (0,))):
    return lax.dot_general(left, right, (dims, ((), ())), preferred_element_type=jnp.float32)


def product(left, right):
    lh, ll = left
    rh, rl = right
    return dot(lh, rh) + (dot(lh, rl) + dot(ll, rh))


def places(blk):
    rows = lax.broadcasted_iota(jnp.int32, (blk, blk), 0)
    cols = lax.broadcasted_iota(jnp.int32, (blk, blk), 1)
    return rows, cols


def pack(first, second):
    blk = first.shape[0]
    rows, cols = places(blk)
    body = jnp.where(rows <= cols, first, second)
    diag = jnp.sum(jnp.where(rows == cols, second, 0.0), axis=0, keepdims=True)
    return body, jnp.broadcast_to(diag, (PAD, blk))


def unpack(body, diag):
    blk = body.shape[0]
    rows, cols = places(blk)
    turned = body.T
    first = jnp.where(rows <= cols, body, turned)
    second = jnp.where(rows > cols, body, jnp.where(rows == cols, diag, turned))
    return first, second


def right_gram_kernel(place, g_ref, after_ref, *out_refs):
    step = pl.program_id(0)
    blk = g_ref.shape[1] // 2
    high, low = split(g_ref[...])
    grams = []
    for b in range(2):
        hb = high[:, b * blk : (b + 1) * blk]
        lb = low[:, b * blk : (b + 1) * blk]
        both = dot(hb, hb, ((0,), (0,)))
        cross = dot(hb, lb, ((0,), (0,)))
        grams.append(both + (cross + cross.T))
    body, diag = pack(*grams)

    for at, ref in enumerate(out_refs):

        @pl.when(step == at)
        def _():
            ref[:blk, :] = body
            ref[blk:, :] = diag


def right_grams(place, tile, blk, flips, after):
    rows = tile.shape[0]
    tall = blk + PAD
    flip = lambda s: jnp.where(s == 0, flips[0], flips[1])
    return pl.pallas_call(
        right_gram_kernel,
        out_shape=(jax.ShapeDtypeStruct((tall, blk), jnp.float32),) * 2,
        grid_spec=pltpu.PrefetchScalarGridSpec(
            num_scalar_prefetch=1,
            grid=(2,),
            in_specs=[
                pl.BlockSpec((rows, 2 * blk), lambda s, place: (0, place[0] ^ flip(s))),
                pl.BlockSpec(memory_space=pl.ANY),
            ],
            out_specs=(pl.BlockSpec((tall, blk), lambda s, place: (0, 0)),) * 2,
        ),
        compiler_params=pltpu.CompilerParams(vmem_limit_bytes=VMEM_LIMIT),
        cost_estimate=SMALL,
        name="right_grams",
    )(place, tile, after)


def left_gram_kernel(place, g_ref, after_ref, out_ref, lhh, lcross):
    step = pl.program_id(0)
    last = pl.num_programs(0) - 1
    blk = lhh.shape[-1]
    high, low = split(g_ref[...])
    for i in range(2):
        hi = high[i * blk : (i + 1) * blk, :]
        lo = low[i * blk : (i + 1) * blk, :]
        both = dot(hi, hi, ((1,), (1,)))
        cross = dot(lo, hi, ((1,), (1,)))

        @pl.when(step == 0)
        def _():
            lhh[i] = both
            lcross[i] = cross

        @pl.when(step > 0)
        def _():
            lhh[i] += both
            lcross[i] += cross

    @pl.when(step == last)
    def _():
        body, diag = pack(*(lhh[b] + (lcross[b] + lcross[b].T) for b in range(2)))
        out_ref[:blk, :] = body
        out_ref[blk:, :] = diag


def left_grams(place, tile, blk, at, after):
    width = tile.shape[1]
    tall = blk + PAD
    return pl.pallas_call(
        left_gram_kernel,
        out_shape=jax.ShapeDtypeStruct((tall, blk), jnp.float32),
        grid_spec=pltpu.PrefetchScalarGridSpec(
            num_scalar_prefetch=1,
            grid=(width // (4 * blk),),
            in_specs=[
                pl.BlockSpec((2 * blk, 4 * blk), lambda s, place: (at(place), s)),
                pl.BlockSpec(memory_space=pl.ANY),
            ],
            out_specs=pl.BlockSpec((tall, blk), lambda s, place: (0, 0)),
            scratch_shapes=[
                pltpu.VMEM((2, blk, blk), jnp.float32),
                pltpu.VMEM((2, blk, blk), jnp.float32),
            ],
        ),
        compiler_params=pltpu.CompilerParams(vmem_limit_bytes=VMEM_LIMIT),
        cost_estimate=SMALL,
        name="left_grams",
    )(place, tile, after)


RAW = (1, 3)


def here():
    return lax.axis_index("row"), lax.axis_index("col")


def own_first(place):
    return place[0] * 2


def core_first(place):
    return (place[0] ^ 1) * 2


def later(k, place):
    return jnp.where(place[0] < 2, 4 + k, jnp.where(k < 2, 2 * k, 2 * k + 1))


def take_kernel(g_ref, out_ref, sems):
    rows, wide = out_ref.shape
    blk = wide // len(RAW)
    top = pl.multiple_of((1 - here()[1]) * rows, rows)
    copies = [
        pltpu.make_async_copy(
            g_ref.at[pl.ds(top, rows), pl.ds(block * blk, blk)], out_ref.at[:, pl.ds(k * blk, blk)], sems.at[k]
        )
        for k, block in enumerate(RAW)
    ]
    for copy in copies:
        copy.start()
    for copy in copies:
        copy.wait()


def take(tile, blk):
    return pl.pallas_call(
        take_kernel,
        out_shape=jax.ShapeDtypeStruct((tile.shape[0] // 2, len(RAW) * blk), jnp.float32),
        in_specs=[pl.BlockSpec(memory_space=pl.ANY)],
        out_specs=pl.BlockSpec(memory_space=pl.ANY),
        scratch_shapes=[pltpu.SemaphoreType.DMA((len(RAW),))],
        compiler_params=pltpu.CompilerParams(vmem_limit_bytes=VMEM_LIMIT),
        cost_estimate=SMALL,
        name="take",
    )(tile)


def fold_kernel(a_ref, b_ref, out_ref):
    out_ref[...] = a_ref[...] + b_ref[...]


def fold(kept, near):
    return pl.pallas_call(
        fold_kernel,
        out_shape=jax.ShapeDtypeStruct(kept.shape, jnp.float32),
        compiler_params=pltpu.CompilerParams(vmem_limit_bytes=VMEM_LIMIT),
        cost_estimate=SMALL,
        name="fold",
    )(kept, near)


def hold_kernel(a_ref, *rest):
    out_ref = rest[-1]
    out_ref[...] = a_ref[...]


def hold(value, *after):
    return pl.pallas_call(
        hold_kernel,
        out_shape=jax.ShapeDtypeStruct(value.shape, jnp.float32),
        in_specs=[pl.BlockSpec(memory_space=pltpu.VMEM)] + [pl.BlockSpec(memory_space=pl.ANY)] * len(after),
        compiler_params=pltpu.CompilerParams(vmem_limit_bytes=VMEM_LIMIT),
        cost_estimate=SMALL,
        name="hold",
    )(value, *after)


def pair_roots(full_dim, stats_ref, body, diag):
    blk = body.shape[0]
    rows, cols = places(blk)
    ident = jnp.where(rows == cols, 1.0, 0.0)
    moving, scales = [], []
    for b, gram in enumerate(unpack(body, diag)):
        factor = (
            beta_mix * stats_ref[b * blk : (b + 1) * blk, :]
            + (1.0 - beta_mix) * (gram / full_dim)
            + eps_shift * ident
        )
        scale = jnp.sqrt(jnp.sum(factor * factor, keepdims=True))
        moving.append(factor / scale)
        scales.append(scale)
    result = None
    for count in range(ITERS):
        steps = [(5.0 * ident - m) * 0.25 for m in moving]
        parts = [split(s) for s in steps]
        if result is None:
            result = steps
        else:
            result = [product(split(r), p) for r, p in zip(result, parts)]
        if count < ITERS - 1:
            squared = [split(product(p, p)) for p in parts]
            fourth = [split(product(s, s)) for s in squared]
            moving = [product(f, split(m)) for f, m in zip(fourth, moving)]
    return [r * jnp.exp(-0.25 * jnp.log(s)) for r, s in zip(result, scales)]


def right_kernel(full_dim, place, stats_ref, a_ref, b_ref, c_ref, g_ref, under_ref, out_ref, half_ref):
    blk = stats_ref.shape[1]
    rows = g_ref.shape[0]
    total = a_ref[...] + b_ref[...] + c_ref[...]
    roots = pair_roots(full_dim, stats_ref, total[:blk], total[blk : blk + 1])
    half_ref[:rows, :] = product(split(g_ref[...]), split(roots[0]))
    half_ref[rows:, :] = under_ref[...]
    body, diag = pack(*roots)
    out_ref[:blk, :] = body
    out_ref[blk:, :] = diag


def right_roots(full_dim, place, stats, kept, near, far, tile, under):
    blk = stats.shape[1]
    tall = blk + PAD
    rows = tile.shape[0] // 2
    flat = pl.BlockSpec((tall, blk), lambda s, place: (0, 0))
    return pl.pallas_call(
        functools.partial(right_kernel, full_dim),
        out_shape=(
            jax.ShapeDtypeStruct((tall, blk), jnp.float32),
            jax.ShapeDtypeStruct((rows + tall, blk), jnp.float32),
        ),
        grid_spec=pltpu.PrefetchScalarGridSpec(
            num_scalar_prefetch=1,
            grid=(1,),
            in_specs=[
                pl.BlockSpec((2 * blk, blk), lambda s, place: (place[0], 0)),
                flat,
                flat,
                flat,
                pl.BlockSpec((rows, blk), lambda s, place: (1 - place[1], own_first(place))),
                flat,
            ],
            out_specs=(
                flat,
                pl.BlockSpec((rows + tall, blk), lambda s, place: (0, 0)),
            ),
        ),
        compiler_params=pltpu.CompilerParams(vmem_limit_bytes=VMEM_LIMIT),
        cost_estimate=SMALL,
        name="right_roots",
    )(place, stats, kept, near, far, tile, under)


def left_kernel(full_dim, place, stats_ref, a_ref, b_ref, out_ref):
    blk = stats_ref.shape[1]
    total = a_ref[...] + b_ref[b_ref.shape[0] - a_ref.shape[0] :, :]
    for b, root in enumerate(pair_roots(full_dim, stats_ref, total[:blk], total[blk : blk + 1])):
        high, low = split(root)
        out_ref[b, 0] = high
        out_ref[b, 1] = low


def left_roots(full_dim, place, stats, kept, came):
    blk = stats.shape[1]
    tall = blk + PAD
    return pl.pallas_call(
        functools.partial(left_kernel, full_dim),
        out_shape=jax.ShapeDtypeStruct((2, 2, blk, blk), jnp.bfloat16),
        grid_spec=pltpu.PrefetchScalarGridSpec(
            num_scalar_prefetch=1,
            grid=(1,),
            in_specs=[
                pl.BlockSpec((2 * blk, blk), lambda s, place: (place[1], 0)),
                pl.BlockSpec((tall, blk), lambda s, place: (0, 0)),
                pl.BlockSpec(came.shape, lambda s, place: (0, 0)),
            ],
            out_specs=pl.BlockSpec((2, 2, blk, blk), lambda s, place: (0, 0, 0, 0)),
        ),
        compiler_params=pltpu.CompilerParams(vmem_limit_bytes=VMEM_LIMIT),
        cost_estimate=SMALL,
        name="left_roots",
    )(place, stats, kept, came)


def put_roots(out_ref, at, roots):
    for b, root in enumerate(roots):
        high, low = split(root)
        out_ref[at + b, 0] = high
        out_ref[at + b, 1] = low


def spread_kernel(own_ref, c_ref, x_ref, xc_ref, out_ref, cut_ref, seconds, body):
    blk = out_ref.shape[-1]
    r = here()[0]
    for flip, ref in enumerate((own_ref, c_ref, x_ref, xc_ref)):
        roots = unpack(ref[:blk, :], ref[blk : blk + 1, :])
        put_roots(out_ref, 2 * (r ^ flip), roots)
        seconds[r ^ flip] = roots[1]
    part = cut_ref.shape[0] - PAD
    body[...], diag = pack(seconds[RAW[0] // 2], seconds[RAW[1] // 2])
    cut_ref[:part, :] = body[pl.ds(pl.multiple_of(r * part, part), part), :]
    cut_ref[part:, :] = diag


def spread_roots(*packed):
    blk = packed[0].shape[1]
    count = len(packed)
    return pl.pallas_call(
        spread_kernel,
        out_shape=(
            jax.ShapeDtypeStruct((2 * count, 2, blk, blk), jnp.bfloat16),
            jax.ShapeDtypeStruct((blk // count + PAD, blk), jnp.float32),
        ),
        scratch_shapes=[pltpu.VMEM((count, blk, blk), jnp.float32), pltpu.VMEM((blk, blk), jnp.float32)],
        compiler_params=pltpu.CompilerParams(vmem_limit_bytes=VMEM_LIMIT),
        cost_estimate=SMALL,
        name="spread_roots",
    )(*packed)


def rest_kernel(a_ref, out_ref):
    out_ref[...] = a_ref[a_ref.shape[0] - out_ref.shape[0] :, :]


def rest_of(value, rows):
    return pl.pallas_call(
        rest_kernel,
        out_shape=jax.ShapeDtypeStruct((value.shape[0] - rows, value.shape[1]), jnp.float32),
        compiler_params=pltpu.CompilerParams(vmem_limit_bytes=VMEM_LIMIT),
        cost_estimate=SMALL,
        name="rest_of",
    )(value)


def join_kernel(own_ref, c_ref, x_ref, xc_ref, out_ref, body):
    part = own_ref.shape[0] - PAD
    r = here()[0]
    for flip, ref in enumerate((own_ref, c_ref, x_ref, xc_ref)):
        body[pl.ds(pl.multiple_of((r ^ flip) * part, part), part), :] = ref[:part, :]
    put_roots(out_ref, 0, unpack(body[...], own_ref[part : part + 1, :]))


def join_roots(*parts):
    blk = parts[0].shape[1]
    return pl.pallas_call(
        join_kernel,
        out_shape=jax.ShapeDtypeStruct((2, 2, blk, blk), jnp.bfloat16),
        scratch_shapes=[pltpu.VMEM((blk, blk), jnp.float32)],
        compiler_params=pltpu.CompilerParams(vmem_limit_bytes=VMEM_LIMIT),
        cost_estimate=SMALL,
        name="join_roots",
    )(*parts)


def core_apply_kernel(place, g_ref, packed_ref, out_ref):
    blk = g_ref.shape[1]
    root = unpack(packed_ref[:blk, :], packed_ref[blk : blk + 1, :])[0]
    out_ref[...] = product(split(g_ref[...]), split(root))


def core_apply(place, tile, packed):
    rows = tile.shape[0] // 2
    tall, blk = packed.shape
    return pl.pallas_call(
        core_apply_kernel,
        out_shape=jax.ShapeDtypeStruct((rows, blk), jnp.float32),
        grid_spec=pltpu.PrefetchScalarGridSpec(
            num_scalar_prefetch=1,
            grid=(1,),
            in_specs=[
                pl.BlockSpec((rows, blk), lambda s, place: (1 - place[1], core_first(place))),
                pl.BlockSpec((tall, blk), lambda s, place: (0, 0)),
            ],
            out_specs=pl.BlockSpec((rows, blk), lambda s, place: (0, 0)),
        ),
        compiler_params=pltpu.CompilerParams(vmem_limit_bytes=VMEM_LIMIT),
        cost_estimate=SMALL,
        name="core_apply",
    )(place, tile, packed)


def right_apply_kernel(width, carries, place, g_ref, right_ref, *rest):
    step = pl.program_id(0)
    out_refs = rest[-len(width) :]
    value = product(split(g_ref[...]), (right_ref[0, 0], right_ref[0, 1]))
    blk = value.shape[1]
    start = 0
    for size, ref in zip(width, out_refs):
        for b in range(start // blk, -(-(start + size) // blk)):
            low, high = max(start, b * blk), min(start + size, (b + 1) * blk)

            @pl.when(step == b)
            def _():
                ref[: value.shape[0], low - start : high - start] = value[:, low - b * blk : high - b * blk]

        start += size
    if carries:
        out_refs[0][value.shape[0] :, :] = rest[0][...]


def right_apply(place, tile, right, first, width, under, after):
    rows = tile.shape[0] // 2
    blk = right.shape[-1]
    in_specs = [
        pl.BlockSpec((rows, blk), lambda s, place: (1 - place[1], later(first + s, place))),
        pl.BlockSpec((1, 2, blk, blk), lambda s, place: (later(first + s, place), 0, 0, 0)),
    ]
    operands = [tile, right]
    tall = rows
    if under is not None:
        tall += under.shape[0]
        in_specs.append(pl.BlockSpec(under.shape, lambda s, place: (0, 0)))
        operands.append(under)
    return pl.pallas_call(
        functools.partial(right_apply_kernel, width, under is not None),
        out_shape=tuple(jax.ShapeDtypeStruct((tall, w), jnp.float32) for w in width),
        grid_spec=pltpu.PrefetchScalarGridSpec(
            num_scalar_prefetch=1,
            grid=(sum(width) // blk,),
            in_specs=in_specs + [pl.BlockSpec(memory_space=pl.ANY)] * len(after),
            out_specs=tuple(pl.BlockSpec((tall, w), lambda s, place: (0, 0)) for w in width),
        ),
        compiler_params=pltpu.CompilerParams(vmem_limit_bytes=VMEM_LIMIT),
        cost_estimate=SMALL,
        name="right_apply",
    )(place, *operands, *after)


def left_product(left_ref, value, out_ref):
    blk = left_ref.shape[-1]
    for i in range(value.shape[0] // blk):
        part = split(value[i * blk : (i + 1) * blk])
        out_ref[i * blk : (i + 1) * blk, :] = product((left_ref[i, 0], left_ref[i, 1]), part)


def update_kernel(place, g_ref, left_ref, right_ref, *rest):
    half = product(split(g_ref[...]), (right_ref[0, 0], right_ref[0, 1]))
    left_product(left_ref, half, rest[-2])
    rest[-1][...] = jnp.zeros_like(rest[-1])


def finish_kernel(columns, half_ref, left_ref, out_before, out_ref, *rest):
    stage, sems = rest[-2:]
    blk = left_ref.shape[-1]
    size = stage.shape[1] // len(columns)
    copies = []
    for b, column in enumerate(columns):
        start = pl.multiple_of(column(here()), size)
        cols = pl.ds(b * size, size)
        for i in range(left_ref.shape[0]):
            rows = pl.ds(i * blk, blk)
            stage[rows, cols] = product((left_ref[i, 0], left_ref[i, 1]), split(half_ref[rows, cols]))
            copies.append(
                pltpu.make_async_copy(stage.at[rows, cols], out_ref.at[rows, pl.ds(start, size)], sems.at[len(copies)])
            )
            copies[-1].start()
    for done_ref in rest[:-2]:
        done_ref[...] = jnp.zeros_like(done_ref)
    for copy in copies:
        copy.wait()


def finish(half, left, out, columns, mark=False):
    width = half.shape[1]
    rows = out.shape[0]
    vmem = pl.BlockSpec(memory_space=pltpu.VMEM)
    anywhere = pl.BlockSpec(memory_space=pl.ANY)
    shapes = (jax.ShapeDtypeStruct(out.shape, jnp.float32), jax.ShapeDtypeStruct((8, 128), jnp.float32))
    return pl.pallas_call(
        functools.partial(finish_kernel, columns),
        out_shape=shapes if mark else shapes[:1],
        in_specs=[vmem, vmem, anywhere],
        out_specs=(anywhere, vmem) if mark else (anywhere,),
        scratch_shapes=[
            pltpu.VMEM((rows, width), jnp.float32),
            pltpu.SemaphoreType.DMA((left.shape[0] * len(columns),)),
        ],
        input_output_aliases={2: 0},
        compiler_params=pltpu.CompilerParams(vmem_limit_bytes=VMEM_LIMIT),
        cost_estimate=SMALL,
        name="finish",
    )(half, left, out)


def update(place, source, left, right, out, out_shape, g_map, out_map):
    rows = out_shape[0]
    blk = left.shape[-1]
    in_specs = [
        pl.BlockSpec((rows, blk), g_map),
        pl.BlockSpec((2, 2, blk, blk), lambda s, place: (0, 0, 0, 0)),
        pl.BlockSpec((1, 2, blk, blk), lambda s, place: (s, 0, 0, 0)),
    ]
    operands = [source, left, right]
    aliases = {}
    if out is not None:
        aliases = {1 + len(operands): 0}
        in_specs.append(pl.BlockSpec(memory_space=pl.ANY))
        operands.append(out)
    return pl.pallas_call(
        update_kernel,
        out_shape=(jax.ShapeDtypeStruct(out_shape, jnp.float32), jax.ShapeDtypeStruct((8, 128), jnp.float32)),
        grid_spec=pltpu.PrefetchScalarGridSpec(
            num_scalar_prefetch=1,
            grid=(right.shape[0],),
            in_specs=in_specs,
            out_specs=(pl.BlockSpec((rows, blk), out_map), pl.BlockSpec((8, 128), lambda s, place: (0, 0))),
        ),
        input_output_aliases=aliases,
        compiler_params=pltpu.CompilerParams(vmem_limit_bytes=VMEM_LIMIT),
        cost_estimate=SMALL,
        name="update",
    )(place, *operands)


def exchange_device(full_dim, n_row, grads, left_stats, right_stats):
    tile_rows, tile_cols = grads.shape[1:]
    blk = left_stats.shape[2]
    tile = pltpu.with_memory_space_constraint(grads.reshape(tile_rows, tile_cols), pltpu.HBM)
    lstats = left_stats.reshape(tile_rows, blk)
    rstats = right_stats.reshape(tile_cols, blk)
    r = lax.axis_index("row")
    c = lax.axis_index("col")
    place = jnp.stack([r, c]).astype(jnp.int32)
    rows = tile_rows // 2
    shape = (rows, 2 * tile_cols)
    halves = tile_cols // blk

    def over(axis, value):
        if axis == "y":
            return lax.ppermute(value, "col", [(0, 1), (1, 0)])
        flip = {"core": 1, "x": 2}[axis]
        return lax.ppermute(value, "row", [(i, i ^ flip) for i in range(n_row)])

    first = take(tile, blk)
    raw = over("y", first)

    send_on, keep_on = right_grams(place, tile, blk, (3, 2), first)
    near_on = over("core", send_on)
    send, keep = right_grams(place, tile, blk, (1, 0), keep_on)
    near = over("core", send)
    far = over("x", fold(keep_on, near_on))
    lsend = left_grams(place, tile, blk, lambda place: 1 - place[1], send)

    own, half = right_roots(full_dim, place, rstats, keep, near, far, tile, lsend)
    came_a = over("y", half)
    own = hold(own, raw, half)
    own_c = over("core", own)
    own_x = over("x", own)
    lkeep = left_grams(place, tile, blk, lambda place: place[1], own)
    came_b = over("y", core_apply(place, tile, own_c))
    own_x = hold(own_x, lkeep)
    roots, part = spread_roots(own, own_c, own_x, over("core", own_x))

    (half,) = right_apply(place, tile, roots, 0, (blk,), part, (came_a,))
    came_c = over("y", half)
    left = left_roots(full_dim, place, lstats, lkeep, came_a)
    (half,) = right_apply(place, tile, roots, 1, (blk,), None, (came_b, left))
    came_d = over("y", half)

    def crossed(block, start=0):
        return (lambda place: (1 - place[1]) * tile_cols + block(place) * blk + start,)

    out, done = update(
        place, tile, left, roots, None, shape,
        lambda s, place: (place[1], s),
        lambda s, place: (0, place[1] * halves + s),
    )
    (half,) = right_apply(place, tile, roots, 2, (blk,), None, (came_c, done))
    came_e = over("y", half)
    (out,) = finish(came_a, left, out, crossed(own_first))
    (out,) = finish(came_b, left, out, crossed(core_first))
    part = rest_of(came_c, rows)
    part_x = over("x", part)
    roots_raw = join_roots(part, over("core", part), part_x, over("core", part_x))
    out, done = update(
        place, raw, left, roots_raw, out, shape,
        lambda s, place: (0, s),
        lambda s, place: (0, (1 - place[1]) * halves + jnp.where(s == 0, RAW[0], RAW[1])),
    )
    last = (blk // 2, blk // 2)
    came_last = [over("y", half) for half in right_apply(place, tile, roots, 3, last, None, (came_d, done))]
    for k, value in enumerate((came_c, came_d, came_e)):
        (out,) = finish(value, left, out, crossed(functools.partial(later, k)))
    for k, value in enumerate(came_last):
        (out,) = finish(value, left, out, crossed(functools.partial(later, 3), k * last[0]))
    return out.reshape(1, rows, 2 * tile_cols)


def per_device(n_row, n_col, grads, left_stats, right_stats):
    mats, tile_rows, tile_cols = grads.shape
    blk = left_stats.shape[2]
    full_dim = tile_cols * n_col
    if mats == 1 and n_col == 2 and n_row == 4 and tile_rows == 4 * blk and tile_cols == 8 * blk:
        return exchange_device(full_dim, n_row, grads, left_stats, right_stats)
    return general_device(full_dim, grads, left_stats, right_stats)


def solution(mesh):
    return jax.shard_map(
        functools.partial(per_device, mesh.shape["row"], mesh.shape["col"]),
        mesh=mesh,
        in_specs=(P("mat", "row", "col"), P("mat", "row", None), P("mat", "col", None)),
        out_specs=P("mat", ("row", "col"), None),
        check_vma=False,
    )
```

```python
import functools

import jax
import jax.numpy as jnp
from jax import lax
from jax.experimental import pallas as pl
from jax.experimental.pallas import tpu as pltpu
from jax.sharding import PartitionSpec as P

ITERS = 3
beta_mix = 0.5
eps_shift = 0.001
PAD = 8
VMEM_LIMIT = 24 * 1024 * 1024
SMALL = pl.CostEstimate(flops=1, bytes_accessed=1, transcendentals=0)


def matmul(left, right):
    return jnp.einsum("...ij,...jk->...ik", left, right, precision=lax.Precision.HIGHEST)


def newton_root(factor):
    size = factor.shape[-1]
    ident = jnp.eye(size, dtype=jnp.float32)
    scale = jnp.sqrt(jnp.sum(factor * factor, axis=(-2, -1), keepdims=True))
    moving = factor / scale
    result = jnp.broadcast_to(ident, factor.shape)
    for count in range(ITERS):
        step_mat = (5.0 * ident - moving) * 0.25
        result = matmul(result, step_mat)
        squared = matmul(step_mat, step_mat)
        moving = matmul(matmul(squared, squared), moving)
    return result * jnp.power(scale, -0.25)


def general_device(full_dim, grads, left_stats, right_stats):
    mats, tile_rows, tile_cols = grads.shape
    blk = left_stats.shape[2]
    row_blocks = tile_rows // blk
    col_blocks = tile_cols // blk
    ident = jnp.eye(blk, dtype=jnp.float32)
    by_rows = grads.reshape(mats, row_blocks, blk, tile_cols)
    left_part = jnp.einsum("mibd,mied->mibe", by_rows, by_rows, precision=lax.Precision.HIGHEST) / full_dim
    by_cols = grads.reshape(mats, tile_rows, col_blocks, blk)
    right_part = (
        jnp.einsum("mdjb,mdje->mjbe", by_cols, by_cols, precision=lax.Precision.HIGHEST) / full_dim
    )
    left_gram = lax.psum(left_part, "col")
    right_gram = lax.psum(right_part, "row")
    left_factor = (
        beta_mix * left_stats.reshape(mats, row_blocks, blk, blk)
        + (1.0 - beta_mix) * left_gram
        + eps_shift * ident
    )
    right_factor = (
        beta_mix * right_stats.reshape(mats, col_blocks, blk, blk)
        + (1.0 - beta_mix) * right_gram
        + eps_shift * ident
    )
    left_root = newton_root(left_factor)
    right_root = newton_root(right_factor)
    half = jnp.einsum("mibe,mied->mibd", left_root, by_rows, precision=lax.Precision.HIGHEST)
    half = half.reshape(mats, tile_rows, col_blocks, blk)
    full = jnp.einsum("mdjb,mjbe->mdje", half, right_root, precision=lax.Precision.HIGHEST)
    full = full.reshape(mats, tile_rows, tile_cols)
    return lax.all_to_all(full, "col", split_axis=1, concat_axis=2, tiled=True)


def here():
    return lax.axis_index("row"), lax.axis_index("col")


def placed(index_map):
    return lambda s: index_map(s, here())


def split(value):
    high = value.astype(jnp.bfloat16)
    low = (value - high.astype(jnp.float32)).astype(jnp.bfloat16)
    return high, low


def dot(left, right, dims=((1,), (0,))):
    return lax.dot_general(left, right, (dims, ((), ())), preferred_element_type=jnp.float32)


def product(left, right):
    lh, ll = left
    rh, rl = right
    return dot(lh, rh) + (dot(lh, rl) + dot(ll, rh))


def places(blk):
    rows = lax.broadcasted_iota(jnp.int32, (blk, blk), 0)
    cols = lax.broadcasted_iota(jnp.int32, (blk, blk), 1)
    return rows, cols


def pack(first, second):
    blk = first.shape[0]
    rows, cols = places(blk)
    body = jnp.where(rows <= cols, first, second)
    diag = jnp.sum(jnp.where(rows == cols, second, 0.0), axis=0, keepdims=True)
    return body, jnp.broadcast_to(diag, (PAD, blk))


def unpack(body, diag):
    blk = body.shape[0]
    rows, cols = places(blk)
    turned = body.T
    first = jnp.where(rows <= cols, body, turned)
    second = jnp.where(rows > cols, body, jnp.where(rows == cols, diag, turned))
    return first, second


def right_gram_kernel(g_ref, after_ref, *out_refs):
    step = pl.program_id(0)
    blk = g_ref.shape[1] // 2
    high, low = split(g_ref[...])
    grams = []
    for b in range(2):
        hb = high[:, b * blk : (b + 1) * blk]
        lb = low[:, b * blk : (b + 1) * blk]
        both = dot(hb, hb, ((0,), (0,)))
        cross = dot(hb, lb, ((0,), (0,)))
        grams.append(both + (cross + cross.T))
    body, diag = pack(*grams)

    for at, ref in enumerate(out_refs):

        @pl.when(step == at)
        def _():
            ref[:blk, :] = body
            ref[blk:, :] = diag


def right_grams(tile, blk, flips, after):
    rows = tile.shape[0]
    tall = blk + PAD
    flip = lambda s: jnp.where(s == 0, flips[0], flips[1])
    return pl.pallas_call(
        right_gram_kernel,
        out_shape=(jax.ShapeDtypeStruct((tall, blk), jnp.float32),) * 2,
        grid_spec=pltpu.PrefetchScalarGridSpec(
            num_scalar_prefetch=0,
            grid=(2,),
            in_specs=[
                pl.BlockSpec((rows, 2 * blk), placed(lambda s, place: (0, place[0] ^ flip(s)))),
                pl.BlockSpec(memory_space=pl.ANY),
            ],
            out_specs=(pl.BlockSpec((tall, blk), lambda s: (0, 0)),) * 2,
        ),
        compiler_params=pltpu.CompilerParams(vmem_limit_bytes=VMEM_LIMIT),
        cost_estimate=SMALL,
        name="right_grams",
    )(tile, after)


def left_gram_kernel(g_ref, after_ref, out_ref, lhh, lcross):
    step = pl.program_id(0)
    last = pl.num_programs(0) - 1
    blk = lhh.shape[-1]
    high, low = split(g_ref[...])
    for i in range(2):
        hi = high[i * blk : (i + 1) * blk, :]
        lo = low[i * blk : (i + 1) * blk, :]
        both = dot(hi, hi, ((1,), (1,)))
        cross = dot(lo, hi, ((1,), (1,)))

        @pl.when(step == 0)
        def _():
            lhh[i] = both
            lcross[i] = cross

        @pl.when(step > 0)
        def _():
            lhh[i] += both
            lcross[i] += cross

    @pl.when(step == last)
    def _():
        body, diag = pack(*(lhh[b] + (lcross[b] + lcross[b].T) for b in range(2)))
        out_ref[:blk, :] = body
        out_ref[blk:, :] = diag


def left_grams(tile, blk, at, after):
    width = tile.shape[1]
    tall = blk + PAD
    return pl.pallas_call(
        left_gram_kernel,
        out_shape=jax.ShapeDtypeStruct((tall, blk), jnp.float32),
        grid_spec=pltpu.PrefetchScalarGridSpec(
            num_scalar_prefetch=0,
            grid=(width // (4 * blk),),
            in_specs=[
                pl.BlockSpec((2 * blk, 4 * blk), placed(lambda s, place: (at(place), s))),
                pl.BlockSpec(memory_space=pl.ANY),
            ],
            out_specs=pl.BlockSpec((tall, blk), lambda s: (0, 0)),
            scratch_shapes=[
                pltpu.VMEM((2, blk, blk), jnp.float32),
                pltpu.VMEM((2, blk, blk), jnp.float32),
            ],
        ),
        compiler_params=pltpu.CompilerParams(vmem_limit_bytes=VMEM_LIMIT),
        cost_estimate=SMALL,
        name="left_grams",
    )(tile, after)


RAW = (1, 3)


def own_first(place):
    return place[0] * 2


def core_first(place):
    return (place[0] ^ 1) * 2


def later(k, place):
    return jnp.where(place[0] < 2, 4 + k, jnp.where(k < 2, 2 * k, 2 * k + 1))


def take_kernel(g_ref, out_ref, sems):
    rows, wide = out_ref.shape
    blk = wide // len(RAW)
    top = pl.multiple_of((1 - here()[1]) * rows, rows)
    copies = [
        pltpu.make_async_copy(
            g_ref.at[pl.ds(top, rows), pl.ds(block * blk, blk)], out_ref.at[:, pl.ds(k * blk, blk)], sems.at[k]
        )
        for k, block in enumerate(RAW)
    ]
    for copy in copies:
        copy.start()
    for copy in copies:
        copy.wait()


def take(tile, blk):
    return pl.pallas_call(
        take_kernel,
        out_shape=jax.ShapeDtypeStruct((tile.shape[0] // 2, len(RAW) * blk), jnp.float32),
        in_specs=[pl.BlockSpec(memory_space=pl.ANY)],
        out_specs=pl.BlockSpec(memory_space=pl.ANY),
        scratch_shapes=[pltpu.SemaphoreType.DMA((len(RAW),))],
        compiler_params=pltpu.CompilerParams(vmem_limit_bytes=VMEM_LIMIT),
        cost_estimate=SMALL,
        name="take",
    )(tile)


def fold_kernel(a_ref, b_ref, out_ref):
    out_ref[...] = a_ref[...] + b_ref[...]


def fold(kept, near):
    return pl.pallas_call(
        fold_kernel,
        out_shape=jax.ShapeDtypeStruct(kept.shape, jnp.float32),
        compiler_params=pltpu.CompilerParams(vmem_limit_bytes=VMEM_LIMIT),
        cost_estimate=SMALL,
        name="fold",
    )(kept, near)


def hold_kernel(a_ref, *rest):
    out_ref = rest[-1]
    out_ref[...] = a_ref[...]


def hold(value, *after):
    return pl.pallas_call(
        hold_kernel,
        out_shape=jax.ShapeDtypeStruct(value.shape, jnp.float32),
        in_specs=[pl.BlockSpec(memory_space=pltpu.VMEM)] + [pl.BlockSpec(memory_space=pl.ANY)] * len(after),
        compiler_params=pltpu.CompilerParams(vmem_limit_bytes=VMEM_LIMIT),
        cost_estimate=SMALL,
        name="hold",
    )(value, *after)


def pair_roots(full_dim, stats_ref, body, diag):
    blk = body.shape[0]
    rows, cols = places(blk)
    ident = jnp.where(rows == cols, 1.0, 0.0)
    moving, scales = [], []
    for b, gram in enumerate(unpack(body, diag)):
        factor = (
            beta_mix * stats_ref[b * blk : (b + 1) * blk, :]
            + (1.0 - beta_mix) * (gram / full_dim)
            + eps_shift * ident
        )
        scale = jnp.sqrt(jnp.sum(factor * factor, keepdims=True))
        moving.append(factor / scale)
        scales.append(scale)
    result = None
    for count in range(ITERS):
        steps = [(5.0 * ident - m) * 0.25 for m in moving]
        parts = [split(s) for s in steps]
        if result is None:
            result = steps
        else:
            result = [product(split(r), p) for r, p in zip(result, parts)]
        if count < ITERS - 1:
            squared = [split(product(p, p)) for p in parts]
            fourth = [split(product(s, s)) for s in squared]
            moving = [product(f, split(m)) for f, m in zip(fourth, moving)]
    return [r * jnp.exp(-0.25 * jnp.log(s)) for r, s in zip(result, scales)]


def right_kernel(full_dim, stats_ref, a_ref, b_ref, c_ref, g_ref, out_ref, half_ref):
    blk = stats_ref.shape[1]
    total = a_ref[...] + b_ref[...] + c_ref[...]
    roots = pair_roots(full_dim, stats_ref, total[:blk], total[blk : blk + 1])
    half_ref[...] = product(split(g_ref[...]), split(roots[0]))
    body, diag = pack(*roots)
    out_ref[:blk, :] = body
    out_ref[blk:, :] = diag


def right_roots(full_dim, stats, kept, near, far, tile):
    blk = stats.shape[1]
    tall = blk + PAD
    rows = tile.shape[0] // 2
    flat = pl.BlockSpec((tall, blk), lambda s: (0, 0))
    return pl.pallas_call(
        functools.partial(right_kernel, full_dim),
        out_shape=(
            jax.ShapeDtypeStruct((tall, blk), jnp.float32),
            jax.ShapeDtypeStruct((rows, blk), jnp.float32),
        ),
        grid_spec=pltpu.PrefetchScalarGridSpec(
            num_scalar_prefetch=0,
            grid=(1,),
            in_specs=[
                pl.BlockSpec((2 * blk, blk), placed(lambda s, place: (place[0], 0))),
                flat,
                flat,
                flat,
                pl.BlockSpec((rows, blk), placed(lambda s, place: (1 - place[1], own_first(place)))),
            ],
            out_specs=(
                flat,
                pl.BlockSpec((rows, blk), lambda s: (0, 0)),
            ),
        ),
        compiler_params=pltpu.CompilerParams(vmem_limit_bytes=VMEM_LIMIT),
        cost_estimate=SMALL,
        name="right_roots",
    )(stats, kept, near, far, tile)


def left_kernel(full_dim, stats_ref, a_ref, b_ref, out_ref):
    blk = stats_ref.shape[1]
    total = a_ref[...] + b_ref[b_ref.shape[0] - a_ref.shape[0] :, :]
    for b, root in enumerate(pair_roots(full_dim, stats_ref, total[:blk], total[blk : blk + 1])):
        high, low = split(root)
        out_ref[b, 0] = high
        out_ref[b, 1] = low


def left_roots(full_dim, stats, kept, came):
    blk = stats.shape[1]
    tall = blk + PAD
    return pl.pallas_call(
        functools.partial(left_kernel, full_dim),
        out_shape=jax.ShapeDtypeStruct((2, 2, blk, blk), jnp.bfloat16),
        grid_spec=pltpu.PrefetchScalarGridSpec(
            num_scalar_prefetch=0,
            grid=(1,),
            in_specs=[
                pl.BlockSpec((2 * blk, blk), placed(lambda s, place: (place[1], 0))),
                pl.BlockSpec((tall, blk), lambda s: (0, 0)),
                pl.BlockSpec(came.shape, lambda s: (0, 0)),
            ],
            out_specs=pl.BlockSpec((2, 2, blk, blk), lambda s: (0, 0, 0, 0)),
        ),
        compiler_params=pltpu.CompilerParams(vmem_limit_bytes=VMEM_LIMIT),
        cost_estimate=SMALL,
        name="left_roots",
    )(stats, kept, came)


def put_roots(out_ref, at, roots):
    for b, root in enumerate(roots):
        high, low = split(root)
        out_ref[at + b, 0] = high
        out_ref[at + b, 1] = low


def spread_kernel(own_ref, c_ref, x_ref, xc_ref, out_ref, cut_ref, seconds, body):
    blk = out_ref.shape[-1]
    r = here()[0]
    for flip, ref in enumerate((own_ref, c_ref, x_ref, xc_ref)):
        roots = unpack(ref[:blk, :], ref[blk : blk + 1, :])
        put_roots(out_ref, 2 * (r ^ flip), roots)
        seconds[r ^ flip] = roots[1]
    part = cut_ref.shape[0] - PAD
    body[...], diag = pack(seconds[RAW[0] // 2], seconds[RAW[1] // 2])
    cut_ref[:part, :] = body[pl.ds(pl.multiple_of(r * part, part), part), :]
    cut_ref[part:, :] = diag


def spread_roots(*packed):
    blk = packed[0].shape[1]
    count = len(packed)
    return pl.pallas_call(
        spread_kernel,
        out_shape=(
            jax.ShapeDtypeStruct((2 * count, 2, blk, blk), jnp.bfloat16),
            jax.ShapeDtypeStruct((blk // count + PAD, blk), jnp.float32),
        ),
        scratch_shapes=[pltpu.VMEM((count, blk, blk), jnp.float32), pltpu.VMEM((blk, blk), jnp.float32)],
        compiler_params=pltpu.CompilerParams(vmem_limit_bytes=VMEM_LIMIT),
        cost_estimate=SMALL,
        name="spread_roots",
    )(*packed)


def rest_kernel(a_ref, out_ref):
    out_ref[...] = a_ref[a_ref.shape[0] - out_ref.shape[0] :, :]


def rest_of(value, rows):
    return pl.pallas_call(
        rest_kernel,
        out_shape=jax.ShapeDtypeStruct((value.shape[0] - rows, value.shape[1]), jnp.float32),
        compiler_params=pltpu.CompilerParams(vmem_limit_bytes=VMEM_LIMIT),
        cost_estimate=SMALL,
        name="rest_of",
    )(value)


def join_kernel(own_ref, c_ref, x_ref, xc_ref, out_ref, body):
    part = own_ref.shape[0] - PAD
    r = here()[0]
    for flip, ref in enumerate((own_ref, c_ref, x_ref, xc_ref)):
        body[pl.ds(pl.multiple_of((r ^ flip) * part, part), part), :] = ref[:part, :]
    put_roots(out_ref, 0, unpack(body[...], own_ref[part : part + 1, :]))


def join_roots(*parts):
    blk = parts[0].shape[1]
    return pl.pallas_call(
        join_kernel,
        out_shape=jax.ShapeDtypeStruct((2, 2, blk, blk), jnp.bfloat16),
        scratch_shapes=[pltpu.VMEM((blk, blk), jnp.float32)],
        compiler_params=pltpu.CompilerParams(vmem_limit_bytes=VMEM_LIMIT),
        cost_estimate=SMALL,
        name="join_roots",
    )(*parts)


def core_apply_kernel(g_ref, packed_ref, under_ref, out_ref):
    rows, blk = g_ref.shape
    root = unpack(packed_ref[:blk, :], packed_ref[blk : blk + 1, :])[0]
    out_ref[:rows, :] = product(split(g_ref[...]), split(root))
    out_ref[rows:, :] = under_ref[...]


def core_apply(tile, packed, under):
    rows = tile.shape[0] // 2
    tall, blk = packed.shape
    return pl.pallas_call(
        core_apply_kernel,
        out_shape=jax.ShapeDtypeStruct((rows + tall, blk), jnp.float32),
        grid_spec=pltpu.PrefetchScalarGridSpec(
            num_scalar_prefetch=0,
            grid=(1,),
            in_specs=[
                pl.BlockSpec((rows, blk), placed(lambda s, place: (1 - place[1], core_first(place)))),
                pl.BlockSpec((tall, blk), lambda s: (0, 0)),
                pl.BlockSpec((tall, blk), lambda s: (0, 0)),
            ],
            out_specs=pl.BlockSpec((rows + tall, blk), lambda s: (0, 0)),
        ),
        compiler_params=pltpu.CompilerParams(vmem_limit_bytes=VMEM_LIMIT),
        cost_estimate=SMALL,
        name="core_apply",
    )(tile, packed, under)


def right_apply_kernel(width, carries, g_ref, right_ref, *rest):
    step = pl.program_id(0)
    out_refs = rest[-len(width) :]
    value = product(split(g_ref[...]), (right_ref[0, 0], right_ref[0, 1]))
    blk = value.shape[1]
    start = 0
    for size, ref in zip(width, out_refs):
        for b in range(start // blk, -(-(start + size) // blk)):
            low, high = max(start, b * blk), min(start + size, (b + 1) * blk)

            @pl.when(step == b)
            def _():
                ref[: value.shape[0], low - start : high - start] = value[:, low - b * blk : high - b * blk]

        start += size
    if carries:
        out_refs[0][value.shape[0] :, :] = rest[0][...]


def right_apply(tile, right, first, width, under, after):
    rows = tile.shape[0] // 2
    blk = right.shape[-1]
    in_specs = [
        pl.BlockSpec((rows, blk), placed(lambda s, place: (1 - place[1], later(first + s, place)))),
        pl.BlockSpec((1, 2, blk, blk), placed(lambda s, place: (later(first + s, place), 0, 0, 0))),
    ]
    operands = [tile, right]
    tall = rows
    if under is not None:
        tall += under.shape[0]
        in_specs.append(pl.BlockSpec(under.shape, lambda s: (0, 0)))
        operands.append(under)
    return pl.pallas_call(
        functools.partial(right_apply_kernel, width, under is not None),
        out_shape=tuple(jax.ShapeDtypeStruct((tall, w), jnp.float32) for w in width),
        grid_spec=pltpu.PrefetchScalarGridSpec(
            num_scalar_prefetch=0,
            grid=(sum(width) // blk,),
            in_specs=in_specs + [pl.BlockSpec(memory_space=pl.ANY)] * len(after),
            out_specs=tuple(pl.BlockSpec((tall, w), lambda s: (0, 0)) for w in width),
        ),
        compiler_params=pltpu.CompilerParams(vmem_limit_bytes=VMEM_LIMIT),
        cost_estimate=SMALL,
        name="right_apply",
    )(*operands, *after)


def left_product(left_ref, value, out_ref):
    blk = left_ref.shape[-1]
    for i in range(value.shape[0] // blk):
        part = split(value[i * blk : (i + 1) * blk])
        out_ref[i * blk : (i + 1) * blk, :] = product((left_ref[i, 0], left_ref[i, 1]), part)


def update_kernel(g_ref, left_ref, right_ref, *rest):
    half = product(split(g_ref[...]), (right_ref[0, 0], right_ref[0, 1]))
    left_product(left_ref, half, rest[-2])
    rest[-1][...] = jnp.zeros_like(rest[-1])


def finish_kernel(columns, half_ref, left_ref, out_before, out_ref, *rest):
    stage, sems = rest[-2:]
    blk = left_ref.shape[-1]
    size = stage.shape[1] // len(columns)
    copies = []
    for b, column in enumerate(columns):
        start = pl.multiple_of(column(here()), size)
        cols = pl.ds(b * size, size)
        for i in range(left_ref.shape[0]):
            rows = pl.ds(i * blk, blk)
            stage[rows, cols] = product((left_ref[i, 0], left_ref[i, 1]), split(half_ref[rows, cols]))
            copies.append(
                pltpu.make_async_copy(stage.at[rows, cols], out_ref.at[rows, pl.ds(start, size)], sems.at[len(copies)])
            )
            copies[-1].start()
    for done_ref in rest[:-2]:
        done_ref[...] = jnp.zeros_like(done_ref)
    for copy in copies:
        copy.wait()


def finish(half, left, out, columns, mark=False):
    width = half.shape[1]
    rows = out.shape[0]
    vmem = pl.BlockSpec(memory_space=pltpu.VMEM)
    anywhere = pl.BlockSpec(memory_space=pl.ANY)
    shapes = (jax.ShapeDtypeStruct(out.shape, jnp.float32), jax.ShapeDtypeStruct((8, 128), jnp.float32))
    return pl.pallas_call(
        functools.partial(finish_kernel, columns),
        out_shape=shapes if mark else shapes[:1],
        in_specs=[vmem, vmem, anywhere],
        out_specs=(anywhere, vmem) if mark else (anywhere,),
        scratch_shapes=[
            pltpu.VMEM((rows, width), jnp.float32),
            pltpu.SemaphoreType.DMA((left.shape[0] * len(columns),)),
        ],
        input_output_aliases={2: 0},
        compiler_params=pltpu.CompilerParams(vmem_limit_bytes=VMEM_LIMIT),
        cost_estimate=SMALL,
        name="finish",
    )(half, left, out)


def update(source, left, right, out, out_shape, g_map, out_map, after=()):
    rows = out_shape[0]
    blk = left.shape[-1]
    in_specs = [
        pl.BlockSpec((rows, blk), placed(g_map)),
        pl.BlockSpec((2, 2, blk, blk), lambda s: (0, 0, 0, 0)),
        pl.BlockSpec((1, 2, blk, blk), lambda s: (s, 0, 0, 0)),
    ]
    operands = [source, left, right]
    aliases = {}
    if out is not None:
        aliases = {len(operands): 0}
        in_specs.append(pl.BlockSpec(memory_space=pl.ANY))
        operands.append(out)
    in_specs += [pl.BlockSpec(memory_space=pl.ANY)] * len(after)
    return pl.pallas_call(
        update_kernel,
        out_shape=(jax.ShapeDtypeStruct(out_shape, jnp.float32), jax.ShapeDtypeStruct((8, 128), jnp.float32)),
        grid_spec=pltpu.PrefetchScalarGridSpec(
            num_scalar_prefetch=0,
            grid=(right.shape[0],),
            in_specs=in_specs,
            out_specs=(pl.BlockSpec((rows, blk), placed(out_map)), pl.BlockSpec((8, 128), lambda s: (0, 0))),
        ),
        input_output_aliases=aliases,
        compiler_params=pltpu.CompilerParams(vmem_limit_bytes=VMEM_LIMIT),
        cost_estimate=SMALL,
        name="update",
    )(*operands, *after)


def exchange_device(full_dim, n_row, grads, left_stats, right_stats):
    tile_rows, tile_cols = grads.shape[1:]
    blk = left_stats.shape[2]
    tile = pltpu.with_memory_space_constraint(grads.reshape(tile_rows, tile_cols), pltpu.HBM)
    lstats = left_stats.reshape(tile_rows, blk)
    rstats = right_stats.reshape(tile_cols, blk)
    rows = tile_rows // 2
    shape = (rows, 2 * tile_cols)
    halves = tile_cols // blk

    def over(axis, value):
        if axis == "y":
            return lax.ppermute(value, "col", [(0, 1), (1, 0)])
        flip = {"core": 1, "x": 2}[axis]
        return lax.ppermute(value, "row", [(i, i ^ flip) for i in range(n_row)])

    first = take(tile, blk)
    raw = over("y", first)

    send_on, keep_on = right_grams(tile, blk, (3, 2), first)
    far = fold(keep_on, over("core", send_on))
    send, keep = right_grams(tile, blk, (1, 0), far)
    near = over("core", send)
    far = over("x", far)

    own, half = right_roots(full_dim, rstats, keep, near, far, tile)
    came_a = over("y", half)
    lsend = left_grams(tile, blk, lambda place: 1 - place[1], half)
    own = hold(own, raw, lsend)
    own_c = over("core", own)
    own_x = over("x", own)
    half = core_apply(tile, own_c, lsend)
    came_b = over("y", half)
    own_x = hold(own_x, half, came_a)
    lkeep = left_grams(tile, blk, lambda place: place[1], half)
    roots, part = spread_roots(own, own_c, own_x, over("core", own_x))

    (half,) = right_apply(tile, roots, 0, (blk,), part, (lkeep,))
    came_c = over("y", half)
    (half,) = right_apply(tile, roots, 1, (blk,), None, (came_b,))
    came_d = over("y", half)

    def crossed(block, start=0):
        return (lambda place: (1 - place[1]) * tile_cols + block(place) * blk + start,)

    left = left_roots(full_dim, lstats, lkeep, came_b)
    out, done = update(
        tile, left, roots, None, shape,
        lambda s, place: (place[1], s),
        lambda s, place: (0, place[1] * halves + s),
    )
    (half,) = right_apply(tile, roots, 2, (blk,), None, (came_c, done))
    came_e = over("y", half)
    last = (blk // 2, blk // 2)
    held = right_apply(tile, roots, 3, last, None, (came_d,))
    came_last = [over("y", half) for half in held]
    (out,) = finish(came_a, left, out, crossed(own_first))
    (out,) = finish(came_b, left, out, crossed(core_first))
    part = rest_of(came_c, rows)
    part_x = over("x", part)
    roots_raw = join_roots(part, over("core", part), part_x, over("core", part_x))
    out, done = update(
        raw, left, roots_raw, out, shape,
        lambda s, place: (0, s),
        lambda s, place: (0, (1 - place[1]) * halves + jnp.where(s == 0, RAW[0], RAW[1])),
        held[:1],
    )
    for k, value in enumerate((came_c, came_d, came_e)):
        (out,) = finish(value, left, out, crossed(functools.partial(later, k)))
    for k, value in enumerate(came_last):
        (out,) = finish(value, left, out, crossed(functools.partial(later, 3), k * last[0]))
    return out.reshape(1, rows, 2 * tile_cols)


def per_device(n_row, n_col, grads, left_stats, right_stats):
    mats, tile_rows, tile_cols = grads.shape
    blk = left_stats.shape[2]
    full_dim = tile_cols * n_col
    if mats == 1 and n_col == 2 and n_row == 4 and tile_rows == 4 * blk and tile_cols == 8 * blk:
        return exchange_device(full_dim, n_row, grads, left_stats, right_stats)
    return general_device(full_dim, grads, left_stats, right_stats)


def solution(mesh):
    return jax.shard_map(
        functools.partial(per_device, mesh.shape["row"], mesh.shape["col"]),
        mesh=mesh,
        in_specs=(P("mat", "row", "col"), P("mat", "row", None), P("mat", "col", None)),
        out_specs=P("mat", ("row", "col"), None),
        check_vma=False,
    )
```

```python
import functools

import jax
import jax.numpy as jnp
from jax import lax
from jax.experimental import pallas as pl
from jax.experimental.pallas import tpu as pltpu
from jax.sharding import PartitionSpec as P

ITERS = 3
beta_mix = 0.5
eps_shift = 0.001
PAD = 8
VMEM_LIMIT = 24 * 1024 * 1024
SMALL = pl.CostEstimate(flops=1, bytes_accessed=1, transcendentals=0)


def matmul(left, right):
    return jnp.einsum("...ij,...jk->...ik", left, right, precision=lax.Precision.HIGHEST)


def newton_root(factor):
    size = factor.shape[-1]
    ident = jnp.eye(size, dtype=jnp.float32)
    scale = jnp.sqrt(jnp.sum(factor * factor, axis=(-2, -1), keepdims=True))
    moving = factor / scale
    result = jnp.broadcast_to(ident, factor.shape)
    for count in range(ITERS):
        step_mat = (5.0 * ident - moving) * 0.25
        result = matmul(result, step_mat)
        squared = matmul(step_mat, step_mat)
        moving = matmul(matmul(squared, squared), moving)
    return result * jnp.power(scale, -0.25)


def general_device(full_dim, grads, left_stats, right_stats):
    mats, tile_rows, tile_cols = grads.shape
    blk = left_stats.shape[2]
    row_blocks = tile_rows // blk
    col_blocks = tile_cols // blk
    ident = jnp.eye(blk, dtype=jnp.float32)
    by_rows = grads.reshape(mats, row_blocks, blk, tile_cols)
    left_part = jnp.einsum("mibd,mied->mibe", by_rows, by_rows, precision=lax.Precision.HIGHEST) / full_dim
    by_cols = grads.reshape(mats, tile_rows, col_blocks, blk)
    right_part = (
        jnp.einsum("mdjb,mdje->mjbe", by_cols, by_cols, precision=lax.Precision.HIGHEST) / full_dim
    )
    left_gram = lax.psum(left_part, "col")
    right_gram = lax.psum(right_part, "row")
    left_factor = (
        beta_mix * left_stats.reshape(mats, row_blocks, blk, blk)
        + (1.0 - beta_mix) * left_gram
        + eps_shift * ident
    )
    right_factor = (
        beta_mix * right_stats.reshape(mats, col_blocks, blk, blk)
        + (1.0 - beta_mix) * right_gram
        + eps_shift * ident
    )
    left_root = newton_root(left_factor)
    right_root = newton_root(right_factor)
    half = jnp.einsum("mibe,mied->mibd", left_root, by_rows, precision=lax.Precision.HIGHEST)
    half = half.reshape(mats, tile_rows, col_blocks, blk)
    full = jnp.einsum("mdjb,mjbe->mdje", half, right_root, precision=lax.Precision.HIGHEST)
    full = full.reshape(mats, tile_rows, tile_cols)
    return lax.all_to_all(full, "col", split_axis=1, concat_axis=2, tiled=True)


def here():
    return lax.axis_index("row"), lax.axis_index("col")


def placed(index_map):
    return lambda s: index_map(s, here())


def split(value):
    high = value.astype(jnp.bfloat16)
    low = (value - high.astype(jnp.float32)).astype(jnp.bfloat16)
    return high, low


def dot(left, right, dims=((1,), (0,))):
    return lax.dot_general(left, right, (dims, ((), ())), preferred_element_type=jnp.float32)


def product(left, right):
    lh, ll = left
    rh, rl = right
    return dot(lh, rh) + (dot(lh, rl) + dot(ll, rh))


def places(blk):
    rows = lax.broadcasted_iota(jnp.int32, (blk, blk), 0)
    cols = lax.broadcasted_iota(jnp.int32, (blk, blk), 1)
    return rows, cols


def pack(first, second):
    blk = first.shape[0]
    rows, cols = places(blk)
    body = jnp.where(rows <= cols, first, second)
    diag = jnp.sum(jnp.where(rows == cols, second, 0.0), axis=0, keepdims=True)
    return body, jnp.broadcast_to(diag, (PAD, blk))


def unpack(body, diag):
    blk = body.shape[0]
    rows, cols = places(blk)
    turned = body.T
    first = jnp.where(rows <= cols, body, turned)
    second = jnp.where(rows > cols, body, jnp.where(rows == cols, diag, turned))
    return first, second


def right_gram_kernel(g_ref, after_ref, *out_refs):
    step = pl.program_id(0)
    blk = g_ref.shape[1] // 2
    high, low = split(g_ref[...])
    grams = []
    for b in range(2):
        hb = high[:, b * blk : (b + 1) * blk]
        lb = low[:, b * blk : (b + 1) * blk]
        both = dot(hb, hb, ((0,), (0,)))
        cross = dot(hb, lb, ((0,), (0,)))
        grams.append(both + (cross + cross.T))
    body, diag = pack(*grams)

    for at, ref in enumerate(out_refs):

        @pl.when(step == at)
        def _():
            ref[:blk, :] = body
            ref[blk:, :] = diag


def right_grams(tile, blk, flips, after):
    rows = tile.shape[0]
    tall = blk + PAD
    flip = lambda s: jnp.where(s == 0, flips[0], flips[1])
    return pl.pallas_call(
        right_gram_kernel,
        out_shape=(jax.ShapeDtypeStruct((tall, blk), jnp.float32),) * 2,
        grid_spec=pltpu.PrefetchScalarGridSpec(
            num_scalar_prefetch=0,
            grid=(2,),
            in_specs=[
                pl.BlockSpec((rows, 2 * blk), placed(lambda s, place: (0, place[0] ^ flip(s)))),
                pl.BlockSpec(memory_space=pl.ANY),
            ],
            out_specs=(pl.BlockSpec((tall, blk), lambda s: (0, 0)),) * 2,
        ),
        compiler_params=pltpu.CompilerParams(vmem_limit_bytes=VMEM_LIMIT),
        cost_estimate=SMALL,
        name="right_grams",
    )(tile, after)


def left_gram_kernel(g_ref, after_ref, out_ref, lhh, lcross):
    step = pl.program_id(0)
    last = pl.num_programs(0) - 1
    blk = lhh.shape[-1]
    high, low = split(g_ref[...])
    for i in range(2):
        hi = high[i * blk : (i + 1) * blk, :]
        lo = low[i * blk : (i + 1) * blk, :]
        both = dot(hi, hi, ((1,), (1,)))
        cross = dot(lo, hi, ((1,), (1,)))

        @pl.when(step == 0)
        def _():
            lhh[i] = both
            lcross[i] = cross

        @pl.when(step > 0)
        def _():
            lhh[i] += both
            lcross[i] += cross

    @pl.when(step == last)
    def _():
        body, diag = pack(*(lhh[b] + (lcross[b] + lcross[b].T) for b in range(2)))
        out_ref[:blk, :] = body
        out_ref[blk:, :] = diag


def left_grams(tile, blk, at, after):
    width = tile.shape[1]
    tall = blk + PAD
    return pl.pallas_call(
        left_gram_kernel,
        out_shape=jax.ShapeDtypeStruct((tall, blk), jnp.float32),
        grid_spec=pltpu.PrefetchScalarGridSpec(
            num_scalar_prefetch=0,
            grid=(width // (4 * blk),),
            in_specs=[
                pl.BlockSpec((2 * blk, 4 * blk), placed(lambda s, place: (at(place), s))),
                pl.BlockSpec(memory_space=pl.ANY),
            ],
            out_specs=pl.BlockSpec((tall, blk), lambda s: (0, 0)),
            scratch_shapes=[
                pltpu.VMEM((2, blk, blk), jnp.float32),
                pltpu.VMEM((2, blk, blk), jnp.float32),
            ],
        ),
        compiler_params=pltpu.CompilerParams(vmem_limit_bytes=VMEM_LIMIT),
        cost_estimate=SMALL,
        name="left_grams",
    )(tile, after)


RAW = (1, 3)


def own_first(place):
    return place[0] * 2


def core_first(place):
    return (place[0] ^ 1) * 2


def later(k, place):
    return jnp.where(place[0] < 2, 4 + k, jnp.where(k < 2, 2 * k, 2 * k + 1))


def take_kernel(g_ref, out_ref, sems):
    rows, wide = out_ref.shape
    blk = wide // len(RAW)
    top = pl.multiple_of((1 - here()[1]) * rows, rows)
    copies = [
        pltpu.make_async_copy(
            g_ref.at[pl.ds(top, rows), pl.ds(block * blk, blk)], out_ref.at[:, pl.ds(k * blk, blk)], sems.at[k]
        )
        for k, block in enumerate(RAW)
    ]
    for copy in copies:
        copy.start()
    for copy in copies:
        copy.wait()


def take(tile, blk):
    return pl.pallas_call(
        take_kernel,
        out_shape=jax.ShapeDtypeStruct((tile.shape[0] // 2, len(RAW) * blk), jnp.float32),
        in_specs=[pl.BlockSpec(memory_space=pl.ANY)],
        out_specs=pl.BlockSpec(memory_space=pl.ANY),
        scratch_shapes=[pltpu.SemaphoreType.DMA((len(RAW),))],
        compiler_params=pltpu.CompilerParams(vmem_limit_bytes=VMEM_LIMIT),
        cost_estimate=SMALL,
        name="take",
    )(tile)


def fold_kernel(a_ref, b_ref, out_ref):
    out_ref[...] = a_ref[...] + b_ref[...]


def fold(kept, near):
    return pl.pallas_call(
        fold_kernel,
        out_shape=jax.ShapeDtypeStruct(kept.shape, jnp.float32),
        compiler_params=pltpu.CompilerParams(vmem_limit_bytes=VMEM_LIMIT),
        cost_estimate=SMALL,
        name="fold",
    )(kept, near)


def hold_kernel(a_ref, *rest):
    out_ref = rest[-1]
    out_ref[...] = a_ref[...]


def hold(value, *after):
    return pl.pallas_call(
        hold_kernel,
        out_shape=jax.ShapeDtypeStruct(value.shape, jnp.float32),
        in_specs=[pl.BlockSpec(memory_space=pltpu.VMEM)] + [pl.BlockSpec(memory_space=pl.ANY)] * len(after),
        compiler_params=pltpu.CompilerParams(vmem_limit_bytes=VMEM_LIMIT),
        cost_estimate=SMALL,
        name="hold",
    )(value, *after)


def pair_roots(full_dim, stats_ref, body, diag):
    blk = body.shape[0]
    rows, cols = places(blk)
    ident = jnp.where(rows == cols, 1.0, 0.0)
    moving, scales = [], []
    for b, gram in enumerate(unpack(body, diag)):
        factor = (
            beta_mix * stats_ref[b * blk : (b + 1) * blk, :]
            + (1.0 - beta_mix) * (gram / full_dim)
            + eps_shift * ident
        )
        scale = jnp.sqrt(jnp.sum(factor * factor, keepdims=True))
        moving.append(factor / scale)
        scales.append(scale)
    result = None
    for count in range(ITERS):
        steps = [(5.0 * ident - m) * 0.25 for m in moving]
        parts = [split(s) for s in steps]
        if result is None:
            result = steps
        else:
            result = [product(split(r), p) for r, p in zip(result, parts)]
        if count < ITERS - 1:
            squared = [split(product(p, p)) for p in parts]
            fourth = [split(product(s, s)) for s in squared]
            moving = [product(f, split(m)) for f, m in zip(fourth, moving)]
    return [r * jnp.exp(-0.25 * jnp.log(s)) for r, s in zip(result, scales)]


def right_kernel(full_dim, stats_ref, a_ref, b_ref, c_ref, g_ref, out_ref, half_ref):
    blk = stats_ref.shape[1]
    total = a_ref[...] + b_ref[...] + c_ref[...]
    roots = pair_roots(full_dim, stats_ref, total[:blk], total[blk : blk + 1])
    half_ref[...] = product(split(g_ref[...]), split(roots[0]))
    body, diag = pack(*roots)
    out_ref[:blk, :] = body
    out_ref[blk:, :] = diag


def right_roots(full_dim, stats, kept, near, far, tile):
    blk = stats.shape[1]
    tall = blk + PAD
    rows = tile.shape[0] // 2
    flat = pl.BlockSpec((tall, blk), lambda s: (0, 0))
    return pl.pallas_call(
        functools.partial(right_kernel, full_dim),
        out_shape=(
            jax.ShapeDtypeStruct((tall, blk), jnp.float32),
            jax.ShapeDtypeStruct((rows, blk), jnp.float32),
        ),
        grid_spec=pltpu.PrefetchScalarGridSpec(
            num_scalar_prefetch=0,
            grid=(1,),
            in_specs=[
                pl.BlockSpec((2 * blk, blk), placed(lambda s, place: (place[0], 0))),
                flat,
                flat,
                flat,
                pl.BlockSpec((rows, blk), placed(lambda s, place: (1 - place[1], own_first(place)))),
            ],
            out_specs=(
                flat,
                pl.BlockSpec((rows, blk), lambda s: (0, 0)),
            ),
        ),
        compiler_params=pltpu.CompilerParams(vmem_limit_bytes=VMEM_LIMIT),
        cost_estimate=SMALL,
        name="right_roots",
    )(stats, kept, near, far, tile)


def left_kernel(full_dim, stats_ref, a_ref, b_ref, out_ref):
    blk = stats_ref.shape[1]
    total = a_ref[...] + b_ref[b_ref.shape[0] - a_ref.shape[0] :, :]
    for b, root in enumerate(pair_roots(full_dim, stats_ref, total[:blk], total[blk : blk + 1])):
        high, low = split(root)
        out_ref[b, 0] = high
        out_ref[b, 1] = low


def left_roots(full_dim, stats, kept, came):
    blk = stats.shape[1]
    tall = blk + PAD
    return pl.pallas_call(
        functools.partial(left_kernel, full_dim),
        out_shape=jax.ShapeDtypeStruct((2, 2, blk, blk), jnp.bfloat16),
        grid_spec=pltpu.PrefetchScalarGridSpec(
            num_scalar_prefetch=0,
            grid=(1,),
            in_specs=[
                pl.BlockSpec((2 * blk, blk), placed(lambda s, place: (place[1], 0))),
                pl.BlockSpec((tall, blk), lambda s: (0, 0)),
                pl.BlockSpec(came.shape, lambda s: (0, 0)),
            ],
            out_specs=pl.BlockSpec((2, 2, blk, blk), lambda s: (0, 0, 0, 0)),
        ),
        compiler_params=pltpu.CompilerParams(vmem_limit_bytes=VMEM_LIMIT),
        cost_estimate=SMALL,
        name="left_roots",
    )(stats, kept, came)


def put_roots(out_ref, at, roots):
    for b, root in enumerate(roots):
        high, low = split(root)
        out_ref[at + b, 0] = high
        out_ref[at + b, 1] = low


def spread_kernel(own_ref, c_ref, x_ref, xc_ref, out_ref, cut_ref, seconds, body):
    blk = out_ref.shape[-1]
    r = here()[0]
    for flip, ref in enumerate((own_ref, c_ref, x_ref, xc_ref)):
        roots = unpack(ref[:blk, :], ref[blk : blk + 1, :])
        put_roots(out_ref, 2 * (r ^ flip), roots)
        seconds[r ^ flip] = roots[1]
    part = cut_ref.shape[0] - PAD
    body[...], diag = pack(seconds[RAW[0] // 2], seconds[RAW[1] // 2])
    cut_ref[:part, :] = body[pl.ds(pl.multiple_of(r * part, part), part), :]
    cut_ref[part:, :] = diag


def spread_roots(*packed):
    blk = packed[0].shape[1]
    count = len(packed)
    return pl.pallas_call(
        spread_kernel,
        out_shape=(
            jax.ShapeDtypeStruct((2 * count, 2, blk, blk), jnp.bfloat16),
            jax.ShapeDtypeStruct((blk // count + PAD, blk), jnp.float32),
        ),
        scratch_shapes=[pltpu.VMEM((count, blk, blk), jnp.float32), pltpu.VMEM((blk, blk), jnp.float32)],
        compiler_params=pltpu.CompilerParams(vmem_limit_bytes=VMEM_LIMIT),
        cost_estimate=SMALL,
        name="spread_roots",
    )(*packed)


def rest_kernel(a_ref, out_ref):
    out_ref[...] = a_ref[a_ref.shape[0] - out_ref.shape[0] :, :]


def rest_of(value, rows):
    return pl.pallas_call(
        rest_kernel,
        out_shape=jax.ShapeDtypeStruct((value.shape[0] - rows, value.shape[1]), jnp.float32),
        compiler_params=pltpu.CompilerParams(vmem_limit_bytes=VMEM_LIMIT),
        cost_estimate=SMALL,
        name="rest_of",
    )(value)


def join_kernel(own_ref, c_ref, x_ref, xc_ref, out_ref, body):
    part = own_ref.shape[0] - PAD
    r = here()[0]
    for flip, ref in enumerate((own_ref, c_ref, x_ref, xc_ref)):
        body[pl.ds(pl.multiple_of((r ^ flip) * part, part), part), :] = ref[:part, :]
    put_roots(out_ref, 0, unpack(body[...], own_ref[part : part + 1, :]))


def join_roots(*parts):
    blk = parts[0].shape[1]
    return pl.pallas_call(
        join_kernel,
        out_shape=jax.ShapeDtypeStruct((2, 2, blk, blk), jnp.bfloat16),
        scratch_shapes=[pltpu.VMEM((blk, blk), jnp.float32)],
        compiler_params=pltpu.CompilerParams(vmem_limit_bytes=VMEM_LIMIT),
        cost_estimate=SMALL,
        name="join_roots",
    )(*parts)


def core_apply_kernel(g_ref, packed_ref, under_ref, out_ref):
    rows, blk = g_ref.shape
    root = unpack(packed_ref[:blk, :], packed_ref[blk : blk + 1, :])[0]
    out_ref[:rows, :] = product(split(g_ref[...]), split(root))
    out_ref[rows:, :] = under_ref[...]


def core_apply(tile, packed, under):
    rows = tile.shape[0] // 2
    tall, blk = packed.shape
    return pl.pallas_call(
        core_apply_kernel,
        out_shape=jax.ShapeDtypeStruct((rows + tall, blk), jnp.float32),
        grid_spec=pltpu.PrefetchScalarGridSpec(
            num_scalar_prefetch=0,
            grid=(1,),
            in_specs=[
                pl.BlockSpec((rows, blk), placed(lambda s, place: (1 - place[1], core_first(place)))),
                pl.BlockSpec((tall, blk), lambda s: (0, 0)),
                pl.BlockSpec((tall, blk), lambda s: (0, 0)),
            ],
            out_specs=pl.BlockSpec((rows + tall, blk), lambda s: (0, 0)),
        ),
        compiler_params=pltpu.CompilerParams(vmem_limit_bytes=VMEM_LIMIT),
        cost_estimate=SMALL,
        name="core_apply",
    )(tile, packed, under)


def right_apply_kernel(pieces, carries, g_ref, right_ref, *rest):
    out_refs = rest[-len(pieces) :]
    value = product(split(g_ref[...]), (right_ref[0, 0], right_ref[0, 1]))
    for (top, rows, start, width), ref in zip(pieces, out_refs):
        ref[:rows, :] = value[top : top + rows, start : start + width]
    if carries:
        out_refs[0][value.shape[0] :, :] = rest[0][...]


def right_apply(tile, right, k, pieces, under, after):
    rows = tile.shape[0] // 2
    blk = right.shape[-1]
    pieces = pieces or ((0, rows, 0, blk),)
    in_specs = [
        pl.BlockSpec((rows, blk), placed(lambda s, place: (1 - place[1], later(k, place)))),
        pl.BlockSpec((1, 2, blk, blk), placed(lambda s, place: (later(k, place), 0, 0, 0))),
    ]
    operands = [tile, right]
    more = 0
    if under is not None:
        more = under.shape[0]
        in_specs.append(pl.BlockSpec(under.shape, lambda s: (0, 0)))
        operands.append(under)
    shapes = [(tall + more, width) for _, tall, _, width in pieces]
    return pl.pallas_call(
        functools.partial(right_apply_kernel, pieces, under is not None),
        out_shape=tuple(jax.ShapeDtypeStruct(shape, jnp.float32) for shape in shapes),
        grid_spec=pltpu.PrefetchScalarGridSpec(
            num_scalar_prefetch=0,
            grid=(1,),
            in_specs=in_specs + [pl.BlockSpec(memory_space=pl.ANY)] * len(after),
            out_specs=tuple(pl.BlockSpec(shape, lambda s: (0, 0)) for shape in shapes),
        ),
        compiler_params=pltpu.CompilerParams(vmem_limit_bytes=VMEM_LIMIT),
        cost_estimate=SMALL,
        name="right_apply",
    )(*operands, *after)


def left_product(left_ref, value, out_ref):
    blk = left_ref.shape[-1]
    for i in range(value.shape[0] // blk):
        part = split(value[i * blk : (i + 1) * blk])
        out_ref[i * blk : (i + 1) * blk, :] = product((left_ref[i, 0], left_ref[i, 1]), part)


def update_kernel(g_ref, left_ref, right_ref, *rest):
    half = product(split(g_ref[...]), (right_ref[0, 0], right_ref[0, 1]))
    left_product(left_ref, half, rest[-2])
    rest[-1][...] = jnp.zeros_like(rest[-1])


def finish_kernel(column, first, half_ref, left_ref, out_before, out_ref, stage, sems):
    blk = left_ref.shape[-1]
    width = stage.shape[1]
    cols = pl.ds(pl.multiple_of(column(here()), width), width)
    copies = []
    for i in range(stage.shape[0] // blk):
        rows = pl.ds(i * blk, blk)
        root = (left_ref[first + i, 0], left_ref[first + i, 1])
        stage[rows, :] = product(root, split(half_ref[rows, :]))
        copies.append(
            pltpu.make_async_copy(stage.at[rows, :], out_ref.at[pl.ds((first + i) * blk, blk), cols], sems.at[i])
        )
        copies[i].start()
    for copy in copies:
        copy.wait()


def finish(half, left, out, column, first=0, count=2):
    width = half.shape[1]
    blk = left.shape[-1]
    vmem = pl.BlockSpec(memory_space=pltpu.VMEM)
    anywhere = pl.BlockSpec(memory_space=pl.ANY)
    return pl.pallas_call(
        functools.partial(finish_kernel, column, first),
        out_shape=jax.ShapeDtypeStruct(out.shape, jnp.float32),
        in_specs=[vmem, vmem, anywhere],
        out_specs=anywhere,
        scratch_shapes=[pltpu.VMEM((count * blk, width), jnp.float32), pltpu.SemaphoreType.DMA((count,))],
        input_output_aliases={2: 0},
        compiler_params=pltpu.CompilerParams(vmem_limit_bytes=VMEM_LIMIT),
        cost_estimate=SMALL,
        name="finish",
    )(half, left, out)


def update(source, left, right, out, out_shape, g_map, out_map, after=()):
    rows = out_shape[0]
    blk = left.shape[-1]
    in_specs = [
        pl.BlockSpec((rows, blk), placed(g_map)),
        pl.BlockSpec((2, 2, blk, blk), lambda s: (0, 0, 0, 0)),
        pl.BlockSpec((1, 2, blk, blk), lambda s: (s, 0, 0, 0)),
    ]
    operands = [source, left, right]
    aliases = {}
    if out is not None:
        aliases = {len(operands): 0}
        in_specs.append(pl.BlockSpec(memory_space=pl.ANY))
        operands.append(out)
    in_specs += [pl.BlockSpec(memory_space=pl.ANY)] * len(after)
    return pl.pallas_call(
        update_kernel,
        out_shape=(jax.ShapeDtypeStruct(out_shape, jnp.float32), jax.ShapeDtypeStruct((8, 128), jnp.float32)),
        grid_spec=pltpu.PrefetchScalarGridSpec(
            num_scalar_prefetch=0,
            grid=(right.shape[0],),
            in_specs=in_specs,
            out_specs=(pl.BlockSpec((rows, blk), placed(out_map)), pl.BlockSpec((8, 128), lambda s: (0, 0))),
        ),
        input_output_aliases=aliases,
        compiler_params=pltpu.CompilerParams(vmem_limit_bytes=VMEM_LIMIT),
        cost_estimate=SMALL,
        name="update",
    )(*operands, *after)


def exchange_device(full_dim, n_row, grads, left_stats, right_stats):
    tile_rows, tile_cols = grads.shape[1:]
    blk = left_stats.shape[2]
    tile = pltpu.with_memory_space_constraint(grads.reshape(tile_rows, tile_cols), pltpu.HBM)
    lstats = left_stats.reshape(tile_rows, blk)
    rstats = right_stats.reshape(tile_cols, blk)
    rows = tile_rows // 2
    shape = (rows, 2 * tile_cols)
    halves = tile_cols // blk

    def over(axis, value):
        if axis == "y":
            return lax.ppermute(value, "col", [(0, 1), (1, 0)])
        flip = {"core": 1, "x": 2}[axis]
        return lax.ppermute(value, "row", [(i, i ^ flip) for i in range(n_row)])

    first = take(tile, blk)
    raw = over("y", first)

    send_on, keep_on = right_grams(tile, blk, (3, 2), first)
    far = fold(keep_on, over("core", send_on))
    send, keep = right_grams(tile, blk, (1, 0), far)
    near = over("core", send)
    far = over("x", far)

    own, half = right_roots(full_dim, rstats, keep, near, far, tile)
    came_a = over("y", half)
    lsend = left_grams(tile, blk, lambda place: 1 - place[1], half)
    own = hold(own, raw, lsend)
    own_c = over("core", own)
    own_x = over("x", own)
    half = core_apply(tile, own_c, lsend)
    came_b = over("y", half)
    own_x = hold(own_x, half, came_a)
    lkeep = left_grams(tile, blk, lambda place: place[1], half)
    roots, part = spread_roots(own, own_c, own_x, over("core", own_x))

    (half,) = right_apply(tile, roots, 0, None, part, (lkeep,))
    came_c = over("y", half)
    (half,) = right_apply(tile, roots, 1, None, None, (came_b,))
    came_d = over("y", half)

    def crossed(block, start=0):
        return lambda place: (1 - place[1]) * tile_cols + block(place) * blk + start

    left = left_roots(full_dim, lstats, lkeep, came_b)
    out, done = update(
        tile, left, roots, None, shape,
        lambda s, place: (place[1], s),
        lambda s, place: (0, place[1] * halves + s),
    )
    (half,) = right_apply(tile, roots, 2, None, None, (came_c, done))
    came_e = over("y", half)
    wide = blk // 2
    last = ((0, rows, 0, wide), (0, blk, wide, wide), (blk, blk, wide, wide))
    held = right_apply(tile, roots, 3, last, None, (came_d,))
    came_last = [over("y", half) for half in held]
    out = finish(came_a, left, out, crossed(own_first))
    out = finish(came_b, left, out, crossed(core_first))
    part = rest_of(came_c, rows)
    part_x = over("x", part)
    roots_raw = join_roots(part, over("core", part), part_x, over("core", part_x))
    out, done = update(
        raw, left, roots_raw, out, shape,
        lambda s, place: (0, s),
        lambda s, place: (0, (1 - place[1]) * halves + jnp.where(s == 0, RAW[0], RAW[1])),
        held[:1],
    )
    for k, value in enumerate((came_c, came_d, came_e)):
        out = finish(value, left, out, crossed(functools.partial(later, k)))
    for (top, tall, start, _), value in zip(last, came_last):
        out = finish(value, left, out, crossed(functools.partial(later, 3), start), top // blk, tall // blk)
    return out.reshape(1, rows, 2 * tile_cols)


def per_device(n_row, n_col, grads, left_stats, right_stats):
    mats, tile_rows, tile_cols = grads.shape
    blk = left_stats.shape[2]
    full_dim = tile_cols * n_col
    if mats == 1 and n_col == 2 and n_row == 4 and tile_rows == 4 * blk and tile_cols == 8 * blk:
        return exchange_device(full_dim, n_row, grads, left_stats, right_stats)
    return general_device(full_dim, grads, left_stats, right_stats)


def solution(mesh):
    return jax.shard_map(
        functools.partial(per_device, mesh.shape["row"], mesh.shape["col"]),
        mesh=mesh,
        in_specs=(P("mat", "row", "col"), P("mat", "row", None), P("mat", "col", None)),
        out_specs=P("mat", ("row", "col"), None),
        check_vma=False,
    )
```

```python
import functools

import jax
import jax.numpy as jnp
from jax import lax
from jax.experimental import pallas as pl
from jax.experimental.pallas import tpu as pltpu
from jax.sharding import PartitionSpec as P

ITERS = 3
beta_mix = 0.5
eps_shift = 0.001
PAD = 8
VMEM_LIMIT = 24 * 1024 * 1024
SMALL = pl.CostEstimate(flops=1, bytes_accessed=1, transcendentals=0)


def matmul(left, right):
    return jnp.einsum("...ij,...jk->...ik", left, right, precision=lax.Precision.HIGHEST)


def newton_root(factor):
    size = factor.shape[-1]
    ident = jnp.eye(size, dtype=jnp.float32)
    scale = jnp.sqrt(jnp.sum(factor * factor, axis=(-2, -1), keepdims=True))
    moving = factor / scale
    result = jnp.broadcast_to(ident, factor.shape)
    for count in range(ITERS):
        step_mat = (5.0 * ident - moving) * 0.25
        result = matmul(result, step_mat)
        squared = matmul(step_mat, step_mat)
        moving = matmul(matmul(squared, squared), moving)
    return result * jnp.power(scale, -0.25)


def general_device(full_dim, grads, left_stats, right_stats):
    mats, tile_rows, tile_cols = grads.shape
    blk = left_stats.shape[2]
    row_blocks = tile_rows // blk
    col_blocks = tile_cols // blk
    ident = jnp.eye(blk, dtype=jnp.float32)
    by_rows = grads.reshape(mats, row_blocks, blk, tile_cols)
    left_part = jnp.einsum("mibd,mied->mibe", by_rows, by_rows, precision=lax.Precision.HIGHEST) / full_dim
    by_cols = grads.reshape(mats, tile_rows, col_blocks, blk)
    right_part = (
        jnp.einsum("mdjb,mdje->mjbe", by_cols, by_cols, precision=lax.Precision.HIGHEST) / full_dim
    )
    left_gram = lax.psum(left_part, "col")
    right_gram = lax.psum(right_part, "row")
    left_factor = (
        beta_mix * left_stats.reshape(mats, row_blocks, blk, blk)
        + (1.0 - beta_mix) * left_gram
        + eps_shift * ident
    )
    right_factor = (
        beta_mix * right_stats.reshape(mats, col_blocks, blk, blk)
        + (1.0 - beta_mix) * right_gram
        + eps_shift * ident
    )
    left_root = newton_root(left_factor)
    right_root = newton_root(right_factor)
    half = jnp.einsum("mibe,mied->mibd", left_root, by_rows, precision=lax.Precision.HIGHEST)
    half = half.reshape(mats, tile_rows, col_blocks, blk)
    full = jnp.einsum("mdjb,mjbe->mdje", half, right_root, precision=lax.Precision.HIGHEST)
    full = full.reshape(mats, tile_rows, tile_cols)
    return lax.all_to_all(full, "col", split_axis=1, concat_axis=2, tiled=True)


def here():
    return lax.axis_index("row"), lax.axis_index("col")


def placed(index_map):
    return lambda s: index_map(s, here())


def split(value):
    high = value.astype(jnp.bfloat16)
    low = (value - high.astype(jnp.float32)).astype(jnp.bfloat16)
    return high, low


def dot(left, right, dims=((1,), (0,))):
    return lax.dot_general(left, right, (dims, ((), ())), preferred_element_type=jnp.float32)


def product(left, right):
    lh, ll = left
    rh, rl = right
    return dot(lh, rh) + (dot(lh, rl) + dot(ll, rh))


def places(blk):
    rows = lax.broadcasted_iota(jnp.int32, (blk, blk), 0)
    cols = lax.broadcasted_iota(jnp.int32, (blk, blk), 1)
    return rows, cols


def pack(first, second):
    blk = first.shape[0]
    rows, cols = places(blk)
    body = jnp.where(rows <= cols, first, second)
    diag = jnp.sum(jnp.where(rows == cols, second, 0.0), axis=0, keepdims=True)
    return body, jnp.broadcast_to(diag, (PAD, blk))


def unpack(body, diag):
    blk = body.shape[0]
    rows, cols = places(blk)
    turned = body.T
    first = jnp.where(rows <= cols, body, turned)
    second = jnp.where(rows > cols, body, jnp.where(rows == cols, diag, turned))
    return first, second


def right_gram_kernel(g_ref, *rest):
    out_refs = rest[-2:]
    step = pl.program_id(0)
    blk = g_ref.shape[1] // 2
    high, low = split(g_ref[...])
    grams = []
    for b in range(2):
        hb = high[:, b * blk : (b + 1) * blk]
        lb = low[:, b * blk : (b + 1) * blk]
        both = dot(hb, hb, ((0,), (0,)))
        cross = dot(hb, lb, ((0,), (0,)))
        grams.append(both + (cross + cross.T))
    body, diag = pack(*grams)

    for at, ref in enumerate(out_refs):

        @pl.when(step == at)
        def _():
            ref[:blk, :] = body
            ref[blk:, :] = diag


def right_grams(tile, blk, flips, *after):
    rows = tile.shape[0]
    tall = blk + PAD
    flip = lambda s: jnp.where(s == 0, flips[0], flips[1])
    return pl.pallas_call(
        right_gram_kernel,
        out_shape=(jax.ShapeDtypeStruct((tall, blk), jnp.float32),) * 2,
        grid_spec=pltpu.PrefetchScalarGridSpec(
            num_scalar_prefetch=0,
            grid=(2,),
            in_specs=[
                pl.BlockSpec((rows, 2 * blk), placed(lambda s, place: (0, place[0] ^ flip(s)))),
            ]
            + [pl.BlockSpec(memory_space=pl.ANY)] * len(after),
            out_specs=(pl.BlockSpec((tall, blk), lambda s: (0, 0)),) * 2,
        ),
        compiler_params=pltpu.CompilerParams(vmem_limit_bytes=VMEM_LIMIT),
        cost_estimate=SMALL,
        name="right_grams",
    )(tile, *after)


def left_gram_kernel(g_ref, after_ref, out_ref, lhh, lcross):
    step = pl.program_id(0)
    last = pl.num_programs(0) - 1
    blk = lhh.shape[-1]
    high, low = split(g_ref[...])
    for i in range(2):
        hi = high[i * blk : (i + 1) * blk, :]
        lo = low[i * blk : (i + 1) * blk, :]
        both = dot(hi, hi, ((1,), (1,)))
        cross = dot(lo, hi, ((1,), (1,)))

        @pl.when(step == 0)
        def _():
            lhh[i] = both
            lcross[i] = cross

        @pl.when(step > 0)
        def _():
            lhh[i] += both
            lcross[i] += cross

    @pl.when(step == last)
    def _():
        body, diag = pack(*(lhh[b] + (lcross[b] + lcross[b].T) for b in range(2)))
        out_ref[:blk, :] = body
        out_ref[blk:, :] = diag


def left_grams(tile, blk, at, after):
    width = tile.shape[1]
    tall = blk + PAD
    return pl.pallas_call(
        left_gram_kernel,
        out_shape=jax.ShapeDtypeStruct((tall, blk), jnp.float32),
        grid_spec=pltpu.PrefetchScalarGridSpec(
            num_scalar_prefetch=0,
            grid=(width // (4 * blk),),
            in_specs=[
                pl.BlockSpec((2 * blk, 4 * blk), placed(lambda s, place: (at(place), s))),
                pl.BlockSpec(memory_space=pl.ANY),
            ],
            out_specs=pl.BlockSpec((tall, blk), lambda s: (0, 0)),
            scratch_shapes=[
                pltpu.VMEM((2, blk, blk), jnp.float32),
                pltpu.VMEM((2, blk, blk), jnp.float32),
            ],
        ),
        compiler_params=pltpu.CompilerParams(vmem_limit_bytes=VMEM_LIMIT),
        cost_estimate=SMALL,
        name="left_grams",
    )(tile, after)


RAW = (1, 3)


def own_first(place):
    return place[0] * 2


def core_first(place):
    return (place[0] ^ 1) * 2


def later(k, place):
    return jnp.where(place[0] < 2, 4 + k, jnp.where(k < 2, 2 * k, 2 * k + 1))


def take_kernel(block, g_ref, *rest):
    out_ref, sem = rest[-2:]
    rows, blk = out_ref.shape
    top = pl.multiple_of((1 - here()[1]) * rows, rows)
    copy = pltpu.make_async_copy(g_ref.at[pl.ds(top, rows), pl.ds(block * blk, blk)], out_ref, sem)
    copy.start()
    copy.wait()


def take(tile, blk, block, *after):
    anywhere = pl.BlockSpec(memory_space=pl.ANY)
    return pl.pallas_call(
        functools.partial(take_kernel, block),
        out_shape=jax.ShapeDtypeStruct((tile.shape[0] // 2, blk), jnp.float32),
        in_specs=[anywhere] * (1 + len(after)),
        out_specs=anywhere,
        scratch_shapes=[pltpu.SemaphoreType.DMA],
        compiler_params=pltpu.CompilerParams(vmem_limit_bytes=VMEM_LIMIT),
        cost_estimate=SMALL,
        name="take",
    )(tile, *after)


def fold_kernel(a_ref, b_ref, out_ref):
    out_ref[...] = a_ref[...] + b_ref[...]


def fold(kept, near):
    return pl.pallas_call(
        fold_kernel,
        out_shape=jax.ShapeDtypeStruct(kept.shape, jnp.float32),
        compiler_params=pltpu.CompilerParams(vmem_limit_bytes=VMEM_LIMIT),
        cost_estimate=SMALL,
        name="fold",
    )(kept, near)


def hold_kernel(a_ref, *rest):
    out_ref = rest[-1]
    out_ref[...] = a_ref[...]


def hold(value, *after):
    return pl.pallas_call(
        hold_kernel,
        out_shape=jax.ShapeDtypeStruct(value.shape, jnp.float32),
        in_specs=[pl.BlockSpec(memory_space=pltpu.VMEM)] + [pl.BlockSpec(memory_space=pl.ANY)] * len(after),
        compiler_params=pltpu.CompilerParams(vmem_limit_bytes=VMEM_LIMIT),
        cost_estimate=SMALL,
        name="hold",
    )(value, *after)


def pair_roots(full_dim, stats_ref, body, diag):
    blk = body.shape[0]
    rows, cols = places(blk)
    ident = jnp.where(rows == cols, 1.0, 0.0)
    moving, scales = [], []
    for b, gram in enumerate(unpack(body, diag)):
        factor = (
            beta_mix * stats_ref[b * blk : (b + 1) * blk, :]
            + (1.0 - beta_mix) * (gram / full_dim)
            + eps_shift * ident
        )
        scale = jnp.sqrt(jnp.sum(factor * factor, keepdims=True))
        moving.append(factor / scale)
        scales.append(scale)
    result = None
    for count in range(ITERS):
        steps = [(5.0 * ident - m) * 0.25 for m in moving]
        parts = [split(s) for s in steps]
        if result is None:
            result = steps
        else:
            result = [product(split(r), p) for r, p in zip(result, parts)]
        if count < ITERS - 1:
            squared = [split(product(p, p)) for p in parts]
            fourth = [split(product(s, s)) for s in squared]
            moving = [product(f, split(m)) for f, m in zip(fourth, moving)]
    return [r * jnp.exp(-0.25 * jnp.log(s)) for r, s in zip(result, scales)]


def right_kernel(full_dim, stats_ref, a_ref, b_ref, c_ref, g_ref, out_ref, half_ref):
    blk = stats_ref.shape[1]
    total = a_ref[...] + b_ref[...] + c_ref[...]
    roots = pair_roots(full_dim, stats_ref, total[:blk], total[blk : blk + 1])
    half_ref[...] = product(split(g_ref[...]), split(roots[0]))
    body, diag = pack(*roots)
    out_ref[:blk, :] = body
    out_ref[blk:, :] = diag


def right_roots(full_dim, stats, kept, near, far, tile):
    blk = stats.shape[1]
    tall = blk + PAD
    rows = tile.shape[0] // 2
    flat = pl.BlockSpec((tall, blk), lambda s: (0, 0))
    return pl.pallas_call(
        functools.partial(right_kernel, full_dim),
        out_shape=(
            jax.ShapeDtypeStruct((tall, blk), jnp.float32),
            jax.ShapeDtypeStruct((rows, blk), jnp.float32),
        ),
        grid_spec=pltpu.PrefetchScalarGridSpec(
            num_scalar_prefetch=0,
            grid=(1,),
            in_specs=[
                pl.BlockSpec((2 * blk, blk), placed(lambda s, place: (place[0], 0))),
                flat,
                flat,
                flat,
                pl.BlockSpec((rows, blk), placed(lambda s, place: (1 - place[1], own_first(place)))),
            ],
            out_specs=(
                flat,
                pl.BlockSpec((rows, blk), lambda s: (0, 0)),
            ),
        ),
        compiler_params=pltpu.CompilerParams(vmem_limit_bytes=VMEM_LIMIT),
        cost_estimate=SMALL,
        name="right_roots",
    )(stats, kept, near, far, tile)


def left_kernel(full_dim, stats_ref, a_ref, b_ref, out_ref):
    blk = stats_ref.shape[1]
    total = a_ref[...] + b_ref[b_ref.shape[0] - a_ref.shape[0] :, :]
    for b, root in enumerate(pair_roots(full_dim, stats_ref, total[:blk], total[blk : blk + 1])):
        high, low = split(root)
        out_ref[b, 0] = high
        out_ref[b, 1] = low


def left_roots(full_dim, stats, kept, came):
    blk = stats.shape[1]
    tall = blk + PAD
    return pl.pallas_call(
        functools.partial(left_kernel, full_dim),
        out_shape=jax.ShapeDtypeStruct((2, 2, blk, blk), jnp.bfloat16),
        grid_spec=pltpu.PrefetchScalarGridSpec(
            num_scalar_prefetch=0,
            grid=(1,),
            in_specs=[
                pl.BlockSpec((2 * blk, blk), placed(lambda s, place: (place[1], 0))),
                pl.BlockSpec((tall, blk), lambda s: (0, 0)),
                pl.BlockSpec(came.shape, lambda s: (0, 0)),
            ],
            out_specs=pl.BlockSpec((2, 2, blk, blk), lambda s: (0, 0, 0, 0)),
        ),
        compiler_params=pltpu.CompilerParams(vmem_limit_bytes=VMEM_LIMIT),
        cost_estimate=SMALL,
        name="left_roots",
    )(stats, kept, came)


def put_roots(out_ref, at, roots):
    for b, root in enumerate(roots):
        high, low = split(root)
        out_ref[at + b, 0] = high
        out_ref[at + b, 1] = low


def spread_kernel(own_ref, c_ref, x_ref, xc_ref, out_ref, cut_ref, seconds, body):
    blk = out_ref.shape[-1]
    r = here()[0]
    for flip, ref in enumerate((own_ref, c_ref, x_ref, xc_ref)):
        roots = unpack(ref[:blk, :], ref[blk : blk + 1, :])
        put_roots(out_ref, 2 * (r ^ flip), roots)
        seconds[r ^ flip] = roots[1]
    part = cut_ref.shape[0] - PAD
    body[...], diag = pack(seconds[RAW[0] // 2], seconds[RAW[1] // 2])
    cut_ref[:part, :] = body[pl.ds(pl.multiple_of(r * part, part), part), :]
    cut_ref[part:, :] = diag


def spread_roots(*packed):
    blk = packed[0].shape[1]
    count = len(packed)
    return pl.pallas_call(
        spread_kernel,
        out_shape=(
            jax.ShapeDtypeStruct((2 * count, 2, blk, blk), jnp.bfloat16),
            jax.ShapeDtypeStruct((blk // count + PAD, blk), jnp.float32),
        ),
        scratch_shapes=[pltpu.VMEM((count, blk, blk), jnp.float32), pltpu.VMEM((blk, blk), jnp.float32)],
        compiler_params=pltpu.CompilerParams(vmem_limit_bytes=VMEM_LIMIT),
        cost_estimate=SMALL,
        name="spread_roots",
    )(*packed)


def rest_kernel(a_ref, out_ref):
    out_ref[...] = a_ref[a_ref.shape[0] - out_ref.shape[0] :, :]


def rest_of(value, rows):
    return pl.pallas_call(
        rest_kernel,
        out_shape=jax.ShapeDtypeStruct((value.shape[0] - rows, value.shape[1]), jnp.float32),
        compiler_params=pltpu.CompilerParams(vmem_limit_bytes=VMEM_LIMIT),
        cost_estimate=SMALL,
        name="rest_of",
    )(value)


def join_kernel(own_ref, c_ref, x_ref, xc_ref, out_ref, body):
    part = own_ref.shape[0] - PAD
    r = here()[0]
    for flip, ref in enumerate((own_ref, c_ref, x_ref, xc_ref)):
        body[pl.ds(pl.multiple_of((r ^ flip) * part, part), part), :] = ref[:part, :]
    put_roots(out_ref, 0, unpack(body[...], own_ref[part : part + 1, :]))


def join_roots(*parts):
    blk = parts[0].shape[1]
    return pl.pallas_call(
        join_kernel,
        out_shape=jax.ShapeDtypeStruct((2, 2, blk, blk), jnp.bfloat16),
        scratch_shapes=[pltpu.VMEM((blk, blk), jnp.float32)],
        compiler_params=pltpu.CompilerParams(vmem_limit_bytes=VMEM_LIMIT),
        cost_estimate=SMALL,
        name="join_roots",
    )(*parts)


def core_apply_kernel(g_ref, packed_ref, under_ref, out_ref):
    rows, blk = g_ref.shape
    root = unpack(packed_ref[:blk, :], packed_ref[blk : blk + 1, :])[0]
    out_ref[:rows, :] = product(split(g_ref[...]), split(root))
    out_ref[rows:, :] = under_ref[...]


def core_apply(tile, packed, under):
    rows = tile.shape[0] // 2
    tall, blk = packed.shape
    return pl.pallas_call(
        core_apply_kernel,
        out_shape=jax.ShapeDtypeStruct((rows + tall, blk), jnp.float32),
        grid_spec=pltpu.PrefetchScalarGridSpec(
            num_scalar_prefetch=0,
            grid=(1,),
            in_specs=[
                pl.BlockSpec((rows, blk), placed(lambda s, place: (1 - place[1], core_first(place)))),
                pl.BlockSpec((tall, blk), lambda s: (0, 0)),
                pl.BlockSpec((tall, blk), lambda s: (0, 0)),
            ],
            out_specs=pl.BlockSpec((rows + tall, blk), lambda s: (0, 0)),
        ),
        compiler_params=pltpu.CompilerParams(vmem_limit_bytes=VMEM_LIMIT),
        cost_estimate=SMALL,
        name="core_apply",
    )(tile, packed, under)


def right_apply_kernel(pieces, carries, g_ref, right_ref, *rest):
    out_refs = rest[-len(pieces) :]
    value = product(split(g_ref[...]), (right_ref[0, 0], right_ref[0, 1]))
    for (top, rows, start, width), ref in zip(pieces, out_refs):
        ref[:rows, :] = value[top : top + rows, start : start + width]
    if carries:
        out_refs[0][value.shape[0] :, :] = rest[0][...]


def right_apply(tile, right, k, pieces, under, after):
    rows = tile.shape[0] // 2
    blk = right.shape[-1]
    pieces = pieces or ((0, rows, 0, blk),)
    in_specs = [
        pl.BlockSpec((rows, blk), placed(lambda s, place: (1 - place[1], later(k, place)))),
        pl.BlockSpec((1, 2, blk, blk), placed(lambda s, place: (later(k, place), 0, 0, 0))),
    ]
    operands = [tile, right]
    more = 0
    if under is not None:
        more = under.shape[0]
        in_specs.append(pl.BlockSpec(under.shape, lambda s: (0, 0)))
        operands.append(under)
    shapes = [(tall + more, width) for _, tall, _, width in pieces]
    return pl.pallas_call(
        functools.partial(right_apply_kernel, pieces, under is not None),
        out_shape=tuple(jax.ShapeDtypeStruct(shape, jnp.float32) for shape in shapes),
        grid_spec=pltpu.PrefetchScalarGridSpec(
            num_scalar_prefetch=0,
            grid=(1,),
            in_specs=in_specs + [pl.BlockSpec(memory_space=pl.ANY)] * len(after),
            out_specs=tuple(pl.BlockSpec(shape, lambda s: (0, 0)) for shape in shapes),
        ),
        compiler_params=pltpu.CompilerParams(vmem_limit_bytes=VMEM_LIMIT),
        cost_estimate=SMALL,
        name="right_apply",
    )(*operands, *after)


def left_product(left_ref, value, out_ref):
    blk = left_ref.shape[-1]
    for i in range(value.shape[0] // blk):
        part = split(value[i * blk : (i + 1) * blk])
        out_ref[i * blk : (i + 1) * blk, :] = product((left_ref[i, 0], left_ref[i, 1]), part)


def update_kernel(g_ref, left_ref, right_ref, *rest):
    half = product(split(g_ref[...]), (right_ref[0, 0], right_ref[0, 1]))
    left_product(left_ref, half, rest[-2])
    rest[-1][...] = jnp.zeros_like(rest[-1])


def finish_kernel(column, first, half_ref, left_ref, out_before, out_ref, stage, sems):
    blk = left_ref.shape[-1]
    width = stage.shape[1]
    cols = pl.ds(pl.multiple_of(column(here()), width), width)
    copies = []
    for i in range(stage.shape[0] // blk):
        rows = pl.ds(i * blk, blk)
        root = (left_ref[first + i, 0], left_ref[first + i, 1])
        stage[rows, :] = product(root, split(half_ref[rows, :]))
        copies.append(
            pltpu.make_async_copy(stage.at[rows, :], out_ref.at[pl.ds((first + i) * blk, blk), cols], sems.at[i])
        )
        copies[i].start()
    for copy in copies:
        copy.wait()


def finish(half, left, out, column, first=0, count=2):
    width = half.shape[1]
    blk = left.shape[-1]
    vmem = pl.BlockSpec(memory_space=pltpu.VMEM)
    anywhere = pl.BlockSpec(memory_space=pl.ANY)
    return pl.pallas_call(
        functools.partial(finish_kernel, column, first),
        out_shape=jax.ShapeDtypeStruct(out.shape, jnp.float32),
        in_specs=[vmem, vmem, anywhere],
        out_specs=anywhere,
        scratch_shapes=[pltpu.VMEM((count * blk, width), jnp.float32), pltpu.SemaphoreType.DMA((count,))],
        input_output_aliases={2: 0},
        compiler_params=pltpu.CompilerParams(vmem_limit_bytes=VMEM_LIMIT),
        cost_estimate=SMALL,
        name="finish",
    )(half, left, out)


def update(source, left, right, out, out_shape, g_map, out_map, first=0, count=None, after=()):
    rows = out_shape[0]
    blk = left.shape[-1]
    in_specs = [
        pl.BlockSpec((rows, blk), placed(g_map)),
        pl.BlockSpec((2, 2, blk, blk), lambda s: (0, 0, 0, 0)),
        pl.BlockSpec((1, 2, blk, blk), lambda s: (first + s, 0, 0, 0)),
    ]
    operands = [source, left, right]
    aliases = {}
    if out is not None:
        aliases = {len(operands): 0}
        in_specs.append(pl.BlockSpec(memory_space=pl.ANY))
        operands.append(out)
    in_specs += [pl.BlockSpec(memory_space=pl.ANY)] * len(after)
    return pl.pallas_call(
        update_kernel,
        out_shape=(jax.ShapeDtypeStruct(out_shape, jnp.float32), jax.ShapeDtypeStruct((8, 128), jnp.float32)),
        grid_spec=pltpu.PrefetchScalarGridSpec(
            num_scalar_prefetch=0,
            grid=(count or right.shape[0],),
            in_specs=in_specs,
            out_specs=(pl.BlockSpec((rows, blk), placed(out_map)), pl.BlockSpec((8, 128), lambda s: (0, 0))),
        ),
        input_output_aliases=aliases,
        compiler_params=pltpu.CompilerParams(vmem_limit_bytes=VMEM_LIMIT),
        cost_estimate=SMALL,
        name="update",
    )(*operands, *after)


def exchange_device(full_dim, n_row, grads, left_stats, right_stats):
    tile_rows, tile_cols = grads.shape[1:]
    blk = left_stats.shape[2]
    tile = grads.reshape(tile_rows, tile_cols)
    lstats = left_stats.reshape(tile_rows, blk)
    rstats = right_stats.reshape(tile_cols, blk)
    rows = tile_rows // 2
    shape = (rows, 2 * tile_cols)
    halves = tile_cols // blk

    def over(axis, value):
        if axis == "y":
            return lax.ppermute(value, "col", [(0, 1), (1, 0)])
        flip = {"core": 1, "x": 2}[axis]
        return lax.ppermute(value, "row", [(i, i ^ flip) for i in range(n_row)])

    first = take(pltpu.with_memory_space_constraint(tile, pltpu.HBM), blk, RAW[0])
    raw = [over("y", first)]

    send_on, keep_on = right_grams(tile, blk, (3, 2), first)
    far = fold(keep_on, over("core", send_on))
    raw.append(over("y", take(tile, blk, RAW[1], send_on)))
    send, keep = right_grams(tile, blk, (1, 0), far, raw[0])
    near = over("core", send)
    far = over("x", far)

    own, half = right_roots(full_dim, rstats, keep, near, far, tile)
    came_a = over("y", half)
    lsend = left_grams(tile, blk, lambda place: 1 - place[1], half)
    own = hold(own, raw[1], lsend)
    own_c = over("core", own)
    own_x = over("x", own)
    half = core_apply(tile, own_c, lsend)
    came_b = over("y", half)
    own_x = hold(own_x, half, came_a)
    lkeep = left_grams(tile, blk, lambda place: place[1], half)
    roots, part = spread_roots(own, own_c, own_x, over("core", own_x))

    (half,) = right_apply(tile, roots, 0, None, part, (lkeep,))
    came_c = over("y", half)
    (half,) = right_apply(tile, roots, 1, None, None, (came_b,))
    came_d = over("y", half)

    def crossed(block, start=0):
        return lambda place: (1 - place[1]) * tile_cols + block(place) * blk + start

    left = left_roots(full_dim, lstats, lkeep, came_b)
    out, done = update(
        tile, left, roots, None, shape,
        lambda s, place: (place[1], s),
        lambda s, place: (0, place[1] * halves + s),
    )
    (half,) = right_apply(tile, roots, 2, None, None, (came_c, done))
    came_e = over("y", half)
    wide = blk // 2
    last = ((0, rows, 0, wide), (0, blk, wide, wide), (blk, blk, wide, wide))
    held = right_apply(tile, roots, 3, last, None, (came_d,))
    came_last = [over("y", half) for half in held]
    out = finish(came_a, left, out, crossed(own_first))
    out = finish(came_b, left, out, crossed(core_first))
    part = rest_of(came_c, rows)
    part_x = over("x", part)
    roots_raw = join_roots(part, over("core", part), part_x, over("core", part_x))
    for k, (block, value) in enumerate(zip(RAW, raw)):
        out, done = update(
            value, left, roots_raw, out, shape,
            lambda s, place: (0, 0),
            lambda s, place, block=block: (0, (1 - place[1]) * halves + block),
            k, 1, held[:1],
        )
    for k, value in enumerate((came_c, came_d, came_e)):
        out = finish(value, left, out, crossed(functools.partial(later, k)))
    for (top, tall, start, _), value in zip(last, came_last):
        out = finish(value, left, out, crossed(functools.partial(later, 3), start), top // blk, tall // blk)
    return out.reshape(1, rows, 2 * tile_cols)


def per_device(n_row, n_col, grads, left_stats, right_stats):
    mats, tile_rows, tile_cols = grads.shape
    blk = left_stats.shape[2]
    full_dim = tile_cols * n_col
    if mats == 1 and n_col == 2 and n_row == 4 and tile_rows == 4 * blk and tile_cols == 8 * blk:
        return exchange_device(full_dim, n_row, grads, left_stats, right_stats)
    return general_device(full_dim, grads, left_stats, right_stats)


def solution(mesh):
    return jax.shard_map(
        functools.partial(per_device, mesh.shape["row"], mesh.shape["col"]),
        mesh=mesh,
        in_specs=(P("mat", "row", "col"), P("mat", "row", None), P("mat", "col", None)),
        out_specs=P("mat", ("row", "col"), None),
        check_vma=False,
    )
```

```python
import functools

import jax
import jax.numpy as jnp
from jax import lax
from jax.experimental import pallas as pl
from jax.experimental.pallas import tpu as pltpu
from jax.sharding import PartitionSpec as P

ITERS = 3
beta_mix = 0.5
eps_shift = 0.001
PAD = 8
VMEM_LIMIT = 24 * 1024 * 1024
SMALL = pl.CostEstimate(flops=1, bytes_accessed=1, transcendentals=0)


def matmul(left, right):
    return jnp.einsum("...ij,...jk->...ik", left, right, precision=lax.Precision.HIGHEST)


def newton_root(factor):
    size = factor.shape[-1]
    ident = jnp.eye(size, dtype=jnp.float32)
    scale = jnp.sqrt(jnp.sum(factor * factor, axis=(-2, -1), keepdims=True))
    moving = factor / scale
    result = jnp.broadcast_to(ident, factor.shape)
    for count in range(ITERS):
        step_mat = (5.0 * ident - moving) * 0.25
        result = matmul(result, step_mat)
        squared = matmul(step_mat, step_mat)
        moving = matmul(matmul(squared, squared), moving)
    return result * jnp.power(scale, -0.25)


def general_device(full_dim, grads, left_stats, right_stats):
    mats, tile_rows, tile_cols = grads.shape
    blk = left_stats.shape[2]
    row_blocks = tile_rows // blk
    col_blocks = tile_cols // blk
    ident = jnp.eye(blk, dtype=jnp.float32)
    by_rows = grads.reshape(mats, row_blocks, blk, tile_cols)
    left_part = jnp.einsum("mibd,mied->mibe", by_rows, by_rows, precision=lax.Precision.HIGHEST) / full_dim
    by_cols = grads.reshape(mats, tile_rows, col_blocks, blk)
    right_part = (
        jnp.einsum("mdjb,mdje->mjbe", by_cols, by_cols, precision=lax.Precision.HIGHEST) / full_dim
    )
    left_gram = lax.psum(left_part, "col")
    right_gram = lax.psum(right_part, "row")
    left_factor = (
        beta_mix * left_stats.reshape(mats, row_blocks, blk, blk)
        + (1.0 - beta_mix) * left_gram
        + eps_shift * ident
    )
    right_factor = (
        beta_mix * right_stats.reshape(mats, col_blocks, blk, blk)
        + (1.0 - beta_mix) * right_gram
        + eps_shift * ident
    )
    left_root = newton_root(left_factor)
    right_root = newton_root(right_factor)
    half = jnp.einsum("mibe,mied->mibd", left_root, by_rows, precision=lax.Precision.HIGHEST)
    half = half.reshape(mats, tile_rows, col_blocks, blk)
    full = jnp.einsum("mdjb,mjbe->mdje", half, right_root, precision=lax.Precision.HIGHEST)
    full = full.reshape(mats, tile_rows, tile_cols)
    return lax.all_to_all(full, "col", split_axis=1, concat_axis=2, tiled=True)


def here():
    return lax.axis_index("row"), lax.axis_index("col")


def placed(index_map):
    return lambda s: index_map(s, here())


def split(value):
    high = value.astype(jnp.bfloat16)
    low = (value - high.astype(jnp.float32)).astype(jnp.bfloat16)
    return high, low


def dot(left, right, dims=((1,), (0,))):
    return lax.dot_general(left, right, (dims, ((), ())), preferred_element_type=jnp.float32)


def product(left, right):
    lh, ll = left
    rh, rl = right
    return dot(lh, rh) + (dot(lh, rl) + dot(ll, rh))


def places(blk):
    rows = lax.broadcasted_iota(jnp.int32, (blk, blk), 0)
    cols = lax.broadcasted_iota(jnp.int32, (blk, blk), 1)
    return rows, cols


def pack(first, second):
    blk = first.shape[0]
    rows, cols = places(blk)
    body = jnp.where(rows <= cols, first, second)
    diag = jnp.sum(jnp.where(rows == cols, second, 0.0), axis=0, keepdims=True)
    return body, jnp.broadcast_to(diag, (PAD, blk))


def unpack(body, diag):
    blk = body.shape[0]
    rows, cols = places(blk)
    turned = body.T
    first = jnp.where(rows <= cols, body, turned)
    second = jnp.where(rows > cols, body, jnp.where(rows == cols, diag, turned))
    return first, second


def put_packed(refs, body, diag):
    at = 0
    for ref in refs:
        rows = min(ref.shape[0], body.shape[0] - at)
        ref[:rows, :] = body[at : at + rows, :]
        at += rows
    refs[-1][refs[-1].shape[0] - PAD :, :] = diag


def right_gram_kernel(parts, g_ref, *rest):
    step = pl.program_id(0)
    out_refs = rest[-1 - parts :]
    blk = g_ref.shape[1] // 2
    high, low = split(g_ref[...])
    grams = []
    for b in range(2):
        hb = high[:, b * blk : (b + 1) * blk]
        lb = low[:, b * blk : (b + 1) * blk]
        both = dot(hb, hb, ((0,), (0,)))
        cross = dot(hb, lb, ((0,), (0,)))
        grams.append(both + (cross + cross.T))
    body, diag = pack(*grams)
    for at, refs in enumerate((out_refs[:parts], out_refs[parts:])):

        @pl.when(step == at)
        def _():
            put_packed(refs, body, diag)


def right_grams(tile, blk, flips, parts, *after):
    rows = tile.shape[0]
    tall = blk + PAD
    flip = lambda s: jnp.where(s == 0, flips[0], flips[1])
    sizes = ((tall + PAD) // 2, (tall - PAD) // 2) if parts == 2 else (tall,)
    sizes += (tall,)
    return pl.pallas_call(
        functools.partial(right_gram_kernel, parts),
        out_shape=tuple(jax.ShapeDtypeStruct((size, blk), jnp.float32) for size in sizes),
        grid_spec=pltpu.PrefetchScalarGridSpec(
            num_scalar_prefetch=0,
            grid=(2,),
            in_specs=[pl.BlockSpec((rows, 2 * blk), placed(lambda s, place: (0, place[0] ^ flip(s))))]
            + [pl.BlockSpec(memory_space=pl.ANY)] * len(after),
            out_specs=tuple(pl.BlockSpec((size, blk), lambda s: (0, 0)) for size in sizes),
        ),
        compiler_params=pltpu.CompilerParams(vmem_limit_bytes=VMEM_LIMIT),
        cost_estimate=SMALL,
        name="right_grams",
    )(tile, *after)


def left_gram_kernel(g_ref, after_ref, out_ref, lhh, lcross):
    step = pl.program_id(0)
    last = pl.num_programs(0) - 1
    blk = lhh.shape[-1]
    high, low = split(g_ref[...])
    for i in range(2):
        hi = high[i * blk : (i + 1) * blk, :]
        lo = low[i * blk : (i + 1) * blk, :]
        both = dot(hi, hi, ((1,), (1,)))
        cross = dot(lo, hi, ((1,), (1,)))

        @pl.when(step == 0)
        def _():
            lhh[i] = both
            lcross[i] = cross

        @pl.when(step > 0)
        def _():
            lhh[i] += both
            lcross[i] += cross

    @pl.when(step == last)
    def _():
        body, diag = pack(*(lhh[b] + (lcross[b] + lcross[b].T) for b in range(2)))
        out_ref[:blk, :] = body
        out_ref[blk:, :] = diag


def left_grams(tile, blk, at, after):
    width = tile.shape[1]
    tall = blk + PAD
    return pl.pallas_call(
        left_gram_kernel,
        out_shape=jax.ShapeDtypeStruct((tall, blk), jnp.float32),
        grid_spec=pltpu.PrefetchScalarGridSpec(
            num_scalar_prefetch=0,
            grid=(width // (4 * blk),),
            in_specs=[
                pl.BlockSpec((2 * blk, 4 * blk), placed(lambda s, place: (at(place), s))),
                pl.BlockSpec(memory_space=pl.ANY),
            ],
            out_specs=pl.BlockSpec((tall, blk), lambda s: (0, 0)),
            scratch_shapes=[
                pltpu.VMEM((2, blk, blk), jnp.float32),
                pltpu.VMEM((2, blk, blk), jnp.float32),
            ],
        ),
        compiler_params=pltpu.CompilerParams(vmem_limit_bytes=VMEM_LIMIT),
        cost_estimate=SMALL,
        name="left_grams",
    )(tile, after)


RAW = 1


def own_first(place):
    return place[0] * 2


def core_first(place):
    return (place[0] ^ 1) * 2


def later(k, place):
    return jnp.where(place[0] < 2, 3 + k, jnp.where(k == 0, 0, jnp.where(k < 3, k + 1, 2 * k - 1)))


def take_kernel(block, g_ref, *rest):
    out_ref, sem = rest[-2:]
    rows, blk = out_ref.shape
    top = pl.multiple_of((1 - here()[1]) * rows, rows)
    copy = pltpu.make_async_copy(g_ref.at[pl.ds(top, rows), pl.ds(block * blk, blk)], out_ref, sem)
    copy.start()
    copy.wait()


def take(tile, blk, block, *after):
    anywhere = pl.BlockSpec(memory_space=pl.ANY)
    return pl.pallas_call(
        functools.partial(take_kernel, block),
        out_shape=jax.ShapeDtypeStruct((tile.shape[0] // 2, blk), jnp.float32),
        in_specs=[anywhere] * (1 + len(after)),
        out_specs=anywhere,
        scratch_shapes=[pltpu.SemaphoreType.DMA],
        compiler_params=pltpu.CompilerParams(vmem_limit_bytes=VMEM_LIMIT),
        cost_estimate=SMALL,
        name="take",
    )(tile, *after)


def fold_kernel(a_ref, top_ref, rest_ref, after_ref, out_ref):
    top = top_ref.shape[0]
    out_ref[:top, :] = a_ref[:top, :] + top_ref[...]
    out_ref[top:, :] = a_ref[top:, :] + rest_ref[...]


def fold(kept, top, rest, after):
    return pl.pallas_call(
        fold_kernel,
        out_shape=jax.ShapeDtypeStruct(kept.shape, jnp.float32),
        in_specs=[pl.BlockSpec(memory_space=pltpu.VMEM)] * 3 + [pl.BlockSpec(memory_space=pl.ANY)],
        compiler_params=pltpu.CompilerParams(vmem_limit_bytes=VMEM_LIMIT),
        cost_estimate=SMALL,
        name="fold",
    )(kept, top, rest, after)


def halve_kernel(a_ref, *rest):
    top_ref, rest_ref = rest[-2:]
    top_ref[...] = a_ref[: top_ref.shape[0], :]
    rest_ref[...] = a_ref[top_ref.shape[0] :, :]


def halve(value, *after):
    tall, blk = value.shape
    sizes = ((tall + PAD) // 2, (tall - PAD) // 2)
    return pl.pallas_call(
        halve_kernel,
        out_shape=tuple(jax.ShapeDtypeStruct((size, blk), jnp.float32) for size in sizes),
        in_specs=[pl.BlockSpec(memory_space=pltpu.VMEM)] + [pl.BlockSpec(memory_space=pl.ANY)] * len(after),
        compiler_params=pltpu.CompilerParams(vmem_limit_bytes=VMEM_LIMIT),
        cost_estimate=SMALL,
        name="halve",
    )(value, *after)


def hold_kernel(a_ref, *rest):
    out_ref = rest[-1]
    out_ref[...] = a_ref[...]


def hold(value, *after):
    return pl.pallas_call(
        hold_kernel,
        out_shape=jax.ShapeDtypeStruct(value.shape, jnp.float32),
        in_specs=[pl.BlockSpec(memory_space=pltpu.VMEM)] + [pl.BlockSpec(memory_space=pl.ANY)] * len(after),
        compiler_params=pltpu.CompilerParams(vmem_limit_bytes=VMEM_LIMIT),
        cost_estimate=SMALL,
        name="hold",
    )(value, *after)


def pair_roots(full_dim, stats_ref, body, diag):
    blk = body.shape[0]
    rows, cols = places(blk)
    ident = jnp.where(rows == cols, 1.0, 0.0)
    moving, scales = [], []
    for b, gram in enumerate(unpack(body, diag)):
        factor = (
            beta_mix * stats_ref[b * blk : (b + 1) * blk, :]
            + (1.0 - beta_mix) * (gram / full_dim)
            + eps_shift * ident
        )
        scale = jnp.sqrt(jnp.sum(factor * factor, keepdims=True))
        moving.append(factor / scale)
        scales.append(scale)
    result = None
    for count in range(ITERS):
        steps = [(5.0 * ident - m) * 0.25 for m in moving]
        parts = [split(s) for s in steps]
        if result is None:
            result = steps
        else:
            result = [product(split(r), p) for r, p in zip(result, parts)]
        if count < ITERS - 1:
            squared = [split(product(p, p)) for p in parts]
            fourth = [split(product(s, s)) for s in squared]
            moving = [product(f, split(m)) for f, m in zip(fourth, moving)]
    return [r * jnp.exp(-0.25 * jnp.log(s)) for r, s in zip(result, scales)]


def right_kernel(full_dim, stats_ref, a_ref, top_ref, rest_ref, c_ref, g_ref, after_ref, out_ref, half_ref):
    blk = stats_ref.shape[1]
    total = a_ref[...] + jnp.concatenate([top_ref[...], rest_ref[...]], axis=0) + c_ref[...]
    roots = pair_roots(full_dim, stats_ref, total[:blk], total[blk : blk + 1])
    half_ref[...] = product(split(g_ref[...]), split(roots[0]))
    body, diag = pack(*roots)
    out_ref[:blk, :] = body
    out_ref[blk:, :] = diag


def right_roots(full_dim, stats, kept, near, far, tile, after):
    blk = stats.shape[1]
    tall = blk + PAD
    rows = tile.shape[0] // 2
    flat = pl.BlockSpec((tall, blk), lambda s: (0, 0))
    return pl.pallas_call(
        functools.partial(right_kernel, full_dim),
        out_shape=(
            jax.ShapeDtypeStruct((tall, blk), jnp.float32),
            jax.ShapeDtypeStruct((rows, blk), jnp.float32),
        ),
        grid_spec=pltpu.PrefetchScalarGridSpec(
            num_scalar_prefetch=0,
            grid=(1,),
            in_specs=[
                pl.BlockSpec((2 * blk, blk), placed(lambda s, place: (place[0], 0))),
                flat,
                *(pl.BlockSpec(part.shape, lambda s: (0, 0)) for part in near),
                flat,
                pl.BlockSpec((rows, blk), placed(lambda s, place: (1 - place[1], own_first(place)))),
                pl.BlockSpec(memory_space=pl.ANY),
            ],
            out_specs=(
                flat,
                pl.BlockSpec((rows, blk), lambda s: (0, 0)),
            ),
        ),
        compiler_params=pltpu.CompilerParams(vmem_limit_bytes=VMEM_LIMIT),
        cost_estimate=SMALL,
        name="right_roots",
    )(stats, kept, *near, far, tile, after)


def left_kernel(full_dim, stats_ref, a_ref, b_ref, out_ref):
    blk = stats_ref.shape[1]
    total = a_ref[...] + b_ref[b_ref.shape[0] - a_ref.shape[0] :, :]
    for b, root in enumerate(pair_roots(full_dim, stats_ref, total[:blk], total[blk : blk + 1])):
        high, low = split(root)
        out_ref[b, 0] = high
        out_ref[b, 1] = low


def left_roots(full_dim, stats, kept, came):
    blk = stats.shape[1]
    tall = blk + PAD
    return pl.pallas_call(
        functools.partial(left_kernel, full_dim),
        out_shape=jax.ShapeDtypeStruct((2, 2, blk, blk), jnp.bfloat16),
        grid_spec=pltpu.PrefetchScalarGridSpec(
            num_scalar_prefetch=0,
            grid=(1,),
            in_specs=[
                pl.BlockSpec((2 * blk, blk), placed(lambda s, place: (place[1], 0))),
                pl.BlockSpec((tall, blk), lambda s: (0, 0)),
                pl.BlockSpec(came.shape, lambda s: (0, 0)),
            ],
            out_specs=pl.BlockSpec((2, 2, blk, blk), lambda s: (0, 0, 0, 0)),
        ),
        compiler_params=pltpu.CompilerParams(vmem_limit_bytes=VMEM_LIMIT),
        cost_estimate=SMALL,
        name="left_roots",
    )(stats, kept, came)


def put_roots(out_ref, at, roots):
    for b, root in enumerate(roots):
        high, low = split(root)
        out_ref[at + b, 0] = high
        out_ref[at + b, 1] = low


def spread_kernel(own_ref, c_ref, x_ref, top_ref, rest_ref, out_ref, cut_ref, seconds, body):
    blk = out_ref.shape[-1]
    half = blk // 2
    r = here()[0]
    last = jnp.concatenate([top_ref[...], rest_ref[...]], axis=0)
    for flip, packed in enumerate((own_ref[...], c_ref[...], x_ref[...], last)):
        roots = unpack(packed[:blk, :], packed[blk : blk + 1, :])
        put_roots(out_ref, 2 * (r ^ flip), roots)
        seconds[r ^ flip] = roots[1]
    root = seconds[RAW // 2]
    pair, diag = pack(root[:half, :half], root[half:, half:])
    body[...] = jnp.concatenate([pair, root[:half, half:]], axis=1)
    part = cut_ref.shape[0] - PAD
    cut_ref[:part, :] = body[pl.ds(pl.multiple_of(r * part, part), part), :]
    cut_ref[part:, :] = jnp.concatenate([diag, diag], axis=1)


def spread_roots(*packed):
    blk = packed[0].shape[1]
    count = len(packed) - 1
    return pl.pallas_call(
        spread_kernel,
        out_shape=(
            jax.ShapeDtypeStruct((2 * count, 2, blk, blk), jnp.bfloat16),
            jax.ShapeDtypeStruct((blk // (2 * count) + PAD, blk), jnp.float32),
        ),
        scratch_shapes=[pltpu.VMEM((count, blk, blk), jnp.float32), pltpu.VMEM((blk // 2, blk), jnp.float32)],
        compiler_params=pltpu.CompilerParams(vmem_limit_bytes=VMEM_LIMIT),
        cost_estimate=SMALL,
        name="spread_roots",
    )(*packed)


def rest_kernel(a_ref, out_ref):
    out_ref[...] = a_ref[a_ref.shape[0] - out_ref.shape[0] :, :]


def rest_of(value, rows):
    return pl.pallas_call(
        rest_kernel,
        out_shape=jax.ShapeDtypeStruct((value.shape[0] - rows, value.shape[1]), jnp.float32),
        compiler_params=pltpu.CompilerParams(vmem_limit_bytes=VMEM_LIMIT),
        cost_estimate=SMALL,
        name="rest_of",
    )(value)


def join_kernel(own_ref, c_ref, x_ref, xc_ref, out_ref, body):
    part = own_ref.shape[0] - PAD
    half = body.shape[0]
    r = here()[0]
    for flip, ref in enumerate((own_ref, c_ref, x_ref, xc_ref)):
        body[pl.ds(pl.multiple_of((r ^ flip) * part, part), part), :] = ref[:part, :]
    first, second = unpack(body[:, :half], own_ref[part : part + 1, :half])
    side = body[:, half:]
    top = jnp.concatenate([first, side], axis=1)
    bottom = jnp.concatenate([side.T, second], axis=1)
    put_roots(out_ref, 0, [jnp.concatenate([top, bottom], axis=0)])


def join_root(*parts):
    blk = parts[0].shape[1]
    return pl.pallas_call(
        join_kernel,
        out_shape=jax.ShapeDtypeStruct((1, 2, blk, blk), jnp.bfloat16),
        scratch_shapes=[pltpu.VMEM((blk // 2, blk), jnp.float32)],
        compiler_params=pltpu.CompilerParams(vmem_limit_bytes=VMEM_LIMIT),
        cost_estimate=SMALL,
        name="join_root",
    )(*parts)


def core_apply_kernel(g_ref, packed_ref, out_ref):
    blk = g_ref.shape[1]
    root = unpack(packed_ref[:blk, :], packed_ref[blk : blk + 1, :])[0]
    out_ref[...] = product(split(g_ref[...]), split(root))


def core_apply(tile, packed):
    rows = tile.shape[0] // 2
    tall, blk = packed.shape
    return pl.pallas_call(
        core_apply_kernel,
        out_shape=jax.ShapeDtypeStruct((rows, blk), jnp.float32),
        grid_spec=pltpu.PrefetchScalarGridSpec(
            num_scalar_prefetch=0,
            grid=(1,),
            in_specs=[
                pl.BlockSpec((rows, blk), placed(lambda s, place: (1 - place[1], core_first(place)))),
                pl.BlockSpec((tall, blk), lambda s: (0, 0)),
            ],
            out_specs=pl.BlockSpec((rows, blk), lambda s: (0, 0)),
        ),
        compiler_params=pltpu.CompilerParams(vmem_limit_bytes=VMEM_LIMIT),
        cost_estimate=SMALL,
        name="core_apply",
    )(tile, packed)


def right_apply_kernel(pieces, carries, g_ref, right_ref, *rest):
    out_refs = rest[-len(pieces) :]
    value = product(split(g_ref[...]), (right_ref[0, 0], right_ref[0, 1]))
    for (top, rows, start, width), ref in zip(pieces, out_refs):
        ref[:rows, :] = value[top : top + rows, start : start + width]
    if carries:
        out_refs[0][value.shape[0] :, :] = rest[0][...]


def right_apply(tile, right, k, pieces, under, after):
    rows = tile.shape[0] // 2
    blk = right.shape[-1]
    pieces = pieces or ((0, rows, 0, blk),)
    in_specs = [
        pl.BlockSpec((rows, blk), placed(lambda s, place: (1 - place[1], later(k, place)))),
        pl.BlockSpec((1, 2, blk, blk), placed(lambda s, place: (later(k, place), 0, 0, 0))),
    ]
    operands = [tile, right]
    more = 0
    if under is not None:
        more = under.shape[0]
        in_specs.append(pl.BlockSpec(under.shape, lambda s: (0, 0)))
        operands.append(under)
    shapes = [(tall + more, width) for _, tall, _, width in pieces]
    return pl.pallas_call(
        functools.partial(right_apply_kernel, pieces, under is not None),
        out_shape=tuple(jax.ShapeDtypeStruct(shape, jnp.float32) for shape in shapes),
        grid_spec=pltpu.PrefetchScalarGridSpec(
            num_scalar_prefetch=0,
            grid=(1,),
            in_specs=in_specs + [pl.BlockSpec(memory_space=pl.ANY)] * len(after),
            out_specs=tuple(pl.BlockSpec(shape, lambda s: (0, 0)) for shape in shapes),
        ),
        compiler_params=pltpu.CompilerParams(vmem_limit_bytes=VMEM_LIMIT),
        cost_estimate=SMALL,
        name="right_apply",
    )(*operands, *after)


def left_product(left_ref, value, out_ref):
    blk = left_ref.shape[-1]
    for i in range(value.shape[0] // blk):
        part = split(value[i * blk : (i + 1) * blk])
        out_ref[i * blk : (i + 1) * blk, :] = product((left_ref[i, 0], left_ref[i, 1]), part)


def update_kernel(g_ref, left_ref, right_ref, *rest):
    half = product(split(g_ref[...]), (right_ref[0, 0], right_ref[0, 1]))
    left_product(left_ref, half, rest[-2])
    rest[-1][...] = jnp.zeros_like(rest[-1])


def finish_kernel(column, first, half_ref, left_ref, out_before, out_ref, stage, sems):
    blk = left_ref.shape[-1]
    width = stage.shape[1]
    cols = pl.ds(pl.multiple_of(column(here()), width), width)
    copies = []
    for i in range(stage.shape[0] // blk):
        rows = pl.ds(i * blk, blk)
        root = (left_ref[first + i, 0], left_ref[first + i, 1])
        stage[rows, :] = product(root, split(half_ref[rows, :]))
        copies.append(
            pltpu.make_async_copy(stage.at[rows, :], out_ref.at[pl.ds((first + i) * blk, blk), cols], sems.at[i])
        )
        copies[i].start()
    for copy in copies:
        copy.wait()


def finish(half, left, out, column, first=0, count=2):
    width = half.shape[1]
    blk = left.shape[-1]
    vmem = pl.BlockSpec(memory_space=pltpu.VMEM)
    anywhere = pl.BlockSpec(memory_space=pl.ANY)
    return pl.pallas_call(
        functools.partial(finish_kernel, column, first),
        out_shape=jax.ShapeDtypeStruct(out.shape, jnp.float32),
        in_specs=[vmem, vmem, anywhere],
        out_specs=anywhere,
        scratch_shapes=[pltpu.VMEM((count * blk, width), jnp.float32), pltpu.SemaphoreType.DMA((count,))],
        input_output_aliases={2: 0},
        compiler_params=pltpu.CompilerParams(vmem_limit_bytes=VMEM_LIMIT),
        cost_estimate=SMALL,
        name="finish",
    )(half, left, out)


def update(source, left, right, out, out_shape, g_map, out_map, after=()):
    rows = out_shape[0]
    blk = left.shape[-1]
    in_specs = [
        pl.BlockSpec((rows, blk), placed(g_map)),
        pl.BlockSpec((2, 2, blk, blk), lambda s: (0, 0, 0, 0)),
        pl.BlockSpec((1, 2, blk, blk), lambda s: (s, 0, 0, 0)),
    ]
    operands = [source, left, right]
    aliases = {}
    if out is not None:
        aliases = {len(operands): 0}
        in_specs.append(pl.BlockSpec(memory_space=pl.ANY))
        operands.append(out)
    in_specs += [pl.BlockSpec(memory_space=pl.ANY)] * len(after)
    return pl.pallas_call(
        update_kernel,
        out_shape=(jax.ShapeDtypeStruct(out_shape, jnp.float32), jax.ShapeDtypeStruct((8, 128), jnp.float32)),
        grid_spec=pltpu.PrefetchScalarGridSpec(
            num_scalar_prefetch=0,
            grid=(right.shape[0],),
            in_specs=in_specs,
            out_specs=(pl.BlockSpec((rows, blk), placed(out_map)), pl.BlockSpec((8, 128), lambda s: (0, 0))),
        ),
        input_output_aliases=aliases,
        compiler_params=pltpu.CompilerParams(vmem_limit_bytes=VMEM_LIMIT),
        cost_estimate=SMALL,
        name="update",
    )(*operands, *after)


def exchange_device(full_dim, n_row, grads, left_stats, right_stats):
    tile_rows, tile_cols = grads.shape[1:]
    blk = left_stats.shape[2]
    tile = grads.reshape(tile_rows, tile_cols)
    lstats = left_stats.reshape(tile_rows, blk)
    rstats = right_stats.reshape(tile_cols, blk)
    rows = tile_rows // 2
    shape = (rows, 2 * tile_cols)
    halves = tile_cols // blk

    def over(axis, value):
        if axis == "y":
            return lax.ppermute(value, "col", [(0, 1), (1, 0)])
        flip = {"core": 1, "x": 2}[axis]
        return lax.ppermute(value, "row", [(i, i ^ flip) for i in range(n_row)])

    first = take(pltpu.with_memory_space_constraint(tile, pltpu.HBM), blk, RAW)
    raw = over("y", first)

    *send_on, keep_on = right_grams(tile, blk, (3, 2), 2, first)
    lsend = left_grams(tile, blk, lambda place: 1 - place[1], send_on[0])
    lcame = over("y", lsend)
    far = fold(keep_on, *(over("core", part) for part in send_on), lsend)
    *send, keep = right_grams(tile, blk, (1, 0), 2, far)
    near = [over("core", part) for part in send]
    far = over("x", far)

    own, half = right_roots(full_dim, rstats, keep, near, far, tile, raw)
    came_a = over("y", half)
    own = hold(own, lcame)
    own_c = over("core", own)
    own_x = over("x", own)
    half = core_apply(tile, own_c)
    came_b = over("y", half)
    parts = halve(own_x, half, came_a)
    lkeep = left_grams(tile, blk, lambda place: place[1], half)
    roots, part = spread_roots(own, own_c, own_x, *(over("core", value) for value in parts))

    (half,) = right_apply(tile, roots, 0, None, part, (lkeep,))
    came_c = over("y", half)
    left = left_roots(full_dim, lstats, lkeep, lcame)
    (half,) = right_apply(tile, roots, 1, None, None, (came_b, left))
    came_d = over("y", half)

    def crossed(block, start=0):
        return lambda place: (1 - place[1]) * tile_cols + block(place) * blk + start

    out, done = update(
        tile, left, roots, None, shape,
        lambda s, place: (place[1], s),
        lambda s, place: (0, place[1] * halves + s),
    )
    (half,) = right_apply(tile, roots, 2, None, None, (came_c, done))
    came_e = over("y", half)
    (half,) = right_apply(tile, roots, 3, None, None, (came_d,))
    came_f = over("y", half)
    out = finish(came_a, left, out, crossed(own_first))
    out = finish(came_b, left, out, crossed(core_first))
    part = rest_of(came_c, rows)
    part_x = over("x", part)
    root_raw = join_root(part, over("core", part), part_x, over("core", part_x))
    out, done = update(
        raw, left, root_raw, out, shape,
        lambda s, place: (0, 0),
        lambda s, place: (0, (1 - place[1]) * halves + RAW),
        (half,),
    )
    wide = blk // 2
    last = ((0, rows, 0, wide), (0, blk, wide, wide), (blk, blk, wide, wide))
    came_last = [over("y", half) for half in right_apply(tile, roots, 4, last, None, (came_e,))]
    for k, value in enumerate((came_c, came_d, came_e, came_f)):
        out = finish(value, left, out, crossed(functools.partial(later, k)))
    for (top, tall, start, _), value in zip(last, came_last):
        out = finish(value, left, out, crossed(functools.partial(later, 4), start), top // blk, tall // blk)
    return out.reshape(1, rows, 2 * tile_cols)


def per_device(n_row, n_col, grads, left_stats, right_stats):
    mats, tile_rows, tile_cols = grads.shape
    blk = left_stats.shape[2]
    full_dim = tile_cols * n_col
    if mats == 1 and n_col == 2 and n_row == 4 and tile_rows == 4 * blk and tile_cols == 8 * blk:
        return exchange_device(full_dim, n_row, grads, left_stats, right_stats)
    return general_device(full_dim, grads, left_stats, right_stats)


def solution(mesh):
    return jax.shard_map(
        functools.partial(per_device, mesh.shape["row"], mesh.shape["col"]),
        mesh=mesh,
        in_specs=(P("mat", "row", "col"), P("mat", "row", None), P("mat", "col", None)),
        out_specs=P("mat", ("row", "col"), None),
        check_vma=False,
    )
```

```python
import functools

import jax
import jax.numpy as jnp
from jax import lax
from jax.experimental import pallas as pl
from jax.experimental.pallas import tpu as pltpu
from jax.sharding import PartitionSpec as P

ITERS = 3
beta_mix = 0.5
eps_shift = 0.001
PAD = 8
VMEM_LIMIT = 24 * 1024 * 1024
SMALL = pl.CostEstimate(flops=1, bytes_accessed=1, transcendentals=0)


def matmul(left, right):
    return jnp.einsum("...ij,...jk->...ik", left, right, precision=lax.Precision.HIGHEST)


def newton_root(factor):
    size = factor.shape[-1]
    ident = jnp.eye(size, dtype=jnp.float32)
    scale = jnp.sqrt(jnp.sum(factor * factor, axis=(-2, -1), keepdims=True))
    moving = factor / scale
    result = jnp.broadcast_to(ident, factor.shape)
    for count in range(ITERS):
        step_mat = (5.0 * ident - moving) * 0.25
        result = matmul(result, step_mat)
        squared = matmul(step_mat, step_mat)
        moving = matmul(matmul(squared, squared), moving)
    return result * jnp.power(scale, -0.25)


def general_device(full_dim, grads, left_stats, right_stats):
    mats, tile_rows, tile_cols = grads.shape
    blk = left_stats.shape[2]
    row_blocks = tile_rows // blk
    col_blocks = tile_cols // blk
    ident = jnp.eye(blk, dtype=jnp.float32)
    by_rows = grads.reshape(mats, row_blocks, blk, tile_cols)
    left_part = jnp.einsum("mibd,mied->mibe", by_rows, by_rows, precision=lax.Precision.HIGHEST) / full_dim
    by_cols = grads.reshape(mats, tile_rows, col_blocks, blk)
    right_part = (
        jnp.einsum("mdjb,mdje->mjbe", by_cols, by_cols, precision=lax.Precision.HIGHEST) / full_dim
    )
    left_gram = lax.psum(left_part, "col")
    right_gram = lax.psum(right_part, "row")
    left_factor = (
        beta_mix * left_stats.reshape(mats, row_blocks, blk, blk)
        + (1.0 - beta_mix) * left_gram
        + eps_shift * ident
    )
    right_factor = (
        beta_mix * right_stats.reshape(mats, col_blocks, blk, blk)
        + (1.0 - beta_mix) * right_gram
        + eps_shift * ident
    )
    left_root = newton_root(left_factor)
    right_root = newton_root(right_factor)
    half = jnp.einsum("mibe,mied->mibd", left_root, by_rows, precision=lax.Precision.HIGHEST)
    half = half.reshape(mats, tile_rows, col_blocks, blk)
    full = jnp.einsum("mdjb,mjbe->mdje", half, right_root, precision=lax.Precision.HIGHEST)
    full = full.reshape(mats, tile_rows, tile_cols)
    return lax.all_to_all(full, "col", split_axis=1, concat_axis=2, tiled=True)


def here():
    return lax.axis_index("row"), lax.axis_index("col")


def placed(index_map):
    return lambda s: index_map(s, here())


def split(value):
    high = value.astype(jnp.bfloat16)
    low = (value - high.astype(jnp.float32)).astype(jnp.bfloat16)
    return high, low


def dot(left, right, dims=((1,), (0,))):
    return lax.dot_general(left, right, (dims, ((), ())), preferred_element_type=jnp.float32)


def product(left, right):
    lh, ll = left
    rh, rl = right
    return dot(lh, rh) + (dot(lh, rl) + dot(ll, rh))


def places(blk):
    rows = lax.broadcasted_iota(jnp.int32, (blk, blk), 0)
    cols = lax.broadcasted_iota(jnp.int32, (blk, blk), 1)
    return rows, cols


def pack(first, second):
    blk = first.shape[0]
    rows, cols = places(blk)
    body = jnp.where(rows <= cols, first, second)
    diag = jnp.sum(jnp.where(rows == cols, second, 0.0), axis=0, keepdims=True)
    return body, jnp.broadcast_to(diag, (PAD, blk))


def unpack(body, diag):
    blk = body.shape[0]
    rows, cols = places(blk)
    turned = body.T
    first = jnp.where(rows <= cols, body, turned)
    second = jnp.where(rows > cols, body, jnp.where(rows == cols, diag, turned))
    return first, second


def right_gram_kernel(g_ref, *rest):
    out_refs = rest[-2:]
    step = pl.program_id(0)
    blk = g_ref.shape[1] // 2
    high, low = split(g_ref[...])
    grams = []
    for b in range(2):
        hb = high[:, b * blk : (b + 1) * blk]
        lb = low[:, b * blk : (b + 1) * blk]
        both = dot(hb, hb, ((0,), (0,)))
        cross = dot(hb, lb, ((0,), (0,)))
        grams.append(both + (cross + cross.T))
    body, diag = pack(*grams)

    for at, ref in enumerate(out_refs):

        @pl.when(step == at)
        def _():
            ref[:blk, :] = body
            ref[blk:, :] = diag


def right_grams(tile, blk, flips, *after):
    rows = tile.shape[0]
    tall = blk + PAD
    flip = lambda s: jnp.where(s == 0, flips[0], flips[1])
    return pl.pallas_call(
        right_gram_kernel,
        out_shape=(jax.ShapeDtypeStruct((tall, blk), jnp.float32),) * 2,
        grid_spec=pltpu.PrefetchScalarGridSpec(
            num_scalar_prefetch=0,
            grid=(2,),
            in_specs=[
                pl.BlockSpec((rows, 2 * blk), placed(lambda s, place: (0, place[0] ^ flip(s)))),
            ]
            + [pl.BlockSpec(memory_space=pl.ANY)] * len(after),
            out_specs=(pl.BlockSpec((tall, blk), lambda s: (0, 0)),) * 2,
        ),
        compiler_params=pltpu.CompilerParams(vmem_limit_bytes=VMEM_LIMIT),
        cost_estimate=SMALL,
        name="right_grams",
    )(tile, *after)


def left_gram_kernel(g_ref, after_ref, out_ref, lhh, lcross):
    step = pl.program_id(0)
    last = pl.num_programs(0) - 1
    blk = lhh.shape[-1]
    high, low = split(g_ref[...])
    for i in range(2):
        hi = high[i * blk : (i + 1) * blk, :]
        lo = low[i * blk : (i + 1) * blk, :]
        both = dot(hi, hi, ((1,), (1,)))
        cross = dot(lo, hi, ((1,), (1,)))

        @pl.when(step == 0)
        def _():
            lhh[i] = both
            lcross[i] = cross

        @pl.when(step > 0)
        def _():
            lhh[i] += both
            lcross[i] += cross

    @pl.when(step == last)
    def _():
        body, diag = pack(*(lhh[b] + (lcross[b] + lcross[b].T) for b in range(2)))
        out_ref[:blk, :] = body
        out_ref[blk:, :] = diag


def left_grams(tile, blk, at, after):
    width = tile.shape[1]
    tall = blk + PAD
    return pl.pallas_call(
        left_gram_kernel,
        out_shape=jax.ShapeDtypeStruct((tall, blk), jnp.float32),
        grid_spec=pltpu.PrefetchScalarGridSpec(
            num_scalar_prefetch=0,
            grid=(width // (4 * blk),),
            in_specs=[
                pl.BlockSpec((2 * blk, 4 * blk), placed(lambda s, place: (at(place), s))),
                pl.BlockSpec(memory_space=pl.ANY),
            ],
            out_specs=pl.BlockSpec((tall, blk), lambda s: (0, 0)),
            scratch_shapes=[
                pltpu.VMEM((2, blk, blk), jnp.float32),
                pltpu.VMEM((2, blk, blk), jnp.float32),
            ],
        ),
        compiler_params=pltpu.CompilerParams(vmem_limit_bytes=VMEM_LIMIT),
        cost_estimate=SMALL,
        name="left_grams",
    )(tile, after)


RAW = (1, 3)


def own_first(place):
    return place[0] * 2


def core_first(place):
    return (place[0] ^ 1) * 2


def later(k, place):
    return jnp.where(place[0] < 2, 4 + k, jnp.where(k < 2, 2 * k, 2 * k + 1))


def take_kernel(block, g_ref, *rest):
    out_ref, sems = rest[-2:]
    rows, blk = out_ref.shape
    count = sems.shape[0]
    part = rows // count
    copies = []
    for k in range(count):
        top = pl.multiple_of((1 - here()[1]) * rows + k * part, part)
        source = g_ref.at[pl.ds(top, part), pl.ds(block * blk, blk)]
        copies.append(pltpu.make_async_copy(source, out_ref.at[pl.ds(k * part, part), :], sems.at[k]))
        copies[k].start()
    for copy in copies:
        copy.wait()


def take(tile, blk, block, count, *after):
    anywhere = pl.BlockSpec(memory_space=pl.ANY)
    return pl.pallas_call(
        functools.partial(take_kernel, block),
        out_shape=jax.ShapeDtypeStruct((tile.shape[0] // 2, blk), jnp.float32),
        in_specs=[anywhere] * (1 + len(after)),
        out_specs=anywhere,
        scratch_shapes=[pltpu.SemaphoreType.DMA((count,))],
        compiler_params=pltpu.CompilerParams(vmem_limit_bytes=VMEM_LIMIT),
        cost_estimate=SMALL,
        name="take",
    )(tile, *after)


def load_kernel(g_ref, after_ref, out_ref, sems):
    count = sems.shape[0]
    part = g_ref.shape[0] // count
    copies = []
    for k in range(count):
        rows = pl.ds(k * part, part)
        copies.append(pltpu.make_async_copy(g_ref.at[rows, :], out_ref.at[rows, :], sems.at[k]))
        copies[k].start()
    for copy in copies:
        copy.wait()


def load(tile, after):
    anywhere = pl.BlockSpec(memory_space=pl.ANY)
    return pl.pallas_call(
        load_kernel,
        out_shape=jax.ShapeDtypeStruct(tile.shape, jnp.float32),
        in_specs=[anywhere, anywhere],
        out_specs=anywhere,
        scratch_shapes=[pltpu.SemaphoreType.DMA((4,))],
        compiler_params=pltpu.CompilerParams(vmem_limit_bytes=VMEM_LIMIT),
        cost_estimate=SMALL,
        name="load",
    )(tile, after)


def fold_kernel(a_ref, b_ref, out_ref):
    out_ref[...] = a_ref[...] + b_ref[...]


def fold(kept, near):
    return pl.pallas_call(
        fold_kernel,
        out_shape=jax.ShapeDtypeStruct(kept.shape, jnp.float32),
        compiler_params=pltpu.CompilerParams(vmem_limit_bytes=VMEM_LIMIT),
        cost_estimate=SMALL,
        name="fold",
    )(kept, near)


def hold_kernel(a_ref, *rest):
    out_ref = rest[-1]
    out_ref[...] = a_ref[...]


def hold(value, *after):
    return pl.pallas_call(
        hold_kernel,
        out_shape=jax.ShapeDtypeStruct(value.shape, jnp.float32),
        in_specs=[pl.BlockSpec(memory_space=pltpu.VMEM)] + [pl.BlockSpec(memory_space=pl.ANY)] * len(after),
        compiler_params=pltpu.CompilerParams(vmem_limit_bytes=VMEM_LIMIT),
        cost_estimate=SMALL,
        name="hold",
    )(value, *after)


def pair_roots(full_dim, stats_ref, body, diag):
    blk = body.shape[0]
    rows, cols = places(blk)
    ident = jnp.where(rows == cols, 1.0, 0.0)
    moving, scales = [], []
    for b, gram in enumerate(unpack(body, diag)):
        factor = (
            beta_mix * stats_ref[b * blk : (b + 1) * blk, :]
            + (1.0 - beta_mix) * (gram / full_dim)
            + eps_shift * ident
        )
        scale = jnp.sqrt(jnp.sum(factor * factor, keepdims=True))
        moving.append(factor / scale)
        scales.append(scale)
    result = None
    for count in range(ITERS):
        steps = [(5.0 * ident - m) * 0.25 for m in moving]
        parts = [split(s) for s in steps]
        if result is None:
            result = steps
        else:
            result = [product(split(r), p) for r, p in zip(result, parts)]
        if count < ITERS - 1:
            squared = [split(product(p, p)) for p in parts]
            fourth = [split(product(s, s)) for s in squared]
            moving = [product(f, split(m)) for f, m in zip(fourth, moving)]
    return [r * jnp.exp(-0.25 * jnp.log(s)) for r, s in zip(result, scales)]


def right_kernel(full_dim, stats_ref, a_ref, b_ref, c_ref, g_ref, out_ref, half_ref):
    blk = stats_ref.shape[1]
    total = a_ref[...] + b_ref[...] + c_ref[...]
    roots = pair_roots(full_dim, stats_ref, total[:blk], total[blk : blk + 1])
    half_ref[...] = product(split(g_ref[...]), split(roots[0]))
    body, diag = pack(*roots)
    out_ref[:blk, :] = body
    out_ref[blk:, :] = diag


def right_roots(full_dim, stats, kept, near, far, tile):
    blk = stats.shape[1]
    tall = blk + PAD
    rows = tile.shape[0] // 2
    flat = pl.BlockSpec((tall, blk), lambda s: (0, 0))
    return pl.pallas_call(
        functools.partial(right_kernel, full_dim),
        out_shape=(
            jax.ShapeDtypeStruct((tall, blk), jnp.float32),
            jax.ShapeDtypeStruct((rows, blk), jnp.float32),
        ),
        grid_spec=pltpu.PrefetchScalarGridSpec(
            num_scalar_prefetch=0,
            grid=(1,),
            in_specs=[
                pl.BlockSpec((2 * blk, blk), placed(lambda s, place: (place[0], 0))),
                flat,
                flat,
                flat,
                pl.BlockSpec((rows, blk), placed(lambda s, place: (1 - place[1], own_first(place)))),
            ],
            out_specs=(
                flat,
                pl.BlockSpec((rows, blk), lambda s: (0, 0)),
            ),
        ),
        compiler_params=pltpu.CompilerParams(vmem_limit_bytes=VMEM_LIMIT),
        cost_estimate=SMALL,
        name="right_roots",
    )(stats, kept, near, far, tile)


def left_kernel(full_dim, stats_ref, a_ref, b_ref, out_ref):
    blk = stats_ref.shape[1]
    total = a_ref[...] + b_ref[b_ref.shape[0] - a_ref.shape[0] :, :]
    for b, root in enumerate(pair_roots(full_dim, stats_ref, total[:blk], total[blk : blk + 1])):
        high, low = split(root)
        out_ref[b, 0] = high
        out_ref[b, 1] = low


def left_roots(full_dim, stats, kept, came):
    blk = stats.shape[1]
    tall = blk + PAD
    return pl.pallas_call(
        functools.partial(left_kernel, full_dim),
        out_shape=jax.ShapeDtypeStruct((2, 2, blk, blk), jnp.bfloat16),
        grid_spec=pltpu.PrefetchScalarGridSpec(
            num_scalar_prefetch=0,
            grid=(1,),
            in_specs=[
                pl.BlockSpec((2 * blk, blk), placed(lambda s, place: (place[1], 0))),
                pl.BlockSpec((tall, blk), lambda s: (0, 0)),
                pl.BlockSpec(came.shape, lambda s: (0, 0)),
            ],
            out_specs=pl.BlockSpec((2, 2, blk, blk), lambda s: (0, 0, 0, 0)),
        ),
        compiler_params=pltpu.CompilerParams(vmem_limit_bytes=VMEM_LIMIT),
        cost_estimate=SMALL,
        name="left_roots",
    )(stats, kept, came)


def put_roots(out_ref, at, roots):
    for b, root in enumerate(roots):
        high, low = split(root)
        out_ref[at + b, 0] = high
        out_ref[at + b, 1] = low


def spread_kernel(own_ref, c_ref, x_ref, xc_ref, out_ref, cut_ref, seconds, body):
    blk = out_ref.shape[-1]
    r = here()[0]
    for flip, ref in enumerate((own_ref, c_ref, x_ref, xc_ref)):
        roots = unpack(ref[:blk, :], ref[blk : blk + 1, :])
        put_roots(out_ref, 2 * (r ^ flip), roots)
        seconds[r ^ flip] = roots[1]
    part = cut_ref.shape[0] - PAD
    body[...], diag = pack(seconds[RAW[0] // 2], seconds[RAW[1] // 2])
    cut_ref[:part, :] = body[pl.ds(pl.multiple_of(r * part, part), part), :]
    cut_ref[part:, :] = diag


def spread_roots(*packed):
    blk = packed[0].shape[1]
    count = len(packed)
    return pl.pallas_call(
        spread_kernel,
        out_shape=(
            jax.ShapeDtypeStruct((2 * count, 2, blk, blk), jnp.bfloat16),
            jax.ShapeDtypeStruct((blk // count + PAD, blk), jnp.float32),
        ),
        scratch_shapes=[pltpu.VMEM((count, blk, blk), jnp.float32), pltpu.VMEM((blk, blk), jnp.float32)],
        compiler_params=pltpu.CompilerParams(vmem_limit_bytes=VMEM_LIMIT),
        cost_estimate=SMALL,
        name="spread_roots",
    )(*packed)


def rest_kernel(a_ref, out_ref):
    out_ref[...] = a_ref[a_ref.shape[0] - out_ref.shape[0] :, :]


def rest_of(value, rows):
    return pl.pallas_call(
        rest_kernel,
        out_shape=jax.ShapeDtypeStruct((value.shape[0] - rows, value.shape[1]), jnp.float32),
        compiler_params=pltpu.CompilerParams(vmem_limit_bytes=VMEM_LIMIT),
        cost_estimate=SMALL,
        name="rest_of",
    )(value)


def join_kernel(own_ref, c_ref, x_ref, xc_ref, out_ref, body):
    part = own_ref.shape[0] - PAD
    r = here()[0]
    for flip, ref in enumerate((own_ref, c_ref, x_ref, xc_ref)):
        body[pl.ds(pl.multiple_of((r ^ flip) * part, part), part), :] = ref[:part, :]
    put_roots(out_ref, 0, unpack(body[...], own_ref[part : part + 1, :]))


def join_roots(*parts):
    blk = parts[0].shape[1]
    return pl.pallas_call(
        join_kernel,
        out_shape=jax.ShapeDtypeStruct((2, 2, blk, blk), jnp.bfloat16),
        scratch_shapes=[pltpu.VMEM((blk, blk), jnp.float32)],
        compiler_params=pltpu.CompilerParams(vmem_limit_bytes=VMEM_LIMIT),
        cost_estimate=SMALL,
        name="join_roots",
    )(*parts)


def core_apply_kernel(g_ref, packed_ref, under_ref, out_ref):
    rows, blk = g_ref.shape
    root = unpack(packed_ref[:blk, :], packed_ref[blk : blk + 1, :])[0]
    out_ref[:rows, :] = product(split(g_ref[...]), split(root))
    out_ref[rows:, :] = under_ref[...]


def core_apply(tile, packed, under):
    rows = tile.shape[0] // 2
    tall, blk = packed.shape
    return pl.pallas_call(
        core_apply_kernel,
        out_shape=jax.ShapeDtypeStruct((rows + tall, blk), jnp.float32),
        grid_spec=pltpu.PrefetchScalarGridSpec(
            num_scalar_prefetch=0,
            grid=(1,),
            in_specs=[
                pl.BlockSpec((rows, blk), placed(lambda s, place: (1 - place[1], core_first(place)))),
                pl.BlockSpec((tall, blk), lambda s: (0, 0)),
                pl.BlockSpec((tall, blk), lambda s: (0, 0)),
            ],
            out_specs=pl.BlockSpec((rows + tall, blk), lambda s: (0, 0)),
        ),
        compiler_params=pltpu.CompilerParams(vmem_limit_bytes=VMEM_LIMIT),
        cost_estimate=SMALL,
        name="core_apply",
    )(tile, packed, under)


def right_apply_kernel(pieces, carries, g_ref, right_ref, *rest):
    out_refs = rest[-len(pieces) :]
    value = product(split(g_ref[...]), (right_ref[0, 0], right_ref[0, 1]))
    for (top, rows, start, width), ref in zip(pieces, out_refs):
        ref[:rows, :] = value[top : top + rows, start : start + width]
    if carries:
        out_refs[0][value.shape[0] :, :] = rest[0][...]


def right_apply(tile, right, k, pieces, under, after):
    rows = tile.shape[0] // 2
    blk = right.shape[-1]
    pieces = pieces or ((0, rows, 0, blk),)
    in_specs = [
        pl.BlockSpec((rows, blk), placed(lambda s, place: (1 - place[1], later(k, place)))),
        pl.BlockSpec((1, 2, blk, blk), placed(lambda s, place: (later(k, place), 0, 0, 0))),
    ]
    operands = [tile, right]
    more = 0
    if under is not None:
        more = under.shape[0]
        in_specs.append(pl.BlockSpec(under.shape, lambda s: (0, 0)))
        operands.append(under)
    shapes = [(tall + more, width) for _, tall, _, width in pieces]
    return pl.pallas_call(
        functools.partial(right_apply_kernel, pieces, under is not None),
        out_shape=tuple(jax.ShapeDtypeStruct(shape, jnp.float32) for shape in shapes),
        grid_spec=pltpu.PrefetchScalarGridSpec(
            num_scalar_prefetch=0,
            grid=(1,),
            in_specs=in_specs + [pl.BlockSpec(memory_space=pl.ANY)] * len(after),
            out_specs=tuple(pl.BlockSpec(shape, lambda s: (0, 0)) for shape in shapes),
        ),
        compiler_params=pltpu.CompilerParams(vmem_limit_bytes=VMEM_LIMIT),
        cost_estimate=SMALL,
        name="right_apply",
    )(*operands, *after)


def left_product(left_ref, value, out_ref):
    blk = left_ref.shape[-1]
    for i in range(value.shape[0] // blk):
        part = split(value[i * blk : (i + 1) * blk])
        out_ref[i * blk : (i + 1) * blk, :] = product((left_ref[i, 0], left_ref[i, 1]), part)


def update_kernel(g_ref, left_ref, right_ref, *rest):
    half = product(split(g_ref[...]), (right_ref[0, 0], right_ref[0, 1]))
    left_product(left_ref, half, rest[-2])
    rest[-1][...] = jnp.zeros_like(rest[-1])


def finish_kernel(column, first, half_ref, left_ref, out_before, out_ref, stage, sems):
    blk = left_ref.shape[-1]
    width = stage.shape[1]
    cols = pl.ds(pl.multiple_of(column(here()), width), width)
    copies = []
    for i in range(stage.shape[0] // blk):
        rows = pl.ds(i * blk, blk)
        root = (left_ref[first + i, 0], left_ref[first + i, 1])
        stage[rows, :] = product(root, split(half_ref[rows, :]))
        copies.append(
            pltpu.make_async_copy(stage.at[rows, :], out_ref.at[pl.ds((first + i) * blk, blk), cols], sems.at[i])
        )
        copies[i].start()
    for copy in copies:
        copy.wait()


def finish(half, left, out, column, first=0, count=2):
    width = half.shape[1]
    blk = left.shape[-1]
    vmem = pl.BlockSpec(memory_space=pltpu.VMEM)
    anywhere = pl.BlockSpec(memory_space=pl.ANY)
    return pl.pallas_call(
        functools.partial(finish_kernel, column, first),
        out_shape=jax.ShapeDtypeStruct(out.shape, jnp.float32),
        in_specs=[vmem, vmem, anywhere],
        out_specs=anywhere,
        scratch_shapes=[pltpu.VMEM((count * blk, width), jnp.float32), pltpu.SemaphoreType.DMA((count,))],
        input_output_aliases={2: 0},
        compiler_params=pltpu.CompilerParams(vmem_limit_bytes=VMEM_LIMIT),
        cost_estimate=SMALL,
        name="finish",
    )(half, left, out)


def update(source, left, right, out, out_shape, g_map, out_map, first=0, count=None, after=()):
    rows = out_shape[0]
    blk = left.shape[-1]
    in_specs = [
        pl.BlockSpec((rows, blk), placed(g_map)),
        pl.BlockSpec((2, 2, blk, blk), lambda s: (0, 0, 0, 0)),
        pl.BlockSpec((1, 2, blk, blk), lambda s: (first + s, 0, 0, 0)),
    ]
    operands = [source, left, right]
    aliases = {}
    if out is not None:
        aliases = {len(operands): 0}
        in_specs.append(pl.BlockSpec(memory_space=pl.ANY))
        operands.append(out)
    in_specs += [pl.BlockSpec(memory_space=pl.ANY)] * len(after)
    return pl.pallas_call(
        update_kernel,
        out_shape=(jax.ShapeDtypeStruct(out_shape, jnp.float32), jax.ShapeDtypeStruct((8, 128), jnp.float32)),
        grid_spec=pltpu.PrefetchScalarGridSpec(
            num_scalar_prefetch=0,
            grid=(count or right.shape[0],),
            in_specs=in_specs,
            out_specs=(pl.BlockSpec((rows, blk), placed(out_map)), pl.BlockSpec((8, 128), lambda s: (0, 0))),
        ),
        input_output_aliases=aliases,
        compiler_params=pltpu.CompilerParams(vmem_limit_bytes=VMEM_LIMIT),
        cost_estimate=SMALL,
        name="update",
    )(*operands, *after)


def exchange_device(full_dim, n_row, grads, left_stats, right_stats):
    tile_rows, tile_cols = grads.shape[1:]
    blk = left_stats.shape[2]
    tile = pltpu.with_memory_space_constraint(grads.reshape(tile_rows, tile_cols), pltpu.HBM)
    lstats = left_stats.reshape(tile_rows, blk)
    rstats = right_stats.reshape(tile_cols, blk)
    rows = tile_rows // 2
    shape = (rows, 2 * tile_cols)
    halves = tile_cols // blk

    def over(axis, value):
        if axis == "y":
            return lax.ppermute(value, "col", [(0, 1), (1, 0)])
        flip = {"core": 1, "x": 2}[axis]
        return lax.ppermute(value, "row", [(i, i ^ flip) for i in range(n_row)])

    first = take(tile, blk, RAW[0], 1)
    raw = [over("y", first)]
    tile = load(tile, first)

    send_on, keep_on = right_grams(tile, blk, (3, 2), first)
    far = fold(keep_on, over("core", send_on))
    raw.append(over("y", take(tile, blk, RAW[1], 16, send_on)))
    send, keep = right_grams(tile, blk, (1, 0), far, raw[0])
    near = over("core", send)
    far = over("x", far)

    own, half = right_roots(full_dim, rstats, keep, near, far, tile)
    came_a = over("y", half)
    lsend = left_grams(tile, blk, lambda place: 1 - place[1], half)
    own = hold(own, raw[1], lsend)
    own_c = over("core", own)
    own_x = over("x", own)
    half = core_apply(tile, own_c, lsend)
    came_b = over("y", half)
    own_x = hold(own_x, half, came_a)
    lkeep = left_grams(tile, blk, lambda place: place[1], half)
    roots, part = spread_roots(own, own_c, own_x, over("core", own_x))

    (half,) = right_apply(tile, roots, 0, None, part, (lkeep,))
    came_c = over("y", half)
    (half,) = right_apply(tile, roots, 1, None, None, (came_b,))
    came_d = over("y", half)

    def crossed(block, start=0):
        return lambda place: (1 - place[1]) * tile_cols + block(place) * blk + start

    left = left_roots(full_dim, lstats, lkeep, came_b)
    out, done = update(
        tile, left, roots, None, shape,
        lambda s, place: (place[1], s),
        lambda s, place: (0, place[1] * halves + s),
    )
    (half,) = right_apply(tile, roots, 2, None, None, (came_c, done))
    came_e = over("y", half)
    wide = blk // 2
    last = ((0, rows, 0, wide), (0, blk, wide, wide), (blk, blk, wide, wide))
    held = right_apply(tile, roots, 3, last, None, (came_d,))
    came_last = [over("y", half) for half in held]
    out = finish(came_a, left, out, crossed(own_first))
    out = finish(came_b, left, out, crossed(core_first))
    part = rest_of(came_c, rows)
    part_x = over("x", part)
    roots_raw = join_roots(part, over("core", part), part_x, over("core", part_x))
    for k, (block, value) in enumerate(zip(RAW, raw)):
        out, done = update(
            value, left, roots_raw, out, shape,
            lambda s, place: (0, 0),
            lambda s, place, block=block: (0, (1 - place[1]) * halves + block),
            k, 1, held[:1],
        )
    for k, value in enumerate((came_c, came_d, came_e)):
        out = finish(value, left, out, crossed(functools.partial(later, k)))
    for (top, tall, start, _), value in zip(last, came_last):
        out = finish(value, left, out, crossed(functools.partial(later, 3), start), top // blk, tall // blk)
    return out.reshape(1, rows, 2 * tile_cols)


def per_device(n_row, n_col, grads, left_stats, right_stats):
    mats, tile_rows, tile_cols = grads.shape
    blk = left_stats.shape[2]
    full_dim = tile_cols * n_col
    if mats == 1 and n_col == 2 and n_row == 4 and tile_rows == 4 * blk and tile_cols == 8 * blk:
        return exchange_device(full_dim, n_row, grads, left_stats, right_stats)
    return general_device(full_dim, grads, left_stats, right_stats)


def solution(mesh):
    return jax.shard_map(
        functools.partial(per_device, mesh.shape["row"], mesh.shape["col"]),
        mesh=mesh,
        in_specs=(P("mat", "row", "col"), P("mat", "row", None), P("mat", "col", None)),
        out_specs=P("mat", ("row", "col"), None),
        check_vma=False,
    )
```

```python
import functools

import jax
import jax.numpy as jnp
from jax import lax
from jax.experimental import pallas as pl
from jax.experimental.pallas import tpu as pltpu
from jax.sharding import PartitionSpec as P

ITERS = 3
beta_mix = 0.5
eps_shift = 0.001
PAD = 8
VMEM_LIMIT = 24 * 1024 * 1024
SMALL = pl.CostEstimate(flops=1, bytes_accessed=1, transcendentals=0)


def matmul(left, right):
    return jnp.einsum("...ij,...jk->...ik", left, right, precision=lax.Precision.HIGHEST)


def newton_root(factor):
    size = factor.shape[-1]
    ident = jnp.eye(size, dtype=jnp.float32)
    scale = jnp.sqrt(jnp.sum(factor * factor, axis=(-2, -1), keepdims=True))
    moving = factor / scale
    result = jnp.broadcast_to(ident, factor.shape)
    for count in range(ITERS):
        step_mat = (5.0 * ident - moving) * 0.25
        result = matmul(result, step_mat)
        squared = matmul(step_mat, step_mat)
        moving = matmul(matmul(squared, squared), moving)
    return result * jnp.power(scale, -0.25)


def general_device(full_dim, grads, left_stats, right_stats):
    mats, tile_rows, tile_cols = grads.shape
    blk = left_stats.shape[2]
    row_blocks = tile_rows // blk
    col_blocks = tile_cols // blk
    ident = jnp.eye(blk, dtype=jnp.float32)
    by_rows = grads.reshape(mats, row_blocks, blk, tile_cols)
    left_part = jnp.einsum("mibd,mied->mibe", by_rows, by_rows, precision=lax.Precision.HIGHEST) / full_dim
    by_cols = grads.reshape(mats, tile_rows, col_blocks, blk)
    right_part = (
        jnp.einsum("mdjb,mdje->mjbe", by_cols, by_cols, precision=lax.Precision.HIGHEST) / full_dim
    )
    left_gram = lax.psum(left_part, "col")
    right_gram = lax.psum(right_part, "row")
    left_factor = (
        beta_mix * left_stats.reshape(mats, row_blocks, blk, blk)
        + (1.0 - beta_mix) * left_gram
        + eps_shift * ident
    )
    right_factor = (
        beta_mix * right_stats.reshape(mats, col_blocks, blk, blk)
        + (1.0 - beta_mix) * right_gram
        + eps_shift * ident
    )
    left_root = newton_root(left_factor)
    right_root = newton_root(right_factor)
    half = jnp.einsum("mibe,mied->mibd", left_root, by_rows, precision=lax.Precision.HIGHEST)
    half = half.reshape(mats, tile_rows, col_blocks, blk)
    full = jnp.einsum("mdjb,mjbe->mdje", half, right_root, precision=lax.Precision.HIGHEST)
    full = full.reshape(mats, tile_rows, tile_cols)
    return lax.all_to_all(full, "col", split_axis=1, concat_axis=2, tiled=True)


def here():
    return lax.axis_index("row"), lax.axis_index("col")


def placed(index_map):
    return lambda s: index_map(s, here())


def split(value):
    high = value.astype(jnp.bfloat16)
    low = (value - high.astype(jnp.float32)).astype(jnp.bfloat16)
    return high, low


def dot(left, right, dims=((1,), (0,))):
    return lax.dot_general(left, right, (dims, ((), ())), preferred_element_type=jnp.float32)


def product(left, right):
    lh, ll = left
    rh, rl = right
    return dot(lh, rh) + (dot(lh, rl) + dot(ll, rh))


def places(blk):
    rows = lax.broadcasted_iota(jnp.int32, (blk, blk), 0)
    cols = lax.broadcasted_iota(jnp.int32, (blk, blk), 1)
    return rows, cols


def pack(first, second):
    blk = first.shape[0]
    rows, cols = places(blk)
    body = jnp.where(rows <= cols, first, second)
    diag = jnp.sum(jnp.where(rows == cols, second, 0.0), axis=0, keepdims=True)
    return body, jnp.broadcast_to(diag, (PAD, blk))


def put_diag(ref, diag):
    wide = ref.shape[1]
    for k in range(ref.shape[0]):
        ref[k : k + 1, :] = diag[:1, k * wide : (k + 1) * wide]


def get_diag(ref):
    return jnp.concatenate([ref[k : k + 1, :] for k in range(ref.shape[0])], axis=1)


def unpack(body, diag):
    blk = body.shape[0]
    rows, cols = places(blk)
    turned = body.T
    first = jnp.where(rows <= cols, body, turned)
    second = jnp.where(rows > cols, body, jnp.where(rows == cols, diag, turned))
    return first, second


def right_gram_kernel(g_ref, *rest):
    out_refs = rest[-2:]
    step = pl.program_id(0)
    blk = g_ref.shape[1] // 2
    high, low = split(g_ref[...])
    grams = []
    for b in range(2):
        hb = high[:, b * blk : (b + 1) * blk]
        lb = low[:, b * blk : (b + 1) * blk]
        both = dot(hb, hb, ((0,), (0,)))
        cross = dot(hb, lb, ((0,), (0,)))
        grams.append(both + (cross + cross.T))
    body, diag = pack(*grams)

    for at, ref in enumerate(out_refs):

        @pl.when(step == at)
        def _():
            ref[:blk, :] = body
            ref[blk:, :] = diag


def right_grams(tile, blk, flips, *after):
    rows = tile.shape[0]
    tall = blk + PAD
    flip = lambda s: jnp.where(s == 0, flips[0], flips[1])
    return pl.pallas_call(
        right_gram_kernel,
        out_shape=(jax.ShapeDtypeStruct((tall, blk), jnp.float32),) * 2,
        grid_spec=pltpu.PrefetchScalarGridSpec(
            num_scalar_prefetch=0,
            grid=(2,),
            in_specs=[
                pl.BlockSpec((rows, 2 * blk), placed(lambda s, place: (0, place[0] ^ flip(s)))),
            ]
            + [pl.BlockSpec(memory_space=pl.ANY)] * len(after),
            out_specs=(pl.BlockSpec((tall, blk), lambda s: (0, 0)),) * 2,
        ),
        compiler_params=pltpu.CompilerParams(vmem_limit_bytes=VMEM_LIMIT),
        cost_estimate=SMALL,
        name="right_grams",
    )(tile, *after)


def left_gram_kernel(g_ref, after_ref, out_ref, diag_ref, lhh, lcross):
    step = pl.program_id(0)
    last = pl.num_programs(0) - 1
    blk = lhh.shape[-1]
    high, low = split(g_ref[...])
    for i in range(2):
        hi = high[i * blk : (i + 1) * blk, :]
        lo = low[i * blk : (i + 1) * blk, :]
        both = dot(hi, hi, ((1,), (1,)))
        cross = dot(lo, hi, ((1,), (1,)))

        @pl.when(step == 0)
        def _():
            lhh[i] = both
            lcross[i] = cross

        @pl.when(step > 0)
        def _():
            lhh[i] += both
            lcross[i] += cross

    @pl.when(step == last)
    def _():
        body, diag = pack(*(lhh[b] + (lcross[b] + lcross[b].T) for b in range(2)))
        out_ref[...] = body
        put_diag(diag_ref, diag)


def left_grams(tile, blk, at, after):
    width = tile.shape[1]
    half = blk // 2
    return pl.pallas_call(
        left_gram_kernel,
        out_shape=(
            jax.ShapeDtypeStruct((blk, blk), jnp.float32),
            jax.ShapeDtypeStruct((2, half), jnp.float32),
        ),
        grid_spec=pltpu.PrefetchScalarGridSpec(
            num_scalar_prefetch=0,
            grid=(width // (4 * blk),),
            in_specs=[
                pl.BlockSpec((2 * blk, 4 * blk), placed(lambda s, place: (at(place), s))),
                pl.BlockSpec(memory_space=pl.ANY),
            ],
            out_specs=(pl.BlockSpec((blk, blk), lambda s: (0, 0)), pl.BlockSpec((2, half), lambda s: (0, 0))),
            scratch_shapes=[
                pltpu.VMEM((2, blk, blk), jnp.float32),
                pltpu.VMEM((2, blk, blk), jnp.float32),
            ],
        ),
        compiler_params=pltpu.CompilerParams(vmem_limit_bytes=VMEM_LIMIT),
        cost_estimate=SMALL,
        name="left_grams",
    )(tile, after)


RAW = (1, 3)


def own_first(place):
    return place[0] * 2


def core_first(place):
    return (place[0] ^ 1) * 2


def later(k, place):
    return jnp.where(place[0] < 2, 4 + k, jnp.where(k < 2, 2 * k, 2 * k + 1))


def take_kernel(block, g_ref, *rest):
    out_ref, sems = rest[-2:]
    rows, blk = out_ref.shape
    count = sems.shape[0]
    part = rows // count
    copies = []
    for k in range(count):
        top = pl.multiple_of((1 - here()[1]) * rows + k * part, part)
        source = g_ref.at[pl.ds(top, part), pl.ds(block * blk, blk)]
        copies.append(pltpu.make_async_copy(source, out_ref.at[pl.ds(k * part, part), :], sems.at[k]))
        copies[k].start()
    for copy in copies:
        copy.wait()


def take(tile, blk, block, count, *after):
    anywhere = pl.BlockSpec(memory_space=pl.ANY)
    return pl.pallas_call(
        functools.partial(take_kernel, block),
        out_shape=jax.ShapeDtypeStruct((tile.shape[0] // 2, blk), jnp.float32),
        in_specs=[anywhere] * (1 + len(after)),
        out_specs=anywhere,
        scratch_shapes=[pltpu.SemaphoreType.DMA((count,))],
        compiler_params=pltpu.CompilerParams(vmem_limit_bytes=VMEM_LIMIT),
        cost_estimate=SMALL,
        name="take",
    )(tile, *after)


def load_kernel(g_ref, after_ref, out_ref, sems):
    count = sems.shape[0]
    part = g_ref.shape[0] // count
    copies = []
    for k in range(count):
        rows = pl.ds(k * part, part)
        copies.append(pltpu.make_async_copy(g_ref.at[rows, :], out_ref.at[rows, :], sems.at[k]))
        copies[k].start()
    for copy in copies:
        copy.wait()


def load(tile, after):
    anywhere = pl.BlockSpec(memory_space=pl.ANY)
    return pl.pallas_call(
        load_kernel,
        out_shape=jax.ShapeDtypeStruct(tile.shape, jnp.float32),
        in_specs=[anywhere, anywhere],
        out_specs=anywhere,
        scratch_shapes=[pltpu.SemaphoreType.DMA((4,))],
        compiler_params=pltpu.CompilerParams(vmem_limit_bytes=VMEM_LIMIT),
        cost_estimate=SMALL,
        name="load",
    )(tile, after)


def fold_kernel(a_ref, b_ref, out_ref):
    out_ref[...] = a_ref[...] + b_ref[...]


def fold(kept, near):
    return pl.pallas_call(
        fold_kernel,
        out_shape=jax.ShapeDtypeStruct(kept.shape, jnp.float32),
        compiler_params=pltpu.CompilerParams(vmem_limit_bytes=VMEM_LIMIT),
        cost_estimate=SMALL,
        name="fold",
    )(kept, near)


def hold_kernel(a_ref, *rest):
    out_ref = rest[-1]
    out_ref[...] = a_ref[...]


def hold(value, *after):
    return pl.pallas_call(
        hold_kernel,
        out_shape=jax.ShapeDtypeStruct(value.shape, jnp.float32),
        in_specs=[pl.BlockSpec(memory_space=pltpu.VMEM)] + [pl.BlockSpec(memory_space=pl.ANY)] * len(after),
        compiler_params=pltpu.CompilerParams(vmem_limit_bytes=VMEM_LIMIT),
        cost_estimate=SMALL,
        name="hold",
    )(value, *after)


def pair_roots(full_dim, stats_ref, body, diag):
    blk = body.shape[0]
    rows, cols = places(blk)
    ident = jnp.where(rows == cols, 1.0, 0.0)
    moving, scales = [], []
    for b, gram in enumerate(unpack(body, diag)):
        factor = (
            beta_mix * stats_ref[b * blk : (b + 1) * blk, :]
            + (1.0 - beta_mix) * (gram / full_dim)
            + eps_shift * ident
        )
        scale = jnp.sqrt(jnp.sum(factor * factor, keepdims=True))
        moving.append(factor / scale)
        scales.append(scale)
    result = None
    for count in range(ITERS):
        steps = [(5.0 * ident - m) * 0.25 for m in moving]
        parts = [split(s) for s in steps]
        if result is None:
            result = steps
        else:
            result = [product(split(r), p) for r, p in zip(result, parts)]
        if count < ITERS - 1:
            squared = [split(product(p, p)) for p in parts]
            fourth = [split(product(s, s)) for s in squared]
            moving = [product(f, split(m)) for f, m in zip(fourth, moving)]
    return [r * jnp.exp(-0.25 * jnp.log(s)) for r, s in zip(result, scales)]


def right_kernel(full_dim, stats_ref, a_ref, b_ref, c_ref, g_ref, out_ref, half_ref):
    blk = stats_ref.shape[1]
    total = a_ref[...] + b_ref[...] + c_ref[...]
    roots = pair_roots(full_dim, stats_ref, total[:blk], total[blk : blk + 1])
    half_ref[...] = product(split(g_ref[...]), split(roots[0]))
    body, diag = pack(*roots)
    out_ref[:blk, :] = body
    out_ref[blk:, :] = diag


def right_roots(full_dim, stats, kept, near, far, tile):
    blk = stats.shape[1]
    tall = blk + PAD
    rows = tile.shape[0] // 2
    flat = pl.BlockSpec((tall, blk), lambda s: (0, 0))
    return pl.pallas_call(
        functools.partial(right_kernel, full_dim),
        out_shape=(
            jax.ShapeDtypeStruct((tall, blk), jnp.float32),
            jax.ShapeDtypeStruct((rows, blk), jnp.float32),
        ),
        grid_spec=pltpu.PrefetchScalarGridSpec(
            num_scalar_prefetch=0,
            grid=(1,),
            in_specs=[
                pl.BlockSpec((2 * blk, blk), placed(lambda s, place: (place[0], 0))),
                flat,
                flat,
                flat,
                pl.BlockSpec((rows, blk), placed(lambda s, place: (1 - place[1], own_first(place)))),
            ],
            out_specs=(
                flat,
                pl.BlockSpec((rows, blk), lambda s: (0, 0)),
            ),
        ),
        compiler_params=pltpu.CompilerParams(vmem_limit_bytes=VMEM_LIMIT),
        cost_estimate=SMALL,
        name="right_roots",
    )(stats, kept, near, far, tile)


def left_kernel(full_dim, stats_ref, a_ref, a_diag, b_ref, rest_ref, after_ref, out_ref):
    blk = stats_ref.shape[1]
    at = rest_ref.shape[0] - PAD + 1
    body = a_ref[...] + b_ref[b_ref.shape[0] - blk :, :]
    for b, root in enumerate(pair_roots(full_dim, stats_ref, body, get_diag(a_diag) + rest_ref[at : at + 1, :])):
        high, low = split(root)
        out_ref[b, 0] = high
        out_ref[b, 1] = low


def left_roots(full_dim, stats, after, *parts):
    blk = stats.shape[1]
    return pl.pallas_call(
        functools.partial(left_kernel, full_dim),
        out_shape=jax.ShapeDtypeStruct((2, 2, blk, blk), jnp.bfloat16),
        grid_spec=pltpu.PrefetchScalarGridSpec(
            num_scalar_prefetch=0,
            grid=(1,),
            in_specs=[pl.BlockSpec((2 * blk, blk), placed(lambda s, place: (place[1], 0)))]
            + [pl.BlockSpec(part.shape, lambda s: (0, 0)) for part in parts]
            + [pl.BlockSpec(memory_space=pl.ANY)],
            out_specs=pl.BlockSpec((2, 2, blk, blk), lambda s: (0, 0, 0, 0)),
        ),
        compiler_params=pltpu.CompilerParams(vmem_limit_bytes=VMEM_LIMIT),
        cost_estimate=SMALL,
        name="left_roots",
    )(stats, *parts, after)


def put_roots(out_ref, at, roots):
    for b, root in enumerate(roots):
        high, low = split(root)
        out_ref[at + b, 0] = high
        out_ref[at + b, 1] = low


def spread_kernel(own_ref, c_ref, x_ref, xc_ref, ldiag_ref, out_ref, cut_ref, seconds, body):
    blk = out_ref.shape[-1]
    r = here()[0]
    for flip, ref in enumerate((own_ref, c_ref, x_ref, xc_ref)):
        roots = unpack(ref[:blk, :], ref[blk : blk + 1, :])
        put_roots(out_ref, 2 * (r ^ flip), roots)
        seconds[r ^ flip] = roots[1]
    part = cut_ref.shape[0] - PAD
    body[...], diag = pack(seconds[RAW[0] // 2], seconds[RAW[1] // 2])
    cut_ref[:part, :] = body[pl.ds(pl.multiple_of(r * part, part), part), :]
    which = lax.broadcasted_iota(jnp.int32, diag.shape, 0)
    cut_ref[part:, :] = jnp.where(which == 1, get_diag(ldiag_ref), diag)


def spread_roots(ldiag, *packed):
    blk = packed[0].shape[1]
    count = len(packed)
    return pl.pallas_call(
        spread_kernel,
        out_shape=(
            jax.ShapeDtypeStruct((2 * count, 2, blk, blk), jnp.bfloat16),
            jax.ShapeDtypeStruct((blk // count + PAD, blk), jnp.float32),
        ),
        scratch_shapes=[pltpu.VMEM((count, blk, blk), jnp.float32), pltpu.VMEM((blk, blk), jnp.float32)],
        compiler_params=pltpu.CompilerParams(vmem_limit_bytes=VMEM_LIMIT),
        cost_estimate=SMALL,
        name="spread_roots",
    )(*packed, ldiag)


def rest_kernel(a_ref, out_ref):
    out_ref[...] = a_ref[a_ref.shape[0] - out_ref.shape[0] :, :]


def rest_of(value, rows):
    return pl.pallas_call(
        rest_kernel,
        out_shape=jax.ShapeDtypeStruct((value.shape[0] - rows, value.shape[1]), jnp.float32),
        compiler_params=pltpu.CompilerParams(vmem_limit_bytes=VMEM_LIMIT),
        cost_estimate=SMALL,
        name="rest_of",
    )(value)


def join_kernel(own_ref, c_ref, x_ref, xc_ref, out_ref, body):
    part = own_ref.shape[0] - PAD
    r = here()[0]
    for flip, ref in enumerate((own_ref, c_ref, x_ref, xc_ref)):
        body[pl.ds(pl.multiple_of((r ^ flip) * part, part), part), :] = ref[:part, :]
    put_roots(out_ref, 0, unpack(body[...], own_ref[part : part + 1, :]))


def join_roots(*parts):
    blk = parts[0].shape[1]
    return pl.pallas_call(
        join_kernel,
        out_shape=jax.ShapeDtypeStruct((2, 2, blk, blk), jnp.bfloat16),
        scratch_shapes=[pltpu.VMEM((blk, blk), jnp.float32)],
        compiler_params=pltpu.CompilerParams(vmem_limit_bytes=VMEM_LIMIT),
        cost_estimate=SMALL,
        name="join_roots",
    )(*parts)


def core_apply_kernel(g_ref, packed_ref, under_ref, out_ref):
    rows, blk = g_ref.shape
    root = unpack(packed_ref[:blk, :], packed_ref[blk : blk + 1, :])[0]
    out_ref[:rows, :] = product(split(g_ref[...]), split(root))
    out_ref[rows:, :] = under_ref[...]


def core_apply(tile, packed, under):
    rows = tile.shape[0] // 2
    tall, blk = packed.shape
    return pl.pallas_call(
        core_apply_kernel,
        out_shape=jax.ShapeDtypeStruct((rows + blk, blk), jnp.float32),
        grid_spec=pltpu.PrefetchScalarGridSpec(
            num_scalar_prefetch=0,
            grid=(1,),
            in_specs=[
                pl.BlockSpec((rows, blk), placed(lambda s, place: (1 - place[1], core_first(place)))),
                pl.BlockSpec((tall, blk), lambda s: (0, 0)),
                pl.BlockSpec((blk, blk), lambda s: (0, 0)),
            ],
            out_specs=pl.BlockSpec((rows + blk, blk), lambda s: (0, 0)),
        ),
        compiler_params=pltpu.CompilerParams(vmem_limit_bytes=VMEM_LIMIT),
        cost_estimate=SMALL,
        name="core_apply",
    )(tile, packed, under)


def right_apply_kernel(pieces, carries, g_ref, right_ref, *rest):
    out_refs = rest[-len(pieces) :]
    value = product(split(g_ref[...]), (right_ref[0, 0], right_ref[0, 1]))
    for (top, rows, start, width), ref in zip(pieces, out_refs):
        ref[:rows, :] = value[top : top + rows, start : start + width]
    if carries:
        out_refs[0][value.shape[0] :, :] = rest[0][...]


def right_apply(tile, right, k, pieces, under, after):
    rows = tile.shape[0] // 2
    blk = right.shape[-1]
    pieces = pieces or ((0, rows, 0, blk),)
    in_specs = [
        pl.BlockSpec((rows, blk), placed(lambda s, place: (1 - place[1], later(k, place)))),
        pl.BlockSpec((1, 2, blk, blk), placed(lambda s, place: (later(k, place), 0, 0, 0))),
    ]
    operands = [tile, right]
    more = 0
    if under is not None:
        more = under.shape[0]
        in_specs.append(pl.BlockSpec(under.shape, lambda s: (0, 0)))
        operands.append(under)
    shapes = [(tall + more, width) for _, tall, _, width in pieces]
    return pl.pallas_call(
        functools.partial(right_apply_kernel, pieces, under is not None),
        out_shape=tuple(jax.ShapeDtypeStruct(shape, jnp.float32) for shape in shapes),
        grid_spec=pltpu.PrefetchScalarGridSpec(
            num_scalar_prefetch=0,
            grid=(1,),
            in_specs=in_specs + [pl.BlockSpec(memory_space=pl.ANY)] * len(after),
            out_specs=tuple(pl.BlockSpec(shape, lambda s: (0, 0)) for shape in shapes),
        ),
        compiler_params=pltpu.CompilerParams(vmem_limit_bytes=VMEM_LIMIT),
        cost_estimate=SMALL,
        name="right_apply",
    )(*operands, *after)


def left_product(left_ref, value, out_ref):
    blk = left_ref.shape[-1]
    for i in range(value.shape[0] // blk):
        part = split(value[i * blk : (i + 1) * blk])
        out_ref[i * blk : (i + 1) * blk, :] = product((left_ref[i, 0], left_ref[i, 1]), part)


def update_kernel(g_ref, left_ref, right_ref, *rest):
    half = product(split(g_ref[...]), (right_ref[0, 0], right_ref[0, 1]))
    left_product(left_ref, half, rest[-2])
    rest[-1][...] = jnp.zeros_like(rest[-1])


def finish_kernel(column, first, half_ref, left_ref, out_before, out_ref, stage, sems):
    blk = left_ref.shape[-1]
    width = stage.shape[1]
    cols = pl.ds(pl.multiple_of(column(here()), width), width)
    copies = []
    for i in range(stage.shape[0] // blk):
        rows = pl.ds(i * blk, blk)
        root = (left_ref[first + i, 0], left_ref[first + i, 1])
        stage[rows, :] = product(root, split(half_ref[rows, :]))
        copies.append(
            pltpu.make_async_copy(stage.at[rows, :], out_ref.at[pl.ds((first + i) * blk, blk), cols], sems.at[i])
        )
        copies[i].start()
    for copy in copies:
        copy.wait()


def finish(half, left, out, column, first=0, count=2):
    width = half.shape[1]
    blk = left.shape[-1]
    vmem = pl.BlockSpec(memory_space=pltpu.VMEM)
    anywhere = pl.BlockSpec(memory_space=pl.ANY)
    return pl.pallas_call(
        functools.partial(finish_kernel, column, first),
        out_shape=jax.ShapeDtypeStruct(out.shape, jnp.float32),
        in_specs=[vmem, vmem, anywhere],
        out_specs=anywhere,
        scratch_shapes=[pltpu.VMEM((count * blk, width), jnp.float32), pltpu.SemaphoreType.DMA((count,))],
        input_output_aliases={2: 0},
        compiler_params=pltpu.CompilerParams(vmem_limit_bytes=VMEM_LIMIT),
        cost_estimate=SMALL,
        name="finish",
    )(half, left, out)


def update(source, left, right, out, out_shape, g_map, out_map, first=0, count=None, after=()):
    rows = out_shape[0]
    blk = left.shape[-1]
    in_specs = [
        pl.BlockSpec((rows, blk), placed(g_map)),
        pl.BlockSpec((2, 2, blk, blk), lambda s: (0, 0, 0, 0)),
        pl.BlockSpec((1, 2, blk, blk), lambda s: (first + s, 0, 0, 0)),
    ]
    operands = [source, left, right]
    aliases = {}
    if out is not None:
        aliases = {len(operands): 0}
        in_specs.append(pl.BlockSpec(memory_space=pl.ANY))
        operands.append(out)
    in_specs += [pl.BlockSpec(memory_space=pl.ANY)] * len(after)
    return pl.pallas_call(
        update_kernel,
        out_shape=(jax.ShapeDtypeStruct(out_shape, jnp.float32), jax.ShapeDtypeStruct((8, 128), jnp.float32)),
        grid_spec=pltpu.PrefetchScalarGridSpec(
            num_scalar_prefetch=0,
            grid=(count or right.shape[0],),
            in_specs=in_specs,
            out_specs=(pl.BlockSpec((rows, blk), placed(out_map)), pl.BlockSpec((8, 128), lambda s: (0, 0))),
        ),
        input_output_aliases=aliases,
        compiler_params=pltpu.CompilerParams(vmem_limit_bytes=VMEM_LIMIT),
        cost_estimate=SMALL,
        name="update",
    )(*operands, *after)


def exchange_device(full_dim, n_row, grads, left_stats, right_stats):
    tile_rows, tile_cols = grads.shape[1:]
    blk = left_stats.shape[2]
    tile = pltpu.with_memory_space_constraint(grads.reshape(tile_rows, tile_cols), pltpu.HBM)
    lstats = left_stats.reshape(tile_rows, blk)
    rstats = right_stats.reshape(tile_cols, blk)
    rows = tile_rows // 2
    shape = (rows, 2 * tile_cols)
    halves = tile_cols // blk

    def over(axis, value):
        if axis == "y":
            return lax.ppermute(value, "col", [(0, 1), (1, 0)])
        flip = {"core": 1, "x": 2}[axis]
        return lax.ppermute(value, "row", [(i, i ^ flip) for i in range(n_row)])

    first = take(tile, blk, RAW[0], 1)
    raw = [over("y", first)]
    tile = load(tile, first)

    send_on, keep_on = right_grams(tile, blk, (3, 2), first)
    far = fold(keep_on, over("core", send_on))
    raw.append(over("y", take(tile, blk, RAW[1], 16, send_on)))
    send, keep = right_grams(tile, blk, (1, 0), far, raw[0])
    near = over("core", send)
    far = over("x", far)

    own, half = right_roots(full_dim, rstats, keep, near, far, tile)
    came_a = over("y", half)
    lsend, ldiag = left_grams(tile, blk, lambda place: 1 - place[1], half)
    own = hold(own, raw[1], lsend)
    own_c = over("core", own)
    own_x = over("x", own)
    half = core_apply(tile, own_c, lsend)
    came_b = over("y", half)
    own_x = hold(own_x, half, came_a)
    lkeep, kdiag = left_grams(tile, blk, lambda place: place[1], half)
    roots, part = spread_roots(ldiag, own, own_c, own_x, over("core", own_x))

    (half,) = right_apply(tile, roots, 0, None, part, (lkeep,))
    came_c = over("y", half)
    (half,) = right_apply(tile, roots, 1, None, None, (came_b,))
    came_d = over("y", half)

    def crossed(block, start=0):
        return lambda place: (1 - place[1]) * tile_cols + block(place) * blk + start

    (half,) = right_apply(tile, roots, 2, None, None, (came_c,))
    came_e = over("y", half)
    left = left_roots(full_dim, lstats, half, lkeep, kdiag, came_b, came_c)
    out, done = update(
        tile, left, roots, None, shape,
        lambda s, place: (place[1], s),
        lambda s, place: (0, place[1] * halves + s),
    )
    wide = blk // 2
    last = ((0, rows, 0, wide), (0, blk, wide, wide), (blk, blk, wide, wide))
    held = right_apply(tile, roots, 3, last, None, (came_d, done))
    came_last = [over("y", half) for half in held]
    out = finish(came_a, left, out, crossed(own_first))
    out = finish(came_b, left, out, crossed(core_first))
    part = rest_of(came_c, rows)
    part_x = over("x", part)
    roots_raw = join_roots(part, over("core", part), part_x, over("core", part_x))
    for k, (block, value) in enumerate(zip(RAW, raw)):
        out, done = update(
            value, left, roots_raw, out, shape,
            lambda s, place: (0, 0),
            lambda s, place, block=block: (0, (1 - place[1]) * halves + block),
            k, 1, held[:1],
        )
    for k, value in enumerate((came_c, came_d, came_e)):
        out = finish(value, left, out, crossed(functools.partial(later, k)))
    for (top, tall, start, _), value in zip(last, came_last):
        out = finish(value, left, out, crossed(functools.partial(later, 3), start), top // blk, tall // blk)
    return out.reshape(1, rows, 2 * tile_cols)


def per_device(n_row, n_col, grads, left_stats, right_stats):
    mats, tile_rows, tile_cols = grads.shape
    blk = left_stats.shape[2]
    full_dim = tile_cols * n_col
    if mats == 1 and n_col == 2 and n_row == 4 and tile_rows == 4 * blk and tile_cols == 8 * blk:
        return exchange_device(full_dim, n_row, grads, left_stats, right_stats)
    return general_device(full_dim, grads, left_stats, right_stats)


def solution(mesh):
    return jax.shard_map(
        functools.partial(per_device, mesh.shape["row"], mesh.shape["col"]),
        mesh=mesh,
        in_specs=(P("mat", "row", "col"), P("mat", "row", None), P("mat", "col", None)),
        out_specs=P("mat", ("row", "col"), None),
        check_vma=False,
    )
```

```python
import functools

import jax
import jax.numpy as jnp
from jax import lax
from jax.experimental import pallas as pl
from jax.experimental.pallas import tpu as pltpu
from jax.sharding import PartitionSpec as P

ITERS = 3
beta_mix = 0.5
eps_shift = 0.001
PAD = 8
VMEM_LIMIT = 24 * 1024 * 1024
SMALL = pl.CostEstimate(flops=1, bytes_accessed=1, transcendentals=0)


def matmul(left, right):
    return jnp.einsum("...ij,...jk->...ik", left, right, precision=lax.Precision.HIGHEST)


def newton_root(factor):
    size = factor.shape[-1]
    ident = jnp.eye(size, dtype=jnp.float32)
    scale = jnp.sqrt(jnp.sum(factor * factor, axis=(-2, -1), keepdims=True))
    moving = factor / scale
    result = jnp.broadcast_to(ident, factor.shape)
    for count in range(ITERS):
        step_mat = (5.0 * ident - moving) * 0.25
        result = matmul(result, step_mat)
        squared = matmul(step_mat, step_mat)
        moving = matmul(matmul(squared, squared), moving)
    return result * jnp.power(scale, -0.25)


def general_device(full_dim, grads, left_stats, right_stats):
    mats, tile_rows, tile_cols = grads.shape
    blk = left_stats.shape[2]
    row_blocks = tile_rows // blk
    col_blocks = tile_cols // blk
    ident = jnp.eye(blk, dtype=jnp.float32)
    by_rows = grads.reshape(mats, row_blocks, blk, tile_cols)
    left_part = jnp.einsum("mibd,mied->mibe", by_rows, by_rows, precision=lax.Precision.HIGHEST) / full_dim
    by_cols = grads.reshape(mats, tile_rows, col_blocks, blk)
    right_part = (
        jnp.einsum("mdjb,mdje->mjbe", by_cols, by_cols, precision=lax.Precision.HIGHEST) / full_dim
    )
    left_gram = lax.psum(left_part, "col")
    right_gram = lax.psum(right_part, "row")
    left_factor = (
        beta_mix * left_stats.reshape(mats, row_blocks, blk, blk)
        + (1.0 - beta_mix) * left_gram
        + eps_shift * ident
    )
    right_factor = (
        beta_mix * right_stats.reshape(mats, col_blocks, blk, blk)
        + (1.0 - beta_mix) * right_gram
        + eps_shift * ident
    )
    left_root = newton_root(left_factor)
    right_root = newton_root(right_factor)
    half = jnp.einsum("mibe,mied->mibd", left_root, by_rows, precision=lax.Precision.HIGHEST)
    half = half.reshape(mats, tile_rows, col_blocks, blk)
    full = jnp.einsum("mdjb,mjbe->mdje", half, right_root, precision=lax.Precision.HIGHEST)
    full = full.reshape(mats, tile_rows, tile_cols)
    return lax.all_to_all(full, "col", split_axis=1, concat_axis=2, tiled=True)


def here():
    return lax.axis_index("row"), lax.axis_index("col")


def placed(index_map):
    return lambda s: index_map(s, here())


def split(value):
    high = value.astype(jnp.bfloat16)
    low = (value - high.astype(jnp.float32)).astype(jnp.bfloat16)
    return high, low


def dot(left, right, dims=((1,), (0,))):
    return lax.dot_general(left, right, (dims, ((), ())), preferred_element_type=jnp.float32)


def product(left, right):
    lh, ll = left
    rh, rl = right
    return dot(lh, rh) + (dot(lh, rl) + dot(ll, rh))


def places(blk):
    rows = lax.broadcasted_iota(jnp.int32, (blk, blk), 0)
    cols = lax.broadcasted_iota(jnp.int32, (blk, blk), 1)
    return rows, cols


def pack(first, second):
    blk = first.shape[0]
    rows, cols = places(blk)
    body = jnp.where(rows <= cols, first, second)
    diag = jnp.sum(jnp.where(rows == cols, second, 0.0), axis=0, keepdims=True)
    return body, jnp.broadcast_to(diag, (PAD, blk))


def unpack(body, diag):
    blk = body.shape[0]
    rows, cols = places(blk)
    turned = body.T
    first = jnp.where(rows <= cols, body, turned)
    second = jnp.where(rows > cols, body, jnp.where(rows == cols, diag, turned))
    return first, second


def right_gram_kernel(g_ref, *rest):
    out_refs = rest[-2:]
    step = pl.program_id(0)
    blk = g_ref.shape[1] // 2
    high, low = split(g_ref[...])
    grams = []
    for b in range(2):
        hb = high[:, b * blk : (b + 1) * blk]
        lb = low[:, b * blk : (b + 1) * blk]
        both = dot(hb, hb, ((0,), (0,)))
        cross = dot(hb, lb, ((0,), (0,)))
        grams.append(both + (cross + cross.T))
    body, diag = pack(*grams)

    for at, ref in enumerate(out_refs):

        @pl.when(step == at)
        def _():
            ref[:blk, :] = body
            ref[blk:, :] = diag


def right_grams(tile, blk, flips, *after):
    rows = tile.shape[0]
    tall = blk + PAD
    flip = lambda s: jnp.where(s == 0, flips[0], flips[1])
    return pl.pallas_call(
        right_gram_kernel,
        out_shape=(jax.ShapeDtypeStruct((tall, blk), jnp.float32),) * 2,
        grid_spec=pltpu.PrefetchScalarGridSpec(
            num_scalar_prefetch=0,
            grid=(2,),
            in_specs=[
                pl.BlockSpec((rows, 2 * blk), placed(lambda s, place: (0, place[0] ^ flip(s)))),
            ]
            + [pl.BlockSpec(memory_space=pl.ANY)] * len(after),
            out_specs=(pl.BlockSpec((tall, blk), lambda s: (0, 0)),) * 2,
        ),
        compiler_params=pltpu.CompilerParams(vmem_limit_bytes=VMEM_LIMIT),
        cost_estimate=SMALL,
        name="right_grams",
    )(tile, *after)


def left_gram_kernel(g_ref, after_ref, out_ref, lhh, lcross):
    step = pl.program_id(0)
    last = pl.num_programs(0) - 1
    blk = lhh.shape[-1]
    high, low = split(g_ref[...])
    for i in range(2):
        hi = high[i * blk : (i + 1) * blk, :]
        lo = low[i * blk : (i + 1) * blk, :]
        both = dot(hi, hi, ((1,), (1,)))
        cross = dot(lo, hi, ((1,), (1,)))

        @pl.when(step == 0)
        def _():
            lhh[i] = both
            lcross[i] = cross

        @pl.when(step > 0)
        def _():
            lhh[i] += both
            lcross[i] += cross

    @pl.when(step == last)
    def _():
        body, diag = pack(*(lhh[b] + (lcross[b] + lcross[b].T) for b in range(2)))
        out_ref[:blk, :] = body
        out_ref[blk:, :] = diag


def left_grams(tile, blk, at, after):
    width = tile.shape[1]
    tall = blk + PAD
    return pl.pallas_call(
        left_gram_kernel,
        out_shape=jax.ShapeDtypeStruct((tall, blk), jnp.float32),
        grid_spec=pltpu.PrefetchScalarGridSpec(
            num_scalar_prefetch=0,
            grid=(width // (4 * blk),),
            in_specs=[
                pl.BlockSpec((2 * blk, 4 * blk), placed(lambda s, place: (at(place), s))),
                pl.BlockSpec(memory_space=pl.ANY),
            ],
            out_specs=pl.BlockSpec((tall, blk), lambda s: (0, 0)),
            scratch_shapes=[
                pltpu.VMEM((2, blk, blk), jnp.float32),
                pltpu.VMEM((2, blk, blk), jnp.float32),
            ],
        ),
        compiler_params=pltpu.CompilerParams(vmem_limit_bytes=VMEM_LIMIT),
        cost_estimate=SMALL,
        name="left_grams",
    )(tile, after)


RAW = (1, 3)


def own_first(place):
    return place[0] * 2


def core_first(place):
    return (place[0] ^ 1) * 2


def later(k, place):
    return jnp.where(place[0] < 2, 4 + k, jnp.where(k < 2, 2 * k, 2 * k + 1))


def take_kernel(block, g_ref, *rest):
    out_ref, sems = rest[-2:]
    rows, blk = out_ref.shape
    count = sems.shape[0]
    part = rows // count
    copies = []
    for k in range(count):
        top = pl.multiple_of((1 - here()[1]) * rows + k * part, part)
        source = g_ref.at[pl.ds(top, part), pl.ds(block * blk, blk)]
        copies.append(pltpu.make_async_copy(source, out_ref.at[pl.ds(k * part, part), :], sems.at[k]))
        copies[k].start()
    for copy in copies:
        copy.wait()


def take(tile, blk, block, count, *after):
    anywhere = pl.BlockSpec(memory_space=pl.ANY)
    return pl.pallas_call(
        functools.partial(take_kernel, block),
        out_shape=jax.ShapeDtypeStruct((tile.shape[0] // 2, blk), jnp.float32),
        in_specs=[anywhere] * (1 + len(after)),
        out_specs=anywhere,
        scratch_shapes=[pltpu.SemaphoreType.DMA((count,))],
        compiler_params=pltpu.CompilerParams(vmem_limit_bytes=VMEM_LIMIT),
        cost_estimate=SMALL,
        name="take",
    )(tile, *after)


def load_kernel(g_ref, after_ref, out_ref, sems):
    count = sems.shape[0]
    part = g_ref.shape[0] // count
    copies = []
    for k in range(count):
        rows = pl.ds(k * part, part)
        copies.append(pltpu.make_async_copy(g_ref.at[rows, :], out_ref.at[rows, :], sems.at[k]))
        copies[k].start()
    for copy in copies:
        copy.wait()


def load(tile, after):
    anywhere = pl.BlockSpec(memory_space=pl.ANY)
    return pl.pallas_call(
        load_kernel,
        out_shape=jax.ShapeDtypeStruct(tile.shape, jnp.float32),
        in_specs=[anywhere, anywhere],
        out_specs=anywhere,
        scratch_shapes=[pltpu.SemaphoreType.DMA((4,))],
        compiler_params=pltpu.CompilerParams(vmem_limit_bytes=VMEM_LIMIT),
        cost_estimate=SMALL,
        name="load",
    )(tile, after)


def fold_kernel(a_ref, b_ref, out_ref):
    out_ref[...] = a_ref[...] + b_ref[...]


def fold(kept, near):
    return pl.pallas_call(
        fold_kernel,
        out_shape=jax.ShapeDtypeStruct(kept.shape, jnp.float32),
        compiler_params=pltpu.CompilerParams(vmem_limit_bytes=VMEM_LIMIT),
        cost_estimate=SMALL,
        name="fold",
    )(kept, near)


def hold_kernel(a_ref, *rest):
    out_ref = rest[-1]
    out_ref[...] = a_ref[...]


def hold(value, *after):
    return pl.pallas_call(
        hold_kernel,
        out_shape=jax.ShapeDtypeStruct(value.shape, jnp.float32),
        in_specs=[pl.BlockSpec(memory_space=pltpu.VMEM)] + [pl.BlockSpec(memory_space=pl.ANY)] * len(after),
        compiler_params=pltpu.CompilerParams(vmem_limit_bytes=VMEM_LIMIT),
        cost_estimate=SMALL,
        name="hold",
    )(value, *after)


def pair_roots(full_dim, stats_ref, body, diag):
    blk = body.shape[0]
    rows, cols = places(blk)
    ident = jnp.where(rows == cols, 1.0, 0.0)
    moving, scales = [], []
    for b, gram in enumerate(unpack(body, diag)):
        factor = (
            beta_mix * stats_ref[b * blk : (b + 1) * blk, :]
            + (1.0 - beta_mix) * (gram / full_dim)
            + eps_shift * ident
        )
        scale = jnp.sqrt(jnp.sum(factor * factor, keepdims=True))
        moving.append(factor / scale)
        scales.append(scale)
    result = None
    for count in range(ITERS):
        steps = [(5.0 * ident - m) * 0.25 for m in moving]
        parts = [split(s) for s in steps]
        if result is None:
            result = steps
        else:
            result = [product(split(r), p) for r, p in zip(result, parts)]
        if count < ITERS - 1:
            squared = [split(product(p, p)) for p in parts]
            fourth = [split(product(s, s)) for s in squared]
            moving = [product(f, split(m)) for f, m in zip(fourth, moving)]
    return [r * jnp.exp(-0.25 * jnp.log(s)) for r, s in zip(result, scales)]


def right_kernel(full_dim, stats_ref, a_ref, b_ref, c_ref, g_ref, out_ref, half_ref):
    blk = stats_ref.shape[1]
    total = a_ref[...] + b_ref[...] + c_ref[...]
    roots = pair_roots(full_dim, stats_ref, total[:blk], total[blk : blk + 1])
    half_ref[...] = product(split(g_ref[...]), split(roots[0]))
    body, diag = pack(*roots)
    out_ref[:blk, :] = body
    out_ref[blk:, :] = diag


def right_roots(full_dim, stats, kept, near, far, tile):
    blk = stats.shape[1]
    tall = blk + PAD
    rows = tile.shape[0] // 2
    flat = pl.BlockSpec((tall, blk), lambda s: (0, 0))
    return pl.pallas_call(
        functools.partial(right_kernel, full_dim),
        out_shape=(
            jax.ShapeDtypeStruct((tall, blk), jnp.float32),
            jax.ShapeDtypeStruct((rows, blk), jnp.float32),
        ),
        grid_spec=pltpu.PrefetchScalarGridSpec(
            num_scalar_prefetch=0,
            grid=(1,),
            in_specs=[
                pl.BlockSpec((2 * blk, blk), placed(lambda s, place: (place[0], 0))),
                flat,
                flat,
                flat,
                pl.BlockSpec((rows, blk), placed(lambda s, place: (1 - place[1], own_first(place)))),
            ],
            out_specs=(
                flat,
                pl.BlockSpec((rows, blk), lambda s: (0, 0)),
            ),
        ),
        compiler_params=pltpu.CompilerParams(vmem_limit_bytes=VMEM_LIMIT),
        cost_estimate=SMALL,
        name="right_roots",
    )(stats, kept, near, far, tile)


def left_kernel(full_dim, stats_ref, a_ref, b_ref, out_ref):
    blk = stats_ref.shape[1]
    total = a_ref[...] + b_ref[b_ref.shape[0] - a_ref.shape[0] :, :]
    for b, root in enumerate(pair_roots(full_dim, stats_ref, total[:blk], total[blk : blk + 1])):
        high, low = split(root)
        out_ref[b, 0] = high
        out_ref[b, 1] = low


def left_roots(full_dim, stats, kept, came):
    blk = stats.shape[1]
    tall = blk + PAD
    return pl.pallas_call(
        functools.partial(left_kernel, full_dim),
        out_shape=jax.ShapeDtypeStruct((2, 2, blk, blk), jnp.bfloat16),
        grid_spec=pltpu.PrefetchScalarGridSpec(
            num_scalar_prefetch=0,
            grid=(1,),
            in_specs=[
                pl.BlockSpec((2 * blk, blk), placed(lambda s, place: (place[1], 0))),
                pl.BlockSpec((tall, blk), lambda s: (0, 0)),
                pl.BlockSpec(came.shape, lambda s: (0, 0)),
            ],
            out_specs=pl.BlockSpec((2, 2, blk, blk), lambda s: (0, 0, 0, 0)),
        ),
        compiler_params=pltpu.CompilerParams(vmem_limit_bytes=VMEM_LIMIT),
        cost_estimate=SMALL,
        name="left_roots",
    )(stats, kept, came)


def put_roots(out_ref, at, roots):
    for b, root in enumerate(roots):
        high, low = split(root)
        out_ref[at + b, 0] = high
        out_ref[at + b, 1] = low


def spread_kernel(own_ref, c_ref, x_ref, xc_ref, out_ref, cut_ref, seconds, body):
    blk = out_ref.shape[-1]
    r = here()[0]
    for flip, ref in enumerate((own_ref, c_ref, x_ref, xc_ref)):
        roots = unpack(ref[:blk, :], ref[blk : blk + 1, :])
        put_roots(out_ref, 2 * (r ^ flip), roots)
        seconds[r ^ flip] = roots[1]
    part = cut_ref.shape[0] - PAD
    body[...], diag = pack(seconds[RAW[0] // 2], seconds[RAW[1] // 2])
    cut_ref[:part, :] = body[pl.ds(pl.multiple_of(r * part, part), part), :]
    cut_ref[part:, :] = diag


def spread_roots(*packed):
    blk = packed[0].shape[1]
    count = len(packed)
    return pl.pallas_call(
        spread_kernel,
        out_shape=(
            jax.ShapeDtypeStruct((2 * count, 2, blk, blk), jnp.bfloat16),
            jax.ShapeDtypeStruct((blk // count + PAD, blk), jnp.float32),
        ),
        scratch_shapes=[pltpu.VMEM((count, blk, blk), jnp.float32), pltpu.VMEM((blk, blk), jnp.float32)],
        compiler_params=pltpu.CompilerParams(vmem_limit_bytes=VMEM_LIMIT),
        cost_estimate=SMALL,
        name="spread_roots",
    )(*packed)


def rest_kernel(a_ref, out_ref):
    out_ref[...] = a_ref[a_ref.shape[0] - out_ref.shape[0] :, :]


def rest_of(value, rows):
    return pl.pallas_call(
        rest_kernel,
        out_shape=jax.ShapeDtypeStruct((value.shape[0] - rows, value.shape[1]), jnp.float32),
        compiler_params=pltpu.CompilerParams(vmem_limit_bytes=VMEM_LIMIT),
        cost_estimate=SMALL,
        name="rest_of",
    )(value)


def join_kernel(own_ref, c_ref, x_ref, xc_ref, out_ref, body):
    part = own_ref.shape[0] - PAD
    r = here()[0]
    for flip, ref in enumerate((own_ref, c_ref, x_ref, xc_ref)):
        body[pl.ds(pl.multiple_of((r ^ flip) * part, part), part), :] = ref[:part, :]
    put_roots(out_ref, 0, unpack(body[...], own_ref[part : part + 1, :]))


def join_roots(*parts):
    blk = parts[0].shape[1]
    return pl.pallas_call(
        join_kernel,
        out_shape=jax.ShapeDtypeStruct((2, 2, blk, blk), jnp.bfloat16),
        scratch_shapes=[pltpu.VMEM((blk, blk), jnp.float32)],
        compiler_params=pltpu.CompilerParams(vmem_limit_bytes=VMEM_LIMIT),
        cost_estimate=SMALL,
        name="join_roots",
    )(*parts)


def core_apply_kernel(g_ref, packed_ref, under_ref, out_ref):
    rows, blk = g_ref.shape
    root = unpack(packed_ref[:blk, :], packed_ref[blk : blk + 1, :])[0]
    out_ref[:rows, :] = product(split(g_ref[...]), split(root))
    out_ref[rows:, :] = under_ref[...]


def core_apply(tile, packed, under):
    rows = tile.shape[0] // 2
    tall, blk = packed.shape
    return pl.pallas_call(
        core_apply_kernel,
        out_shape=jax.ShapeDtypeStruct((rows + tall, blk), jnp.float32),
        grid_spec=pltpu.PrefetchScalarGridSpec(
            num_scalar_prefetch=0,
            grid=(1,),
            in_specs=[
                pl.BlockSpec((rows, blk), placed(lambda s, place: (1 - place[1], core_first(place)))),
                pl.BlockSpec((tall, blk), lambda s: (0, 0)),
                pl.BlockSpec((tall, blk), lambda s: (0, 0)),
            ],
            out_specs=pl.BlockSpec((rows + tall, blk), lambda s: (0, 0)),
        ),
        compiler_params=pltpu.CompilerParams(vmem_limit_bytes=VMEM_LIMIT),
        cost_estimate=SMALL,
        name="core_apply",
    )(tile, packed, under)


def right_apply_kernel(pieces, carries, g_ref, right_ref, *rest):
    out_refs = rest[-len(pieces) :]
    value = product(split(g_ref[...]), (right_ref[0, 0], right_ref[0, 1]))
    for (top, rows, start, width), ref in zip(pieces, out_refs):
        ref[:rows, :] = value[top : top + rows, start : start + width]
    if carries:
        out_refs[0][value.shape[0] :, :] = rest[0][...]


def right_apply(tile, right, k, pieces, under, after):
    rows = tile.shape[0] // 2
    blk = right.shape[-1]
    pieces = pieces or ((0, rows, 0, blk),)
    in_specs = [
        pl.BlockSpec((rows, blk), placed(lambda s, place: (1 - place[1], later(k, place)))),
        pl.BlockSpec((1, 2, blk, blk), placed(lambda s, place: (later(k, place), 0, 0, 0))),
    ]
    operands = [tile, right]
    more = 0
    if under is not None:
        more = under.shape[0]
        in_specs.append(pl.BlockSpec(under.shape, lambda s: (0, 0)))
        operands.append(under)
    shapes = [(tall + more, width) for _, tall, _, width in pieces]
    return pl.pallas_call(
        functools.partial(right_apply_kernel, pieces, under is not None),
        out_shape=tuple(jax.ShapeDtypeStruct(shape, jnp.float32) for shape in shapes),
        grid_spec=pltpu.PrefetchScalarGridSpec(
            num_scalar_prefetch=0,
            grid=(1,),
            in_specs=in_specs + [pl.BlockSpec(memory_space=pl.ANY)] * len(after),
            out_specs=tuple(pl.BlockSpec(shape, lambda s: (0, 0)) for shape in shapes),
        ),
        compiler_params=pltpu.CompilerParams(vmem_limit_bytes=VMEM_LIMIT),
        cost_estimate=SMALL,
        name="right_apply",
    )(*operands, *after)


def left_product(left_ref, value, out_ref):
    blk = left_ref.shape[-1]
    for i in range(value.shape[0] // blk):
        part = split(value[i * blk : (i + 1) * blk])
        out_ref[i * blk : (i + 1) * blk, :] = product((left_ref[i, 0], left_ref[i, 1]), part)


def update_kernel(g_ref, left_ref, right_ref, *rest):
    half = product(split(g_ref[...]), (right_ref[0, 0], right_ref[0, 1]))
    left_product(left_ref, half, rest[-2])
    rest[-1][...] = jnp.zeros_like(rest[-1])


def finish_kernel(column, first, half_ref, left_ref, out_before, out_ref, stage, sems):
    blk = left_ref.shape[-1]
    width = stage.shape[1]
    part = blk // 2
    cols = pl.ds(pl.multiple_of(column(here()), width), width)
    copies = []
    for i in range(stage.shape[0] // blk):
        value = split(half_ref[pl.ds(i * blk, blk), :])
        for k in range(2):
            root = tuple(left_ref[first + i, h, pl.ds(k * part, part), :] for h in range(2))
            rows = pl.ds(i * blk + k * part, part)
            stage[rows, :] = product(root, value)
            there = out_ref.at[pl.ds((first + i) * blk + k * part, part), cols]
            copies.append(pltpu.make_async_copy(stage.at[rows, :], there, sems.at[len(copies)]))
            copies[-1].start()
    for copy in copies:
        copy.wait()


def finish(half, left, out, column, first=0, count=2):
    width = half.shape[1]
    blk = left.shape[-1]
    vmem = pl.BlockSpec(memory_space=pltpu.VMEM)
    anywhere = pl.BlockSpec(memory_space=pl.ANY)
    return pl.pallas_call(
        functools.partial(finish_kernel, column, first),
        out_shape=jax.ShapeDtypeStruct(out.shape, jnp.float32),
        in_specs=[vmem, vmem, anywhere],
        out_specs=anywhere,
        scratch_shapes=[pltpu.VMEM((count * blk, width), jnp.float32), pltpu.SemaphoreType.DMA((2 * count,))],
        input_output_aliases={2: 0},
        compiler_params=pltpu.CompilerParams(vmem_limit_bytes=VMEM_LIMIT),
        cost_estimate=SMALL,
        name="finish",
    )(half, left, out)


def update(source, left, right, out, out_shape, g_map, out_map, first=0, count=None, after=()):
    rows = out_shape[0]
    blk = left.shape[-1]
    in_specs = [
        pl.BlockSpec((rows, blk), placed(g_map)),
        pl.BlockSpec((2, 2, blk, blk), lambda s: (0, 0, 0, 0)),
        pl.BlockSpec((1, 2, blk, blk), lambda s: (first + s, 0, 0, 0)),
    ]
    operands = [source, left, right]
    aliases = {}
    if out is not None:
        aliases = {len(operands): 0}
        in_specs.append(pl.BlockSpec(memory_space=pl.ANY))
        operands.append(out)
    in_specs += [pl.BlockSpec(memory_space=pl.ANY)] * len(after)
    return pl.pallas_call(
        update_kernel,
        out_shape=(jax.ShapeDtypeStruct(out_shape, jnp.float32), jax.ShapeDtypeStruct((8, 128), jnp.float32)),
        grid_spec=pltpu.PrefetchScalarGridSpec(
            num_scalar_prefetch=0,
            grid=(count or right.shape[0],),
            in_specs=in_specs,
            out_specs=(pl.BlockSpec((rows, blk), placed(out_map)), pl.BlockSpec((8, 128), lambda s: (0, 0))),
        ),
        input_output_aliases=aliases,
        compiler_params=pltpu.CompilerParams(vmem_limit_bytes=VMEM_LIMIT),
        cost_estimate=SMALL,
        name="update",
    )(*operands, *after)


def exchange_device(full_dim, n_row, grads, left_stats, right_stats):
    tile_rows, tile_cols = grads.shape[1:]
    blk = left_stats.shape[2]
    tile = pltpu.with_memory_space_constraint(grads.reshape(tile_rows, tile_cols), pltpu.HBM)
    lstats = left_stats.reshape(tile_rows, blk)
    rstats = right_stats.reshape(tile_cols, blk)
    rows = tile_rows // 2
    shape = (rows, 2 * tile_cols)
    halves = tile_cols // blk

    def over(axis, value):
        if axis == "y":
            return lax.ppermute(value, "col", [(0, 1), (1, 0)])
        flip = {"core": 1, "x": 2}[axis]
        return lax.ppermute(value, "row", [(i, i ^ flip) for i in range(n_row)])

    first = take(tile, blk, RAW[0], 1)
    raw = [over("y", first)]
    tile = load(tile, first)

    send_on, keep_on = right_grams(tile, blk, (3, 2), first)
    far = fold(keep_on, over("core", send_on))
    raw.append(over("y", take(tile, blk, RAW[1], 16, send_on)))
    send, keep = right_grams(tile, blk, (1, 0), far, raw[0])
    near = over("core", send)
    far = over("x", far)

    own, half = right_roots(full_dim, rstats, keep, near, far, tile)
    came_a = over("y", half)
    lsend = left_grams(tile, blk, lambda place: 1 - place[1], half)
    own = hold(own, raw[1], lsend)
    own_c = over("core", own)
    own_x = over("x", own)
    half = core_apply(tile, own_c, lsend)
    came_b = over("y", half)
    own_x = hold(own_x, half, came_a)
    lkeep = left_grams(tile, blk, lambda place: place[1], half)
    roots, part = spread_roots(own, own_c, own_x, over("core", own_x))

    (half,) = right_apply(tile, roots, 0, None, part, (lkeep,))
    came_c = over("y", half)
    (half,) = right_apply(tile, roots, 1, None, None, (came_b,))
    came_d = over("y", half)

    def crossed(block, start=0):
        return lambda place: (1 - place[1]) * tile_cols + block(place) * blk + start

    left = left_roots(full_dim, lstats, lkeep, came_b)
    out, done = update(
        tile, left, roots, None, shape,
        lambda s, place: (place[1], s),
        lambda s, place: (0, place[1] * halves + s),
    )
    (half,) = right_apply(tile, roots, 2, None, None, (came_c, done))
    came_e = over("y", half)
    wide = blk // 2
    last = ((0, rows, 0, wide), (0, blk, wide, wide), (blk, blk, wide, wide))
    held = right_apply(tile, roots, 3, last, None, (came_d,))
    came_last = [over("y", half) for half in held]
    out = finish(came_a, left, out, crossed(own_first))
    out = finish(came_b, left, out, crossed(core_first))
    part = rest_of(came_c, rows)
    part_x = over("x", part)
    roots_raw = join_roots(part, over("core", part), part_x, over("core", part_x))
    for k, (block, value) in enumerate(zip(RAW, raw)):
        out, done = update(
            value, left, roots_raw, out, shape,
            lambda s, place: (0, 0),
            lambda s, place, block=block: (0, (1 - place[1]) * halves + block),
            k, 1, held[:1],
        )
    for k, value in enumerate((came_c, came_d, came_e)):
        out = finish(value, left, out, crossed(functools.partial(later, k)))
    for (top, tall, start, _), value in zip(last, came_last):
        out = finish(value, left, out, crossed(functools.partial(later, 3), start), top // blk, tall // blk)
    return out.reshape(1, rows, 2 * tile_cols)


def per_device(n_row, n_col, grads, left_stats, right_stats):
    mats, tile_rows, tile_cols = grads.shape
    blk = left_stats.shape[2]
    full_dim = tile_cols * n_col
    if mats == 1 and n_col == 2 and n_row == 4 and tile_rows == 4 * blk and tile_cols == 8 * blk:
        return exchange_device(full_dim, n_row, grads, left_stats, right_stats)
    return general_device(full_dim, grads, left_stats, right_stats)


def solution(mesh):
    return jax.shard_map(
        functools.partial(per_device, mesh.shape["row"], mesh.shape["col"]),
        mesh=mesh,
        in_specs=(P("mat", "row", "col"), P("mat", "row", None), P("mat", "col", None)),
        out_specs=P("mat", ("row", "col"), None),
        check_vma=False,
    )
```

```python
import functools

import jax
import jax.numpy as jnp
from jax import lax
from jax.experimental import pallas as pl
from jax.experimental.pallas import tpu as pltpu
from jax.sharding import PartitionSpec as P

ITERS = 3
beta_mix = 0.5
eps_shift = 0.001
PAD = 8
VMEM_LIMIT = 24 * 1024 * 1024
SMALL = pl.CostEstimate(flops=1, bytes_accessed=1, transcendentals=0)


def matmul(left, right):
    return jnp.einsum("...ij,...jk->...ik", left, right, precision=lax.Precision.HIGHEST)


def newton_root(factor):
    size = factor.shape[-1]
    ident = jnp.eye(size, dtype=jnp.float32)
    scale = jnp.sqrt(jnp.sum(factor * factor, axis=(-2, -1), keepdims=True))
    moving = factor / scale
    result = jnp.broadcast_to(ident, factor.shape)
    for count in range(ITERS):
        step_mat = (5.0 * ident - moving) * 0.25
        result = matmul(result, step_mat)
        squared = matmul(step_mat, step_mat)
        moving = matmul(matmul(squared, squared), moving)
    return result * jnp.power(scale, -0.25)


def general_device(full_dim, grads, left_stats, right_stats):
    mats, tile_rows, tile_cols = grads.shape
    blk = left_stats.shape[2]
    row_blocks = tile_rows // blk
    col_blocks = tile_cols // blk
    ident = jnp.eye(blk, dtype=jnp.float32)
    by_rows = grads.reshape(mats, row_blocks, blk, tile_cols)
    left_part = jnp.einsum("mibd,mied->mibe", by_rows, by_rows, precision=lax.Precision.HIGHEST) / full_dim
    by_cols = grads.reshape(mats, tile_rows, col_blocks, blk)
    right_part = (
        jnp.einsum("mdjb,mdje->mjbe", by_cols, by_cols, precision=lax.Precision.HIGHEST) / full_dim
    )
    left_gram = lax.psum(left_part, "col")
    right_gram = lax.psum(right_part, "row")
    left_factor = (
        beta_mix * left_stats.reshape(mats, row_blocks, blk, blk)
        + (1.0 - beta_mix) * left_gram
        + eps_shift * ident
    )
    right_factor = (
        beta_mix * right_stats.reshape(mats, col_blocks, blk, blk)
        + (1.0 - beta_mix) * right_gram
        + eps_shift * ident
    )
    left_root = newton_root(left_factor)
    right_root = newton_root(right_factor)
    half = jnp.einsum("mibe,mied->mibd", left_root, by_rows, precision=lax.Precision.HIGHEST)
    half = half.reshape(mats, tile_rows, col_blocks, blk)
    full = jnp.einsum("mdjb,mjbe->mdje", half, right_root, precision=lax.Precision.HIGHEST)
    full = full.reshape(mats, tile_rows, tile_cols)
    return lax.all_to_all(full, "col", split_axis=1, concat_axis=2, tiled=True)


def here():
    return lax.axis_index("row"), lax.axis_index("col")


def placed(index_map):
    return lambda s: index_map(s, here())


def split(value):
    high = value.astype(jnp.bfloat16)
    low = (value - high.astype(jnp.float32)).astype(jnp.bfloat16)
    return high, low


def dot(left, right, dims=((1,), (0,))):
    return lax.dot_general(left, right, (dims, ((), ())), preferred_element_type=jnp.float32)


def product(left, right):
    lh, ll = left
    rh, rl = right
    return dot(lh, rh) + (dot(lh, rl) + dot(ll, rh))


def places(blk):
    rows = lax.broadcasted_iota(jnp.int32, (blk, blk), 0)
    cols = lax.broadcasted_iota(jnp.int32, (blk, blk), 1)
    return rows, cols


def pack(first, second):
    blk = first.shape[0]
    rows, cols = places(blk)
    body = jnp.where(rows <= cols, first, second)
    diag = jnp.sum(jnp.where(rows == cols, second, 0.0), axis=0, keepdims=True)
    return body, jnp.broadcast_to(diag, (PAD, blk))


def put_diag(ref, diag):
    wide = ref.shape[1]
    for k in range(ref.shape[0]):
        ref[k : k + 1, :] = diag[:1, k * wide : (k + 1) * wide]


def get_diag(ref):
    return jnp.concatenate([ref[k : k + 1, :] for k in range(ref.shape[0])], axis=1)


def unpack(body, diag):
    blk = body.shape[0]
    rows, cols = places(blk)
    turned = body.T
    first = jnp.where(rows <= cols, body, turned)
    second = jnp.where(rows > cols, body, jnp.where(rows == cols, diag, turned))
    return first, second


def right_gram_kernel(g_ref, *rest):
    out_refs = rest[-2:]
    step = pl.program_id(0)
    blk = g_ref.shape[1] // 2
    high, low = split(g_ref[...])
    grams = []
    for b in range(2):
        hb = high[:, b * blk : (b + 1) * blk]
        lb = low[:, b * blk : (b + 1) * blk]
        both = dot(hb, hb, ((0,), (0,)))
        cross = dot(hb, lb, ((0,), (0,)))
        grams.append(both + (cross + cross.T))
    body, diag = pack(*grams)

    for at, ref in enumerate(out_refs):

        @pl.when(step == at)
        def _():
            ref[:blk, :] = body
            ref[blk:, :] = diag


def right_grams(tile, blk, flips, *after):
    rows = tile.shape[0]
    tall = blk + PAD
    flip = lambda s: jnp.where(s == 0, flips[0], flips[1])
    return pl.pallas_call(
        right_gram_kernel,
        out_shape=(jax.ShapeDtypeStruct((tall, blk), jnp.float32),) * 2,
        grid_spec=pltpu.PrefetchScalarGridSpec(
            num_scalar_prefetch=0,
            grid=(2,),
            in_specs=[
                pl.BlockSpec((rows, 2 * blk), placed(lambda s, place: (0, place[0] ^ flip(s)))),
            ]
            + [pl.BlockSpec(memory_space=pl.ANY)] * len(after),
            out_specs=(pl.BlockSpec((tall, blk), lambda s: (0, 0)),) * 2,
        ),
        compiler_params=pltpu.CompilerParams(vmem_limit_bytes=VMEM_LIMIT),
        cost_estimate=SMALL,
        name="right_grams",
    )(tile, *after)


def left_gram_kernel(g_ref, after_ref, out_ref, diag_ref, lhh, lcross):
    step = pl.program_id(0)
    last = pl.num_programs(0) - 1
    blk = lhh.shape[-1]
    high, low = split(g_ref[...])
    for i in range(2):
        hi = high[i * blk : (i + 1) * blk, :]
        lo = low[i * blk : (i + 1) * blk, :]
        both = dot(hi, hi, ((1,), (1,)))
        cross = dot(lo, hi, ((1,), (1,)))

        @pl.when(step == 0)
        def _():
            lhh[i] = both
            lcross[i] = cross

        @pl.when(step > 0)
        def _():
            lhh[i] += both
            lcross[i] += cross

    @pl.when(step == last)
    def _():
        body, diag = pack(*(lhh[b] + (lcross[b] + lcross[b].T) for b in range(2)))
        out_ref[...] = body
        put_diag(diag_ref, diag)


def left_grams(tile, blk, at, after):
    width = tile.shape[1]
    half = blk // 2
    return pl.pallas_call(
        left_gram_kernel,
        out_shape=(
            jax.ShapeDtypeStruct((blk, blk), jnp.float32),
            jax.ShapeDtypeStruct((2, half), jnp.float32),
        ),
        grid_spec=pltpu.PrefetchScalarGridSpec(
            num_scalar_prefetch=0,
            grid=(width // (4 * blk),),
            in_specs=[
                pl.BlockSpec((2 * blk, 4 * blk), placed(lambda s, place: (at(place), s))),
                pl.BlockSpec(memory_space=pl.ANY),
            ],
            out_specs=(pl.BlockSpec((blk, blk), lambda s: (0, 0)), pl.BlockSpec((2, half), lambda s: (0, 0))),
            scratch_shapes=[
                pltpu.VMEM((2, blk, blk), jnp.float32),
                pltpu.VMEM((2, blk, blk), jnp.float32),
            ],
        ),
        compiler_params=pltpu.CompilerParams(vmem_limit_bytes=VMEM_LIMIT),
        cost_estimate=SMALL,
        name="left_grams",
    )(tile, after)


RAW = (1, 3)


def own_first(place):
    return place[0] * 2


def core_first(place):
    return (place[0] ^ 1) * 2


def later(k, place):
    return jnp.where(place[0] < 2, 4 + k, jnp.where(k < 2, 2 * k, 2 * k + 1))


def take_kernel(block, g_ref, *rest):
    out_ref, sems = rest[-2:]
    rows, blk = out_ref.shape
    count = sems.shape[0]
    part = rows // count
    copies = []
    for k in range(count):
        top = pl.multiple_of((1 - here()[1]) * rows + k * part, part)
        source = g_ref.at[pl.ds(top, part), pl.ds(block * blk, blk)]
        copies.append(pltpu.make_async_copy(source, out_ref.at[pl.ds(k * part, part), :], sems.at[k]))
        copies[k].start()
    for copy in copies:
        copy.wait()


def take(tile, blk, block, count, *after):
    anywhere = pl.BlockSpec(memory_space=pl.ANY)
    return pl.pallas_call(
        functools.partial(take_kernel, block),
        out_shape=jax.ShapeDtypeStruct((tile.shape[0] // 2, blk), jnp.float32),
        in_specs=[anywhere] * (1 + len(after)),
        out_specs=anywhere,
        scratch_shapes=[pltpu.SemaphoreType.DMA((count,))],
        compiler_params=pltpu.CompilerParams(vmem_limit_bytes=VMEM_LIMIT),
        cost_estimate=SMALL,
        name="take",
    )(tile, *after)


def load_kernel(g_ref, after_ref, out_ref, sems):
    count = sems.shape[0]
    part = g_ref.shape[0] // count
    copies = []
    for k in range(count):
        rows = pl.ds(k * part, part)
        copies.append(pltpu.make_async_copy(g_ref.at[rows, :], out_ref.at[rows, :], sems.at[k]))
        copies[k].start()
    for copy in copies:
        copy.wait()


def load(tile, after):
    anywhere = pl.BlockSpec(memory_space=pl.ANY)
    return pl.pallas_call(
        load_kernel,
        out_shape=jax.ShapeDtypeStruct(tile.shape, jnp.float32),
        in_specs=[anywhere, anywhere],
        out_specs=anywhere,
        scratch_shapes=[pltpu.SemaphoreType.DMA((4,))],
        compiler_params=pltpu.CompilerParams(vmem_limit_bytes=VMEM_LIMIT),
        cost_estimate=SMALL,
        name="load",
    )(tile, after)


def fold_kernel(a_ref, b_ref, out_ref):
    out_ref[...] = a_ref[...] + b_ref[...]


def fold(kept, near):
    return pl.pallas_call(
        fold_kernel,
        out_shape=jax.ShapeDtypeStruct(kept.shape, jnp.float32),
        compiler_params=pltpu.CompilerParams(vmem_limit_bytes=VMEM_LIMIT),
        cost_estimate=SMALL,
        name="fold",
    )(kept, near)


def hold_kernel(a_ref, *rest):
    out_ref = rest[-1]
    out_ref[...] = a_ref[...]


def hold(value, *after):
    return pl.pallas_call(
        hold_kernel,
        out_shape=jax.ShapeDtypeStruct(value.shape, jnp.float32),
        in_specs=[pl.BlockSpec(memory_space=pltpu.VMEM)] + [pl.BlockSpec(memory_space=pl.ANY)] * len(after),
        compiler_params=pltpu.CompilerParams(vmem_limit_bytes=VMEM_LIMIT),
        cost_estimate=SMALL,
        name="hold",
    )(value, *after)


def pair_roots(full_dim, stats_ref, body, diag):
    blk = body.shape[0]
    rows, cols = places(blk)
    ident = jnp.where(rows == cols, 1.0, 0.0)
    moving, scales = [], []
    for b, gram in enumerate(unpack(body, diag)):
        factor = (
            beta_mix * stats_ref[b * blk : (b + 1) * blk, :]
            + (1.0 - beta_mix) * (gram / full_dim)
            + eps_shift * ident
        )
        scale = jnp.sqrt(jnp.sum(factor * factor, keepdims=True))
        moving.append(factor / scale)
        scales.append(scale)
    result = None
    for count in range(ITERS):
        steps = [(5.0 * ident - m) * 0.25 for m in moving]
        parts = [split(s) for s in steps]
        if result is None:
            result = steps
        else:
            result = [product(split(r), p) for r, p in zip(result, parts)]
        if count < ITERS - 1:
            squared = [split(product(p, p)) for p in parts]
            fourth = [split(product(s, s)) for s in squared]
            moving = [product(f, split(m)) for f, m in zip(fourth, moving)]
    return [r * jnp.exp(-0.25 * jnp.log(s)) for r, s in zip(result, scales)]


def right_kernel(full_dim, stats_ref, a_ref, b_ref, c_ref, g_ref, out_ref, half_ref):
    blk = stats_ref.shape[1]
    total = a_ref[...] + b_ref[...] + c_ref[...]
    roots = pair_roots(full_dim, stats_ref, total[:blk], total[blk : blk + 1])
    half_ref[...] = product(split(g_ref[...]), split(roots[0]))
    body, diag = pack(*roots)
    out_ref[:blk, :] = body
    out_ref[blk:, :] = diag


def right_roots(full_dim, stats, kept, near, far, tile):
    blk = stats.shape[1]
    tall = blk + PAD
    rows = tile.shape[0] // 2
    flat = pl.BlockSpec((tall, blk), lambda s: (0, 0))
    return pl.pallas_call(
        functools.partial(right_kernel, full_dim),
        out_shape=(
            jax.ShapeDtypeStruct((tall, blk), jnp.float32),
            jax.ShapeDtypeStruct((rows, blk), jnp.float32),
        ),
        grid_spec=pltpu.PrefetchScalarGridSpec(
            num_scalar_prefetch=0,
            grid=(1,),
            in_specs=[
                pl.BlockSpec((2 * blk, blk), placed(lambda s, place: (place[0], 0))),
                flat,
                flat,
                flat,
                pl.BlockSpec((rows, blk), placed(lambda s, place: (1 - place[1], own_first(place)))),
            ],
            out_specs=(
                flat,
                pl.BlockSpec((rows, blk), lambda s: (0, 0)),
            ),
        ),
        compiler_params=pltpu.CompilerParams(vmem_limit_bytes=VMEM_LIMIT),
        cost_estimate=SMALL,
        name="right_roots",
    )(stats, kept, near, far, tile)


def left_kernel(full_dim, stats_ref, a_ref, a_diag, b_ref, rest_ref, after_ref, out_ref):
    blk = stats_ref.shape[1]
    at = rest_ref.shape[0] - PAD + 1
    body = a_ref[...] + b_ref[b_ref.shape[0] - blk :, :]
    for b, root in enumerate(pair_roots(full_dim, stats_ref, body, get_diag(a_diag) + rest_ref[at : at + 1, :])):
        high, low = split(root)
        out_ref[b, 0] = high
        out_ref[b, 1] = low


def left_roots(full_dim, stats, after, *parts):
    blk = stats.shape[1]
    return pl.pallas_call(
        functools.partial(left_kernel, full_dim),
        out_shape=jax.ShapeDtypeStruct((2, 2, blk, blk), jnp.bfloat16),
        grid_spec=pltpu.PrefetchScalarGridSpec(
            num_scalar_prefetch=0,
            grid=(1,),
            in_specs=[pl.BlockSpec((2 * blk, blk), placed(lambda s, place: (place[1], 0)))]
            + [pl.BlockSpec(part.shape, lambda s: (0, 0)) for part in parts]
            + [pl.BlockSpec(memory_space=pl.ANY)],
            out_specs=pl.BlockSpec((2, 2, blk, blk), lambda s: (0, 0, 0, 0)),
        ),
        compiler_params=pltpu.CompilerParams(vmem_limit_bytes=VMEM_LIMIT),
        cost_estimate=SMALL,
        name="left_roots",
    )(stats, *parts, after)


def put_roots(out_ref, at, roots):
    for b, root in enumerate(roots):
        high, low = split(root)
        out_ref[at + b, 0] = high
        out_ref[at + b, 1] = low


def spread_kernel(own_ref, c_ref, x_ref, xc_ref, ldiag_ref, out_ref, cut_ref, seconds, body):
    blk = out_ref.shape[-1]
    r = here()[0]
    for flip, ref in enumerate((own_ref, c_ref, x_ref, xc_ref)):
        roots = unpack(ref[:blk, :], ref[blk : blk + 1, :])
        put_roots(out_ref, 2 * (r ^ flip), roots)
        seconds[r ^ flip] = roots[1]
    part = cut_ref.shape[0] - PAD
    body[...], diag = pack(seconds[RAW[0] // 2], seconds[RAW[1] // 2])
    cut_ref[:part, :] = body[pl.ds(pl.multiple_of(r * part, part), part), :]
    which = lax.broadcasted_iota(jnp.int32, diag.shape, 0)
    cut_ref[part:, :] = jnp.where(which == 1, get_diag(ldiag_ref), diag)


def spread_roots(ldiag, *packed):
    blk = packed[0].shape[1]
    count = len(packed)
    return pl.pallas_call(
        spread_kernel,
        out_shape=(
            jax.ShapeDtypeStruct((2 * count, 2, blk, blk), jnp.bfloat16),
            jax.ShapeDtypeStruct((blk // count + PAD, blk), jnp.float32),
        ),
        scratch_shapes=[pltpu.VMEM((count, blk, blk), jnp.float32), pltpu.VMEM((blk, blk), jnp.float32)],
        compiler_params=pltpu.CompilerParams(vmem_limit_bytes=VMEM_LIMIT),
        cost_estimate=SMALL,
        name="spread_roots",
    )(*packed, ldiag)


def rest_kernel(a_ref, out_ref):
    out_ref[...] = a_ref[a_ref.shape[0] - out_ref.shape[0] :, :]


def rest_of(value, rows):
    return pl.pallas_call(
        rest_kernel,
        out_shape=jax.ShapeDtypeStruct((value.shape[0] - rows, value.shape[1]), jnp.float32),
        compiler_params=pltpu.CompilerParams(vmem_limit_bytes=VMEM_LIMIT),
        cost_estimate=SMALL,
        name="rest_of",
    )(value)


def join_kernel(own_ref, c_ref, x_ref, xc_ref, out_ref, body):
    part = own_ref.shape[0] - PAD
    r = here()[0]
    for flip, ref in enumerate((own_ref, c_ref, x_ref, xc_ref)):
        body[pl.ds(pl.multiple_of((r ^ flip) * part, part), part), :] = ref[:part, :]
    put_roots(out_ref, 0, unpack(body[...], own_ref[part : part + 1, :]))


def join_roots(*parts):
    blk = parts[0].shape[1]
    return pl.pallas_call(
        join_kernel,
        out_shape=jax.ShapeDtypeStruct((2, 2, blk, blk), jnp.bfloat16),
        scratch_shapes=[pltpu.VMEM((blk, blk), jnp.float32)],
        compiler_params=pltpu.CompilerParams(vmem_limit_bytes=VMEM_LIMIT),
        cost_estimate=SMALL,
        name="join_roots",
    )(*parts)


def core_apply_kernel(g_ref, packed_ref, under_ref, out_ref):
    rows, blk = g_ref.shape
    root = unpack(packed_ref[:blk, :], packed_ref[blk : blk + 1, :])[0]
    out_ref[:rows, :] = product(split(g_ref[...]), split(root))
    out_ref[rows:, :] = under_ref[...]


def core_apply(tile, packed, under):
    rows = tile.shape[0] // 2
    tall, blk = packed.shape
    return pl.pallas_call(
        core_apply_kernel,
        out_shape=jax.ShapeDtypeStruct((rows + blk, blk), jnp.float32),
        grid_spec=pltpu.PrefetchScalarGridSpec(
            num_scalar_prefetch=0,
            grid=(1,),
            in_specs=[
                pl.BlockSpec((rows, blk), placed(lambda s, place: (1 - place[1], core_first(place)))),
                pl.BlockSpec((tall, blk), lambda s: (0, 0)),
                pl.BlockSpec((blk, blk), lambda s: (0, 0)),
            ],
            out_specs=pl.BlockSpec((rows + blk, blk), lambda s: (0, 0)),
        ),
        compiler_params=pltpu.CompilerParams(vmem_limit_bytes=VMEM_LIMIT),
        cost_estimate=SMALL,
        name="core_apply",
    )(tile, packed, under)


def right_apply_kernel(pieces, carries, g_ref, right_ref, *rest):
    out_refs = rest[-len(pieces) :]
    value = product(split(g_ref[...]), (right_ref[0, 0], right_ref[0, 1]))
    for (top, rows, start, width), ref in zip(pieces, out_refs):
        ref[:rows, :] = value[top : top + rows, start : start + width]
    if carries:
        out_refs[0][value.shape[0] :, :] = rest[0][...]


def right_apply(tile, right, k, pieces, under, after):
    rows = tile.shape[0] // 2
    blk = right.shape[-1]
    pieces = pieces or ((0, rows, 0, blk),)
    in_specs = [
        pl.BlockSpec((rows, blk), placed(lambda s, place: (1 - place[1], later(k, place)))),
        pl.BlockSpec((1, 2, blk, blk), placed(lambda s, place: (later(k, place), 0, 0, 0))),
    ]
    operands = [tile, right]
    more = 0
    if under is not None:
        more = under.shape[0]
        in_specs.append(pl.BlockSpec(under.shape, lambda s: (0, 0)))
        operands.append(under)
    shapes = [(tall + more, width) for _, tall, _, width in pieces]
    return pl.pallas_call(
        functools.partial(right_apply_kernel, pieces, under is not None),
        out_shape=tuple(jax.ShapeDtypeStruct(shape, jnp.float32) for shape in shapes),
        grid_spec=pltpu.PrefetchScalarGridSpec(
            num_scalar_prefetch=0,
            grid=(1,),
            in_specs=in_specs + [pl.BlockSpec(memory_space=pl.ANY)] * len(after),
            out_specs=tuple(pl.BlockSpec(shape, lambda s: (0, 0)) for shape in shapes),
        ),
        compiler_params=pltpu.CompilerParams(vmem_limit_bytes=VMEM_LIMIT),
        cost_estimate=SMALL,
        name="right_apply",
    )(*operands, *after)


def left_product(left_ref, value, out_ref):
    blk = left_ref.shape[-1]
    for i in range(value.shape[0] // blk):
        part = split(value[i * blk : (i + 1) * blk])
        out_ref[i * blk : (i + 1) * blk, :] = product((left_ref[i, 0], left_ref[i, 1]), part)


def update_kernel(g_ref, left_ref, right_ref, *rest):
    half = product(split(g_ref[...]), (right_ref[0, 0], right_ref[0, 1]))
    left_product(left_ref, half, rest[-2])
    rest[-1][...] = jnp.zeros_like(rest[-1])


def finish_kernel(column, first, half_ref, left_ref, out_before, out_ref, stage, sems):
    blk = left_ref.shape[-1]
    width = stage.shape[1]
    part = blk // 2
    cols = pl.ds(pl.multiple_of(column(here()), width), width)
    copies = []
    for i in range(stage.shape[0] // blk):
        value = split(half_ref[pl.ds(i * blk, blk), :])
        for k in range(2):
            root = tuple(left_ref[first + i, h, pl.ds(k * part, part), :] for h in range(2))
            rows = pl.ds(i * blk + k * part, part)
            stage[rows, :] = product(root, value)
            there = out_ref.at[pl.ds((first + i) * blk + k * part, part), cols]
            copies.append(pltpu.make_async_copy(stage.at[rows, :], there, sems.at[len(copies)]))
            copies[-1].start()
    for copy in copies:
        copy.wait()


def finish(half, left, out, column, first=0, count=2):
    width = half.shape[1]
    blk = left.shape[-1]
    vmem = pl.BlockSpec(memory_space=pltpu.VMEM)
    anywhere = pl.BlockSpec(memory_space=pl.ANY)
    return pl.pallas_call(
        functools.partial(finish_kernel, column, first),
        out_shape=jax.ShapeDtypeStruct(out.shape, jnp.float32),
        in_specs=[vmem, vmem, anywhere],
        out_specs=anywhere,
        scratch_shapes=[pltpu.VMEM((count * blk, width), jnp.float32), pltpu.SemaphoreType.DMA((2 * count,))],
        input_output_aliases={2: 0},
        compiler_params=pltpu.CompilerParams(vmem_limit_bytes=VMEM_LIMIT),
        cost_estimate=SMALL,
        name="finish",
    )(half, left, out)


def update(source, left, right, out, out_shape, g_map, out_map, first=0, count=None, after=()):
    rows = out_shape[0]
    blk = left.shape[-1]
    in_specs = [
        pl.BlockSpec((rows, blk), placed(g_map)),
        pl.BlockSpec((2, 2, blk, blk), lambda s: (0, 0, 0, 0)),
        pl.BlockSpec((1, 2, blk, blk), lambda s: (first + s, 0, 0, 0)),
    ]
    operands = [source, left, right]
    aliases = {}
    if out is not None:
        aliases = {len(operands): 0}
        in_specs.append(pl.BlockSpec(memory_space=pl.ANY))
        operands.append(out)
    in_specs += [pl.BlockSpec(memory_space=pl.ANY)] * len(after)
    return pl.pallas_call(
        update_kernel,
        out_shape=(jax.ShapeDtypeStruct(out_shape, jnp.float32), jax.ShapeDtypeStruct((8, 128), jnp.float32)),
        grid_spec=pltpu.PrefetchScalarGridSpec(
            num_scalar_prefetch=0,
            grid=(count or right.shape[0],),
            in_specs=in_specs,
            out_specs=(pl.BlockSpec((rows, blk), placed(out_map)), pl.BlockSpec((8, 128), lambda s: (0, 0))),
        ),
        input_output_aliases=aliases,
        compiler_params=pltpu.CompilerParams(vmem_limit_bytes=VMEM_LIMIT),
        cost_estimate=SMALL,
        name="update",
    )(*operands, *after)


def exchange_device(full_dim, n_row, grads, left_stats, right_stats):
    tile_rows, tile_cols = grads.shape[1:]
    blk = left_stats.shape[2]
    tile = pltpu.with_memory_space_constraint(grads.reshape(tile_rows, tile_cols), pltpu.HBM)
    lstats = left_stats.reshape(tile_rows, blk)
    rstats = right_stats.reshape(tile_cols, blk)
    rows = tile_rows // 2
    shape = (rows, 2 * tile_cols)
    halves = tile_cols // blk

    def over(axis, value):
        if axis == "y":
            return lax.ppermute(value, "col", [(0, 1), (1, 0)])
        flip = {"core": 1, "x": 2}[axis]
        return lax.ppermute(value, "row", [(i, i ^ flip) for i in range(n_row)])

    first = take(tile, blk, RAW[0], 1)
    raw = [over("y", first)]
    tile = load(tile, first)

    send_on, keep_on = right_grams(tile, blk, (3, 2), first)
    far = fold(keep_on, over("core", send_on))
    raw.append(over("y", take(tile, blk, RAW[1], 16, send_on)))
    send, keep = right_grams(tile, blk, (1, 0), far, raw[0])
    near = over("core", send)
    far = over("x", far)

    own, half = right_roots(full_dim, rstats, keep, near, far, tile)
    came_a = over("y", half)
    lsend, ldiag = left_grams(tile, blk, lambda place: 1 - place[1], half)
    own = hold(own, raw[1], lsend)
    own_c = over("core", own)
    own_x = over("x", own)
    half = core_apply(tile, own_c, lsend)
    came_b = over("y", half)
    own_x = hold(own_x, half, came_a)
    lkeep, kdiag = left_grams(tile, blk, lambda place: place[1], half)
    roots, part = spread_roots(ldiag, own, own_c, own_x, over("core", own_x))

    (half,) = right_apply(tile, roots, 0, None, part, (lkeep,))
    came_c = over("y", half)
    (half,) = right_apply(tile, roots, 1, None, None, (came_b,))
    came_d = over("y", half)

    def crossed(block, start=0):
        return lambda place: (1 - place[1]) * tile_cols + block(place) * blk + start

    (half,) = right_apply(tile, roots, 2, None, None, (came_c,))
    came_e = over("y", half)
    left = left_roots(full_dim, lstats, half, lkeep, kdiag, came_b, came_c)
    out, done = update(
        tile, left, roots, None, shape,
        lambda s, place: (place[1], s),
        lambda s, place: (0, place[1] * halves + s),
    )
    wide = blk // 2
    last = ((0, rows, 0, wide), (0, blk, wide, wide), (blk, blk, wide, wide))
    held = right_apply(tile, roots, 3, last, None, (came_d, done))
    came_last = [over("y", half) for half in held]
    out = finish(came_a, left, out, crossed(own_first))
    out = finish(came_b, left, out, crossed(core_first))
    part = rest_of(came_c, rows)
    part_x = over("x", part)
    roots_raw = join_roots(part, over("core", part), part_x, over("core", part_x))
    for k, (block, value) in enumerate(zip(RAW, raw)):
        out, done = update(
            value, left, roots_raw, out, shape,
            lambda s, place: (0, 0),
            lambda s, place, block=block: (0, (1 - place[1]) * halves + block),
            k, 1, held[:1],
        )
    for k, value in enumerate((came_c, came_d, came_e)):
        out = finish(value, left, out, crossed(functools.partial(later, k)))
    for (top, tall, start, _), value in zip(last, came_last):
        out = finish(value, left, out, crossed(functools.partial(later, 3), start), top // blk, tall // blk)
    return out.reshape(1, rows, 2 * tile_cols)


def per_device(n_row, n_col, grads, left_stats, right_stats):
    mats, tile_rows, tile_cols = grads.shape
    blk = left_stats.shape[2]
    full_dim = tile_cols * n_col
    if mats == 1 and n_col == 2 and n_row == 4 and tile_rows == 4 * blk and tile_cols == 8 * blk:
        return exchange_device(full_dim, n_row, grads, left_stats, right_stats)
    return general_device(full_dim, grads, left_stats, right_stats)


def solution(mesh):
    return jax.shard_map(
        functools.partial(per_device, mesh.shape["row"], mesh.shape["col"]),
        mesh=mesh,
        in_specs=(P("mat", "row", "col"), P("mat", "row", None), P("mat", "col", None)),
        out_specs=P("mat", ("row", "col"), None),
        check_vma=False,
    )
```
